128 devices in a mesh: tile: 16 (over z, y), rep: 8 (over x, core).
Axes of the slice: x: 4, y: 4, z: 4, core: 2. Of those that a mesh axis runs over, the one named last changes fastest.
Arguments:
- patch_features: bfloat16 [8, 4096, 1024], P('rep', 'tile'), may hold values from -6 to 6
- labels: int32 [128, 32], replicated, may hold values from 0 to 3
- assigned_specialists: int32 [8, 4096, 2], P('rep', 'tile'), may hold values from 0 to 15, all different within a row; in each aligned block of 256 rows (0 to 255, 256 to 511, ..., all dimensions but the last counted through in order) at most 48 rows name the same one
- loss_sensitivity: bfloat16 [8, 4096, 1024], P('rep', 'tile'), may hold values from -6 to 6
- attn_qkv: bfloat16 [1024, 3072], replicated, may hold values from -2 to 2, as said below
- attn_out: bfloat16 [1024, 1024], replicated, may hold values from -0.1875 to 0.1875
- router: bfloat16 [1024, 16], replicated, may hold values from -0.1875 to 0.1875
- expert_up: bfloat16 [16, 1024, 2048], P('tile'), may hold values from -0.1875 to 0.1875
- expert_down: bfloat16 [16, 2048, 1024], P('tile'), may hold values from -0.125 to 0.125
Outputs:
- layer_result: bfloat16 [8, 4096, 1024], P('rep', 'tile')
- grad_up: float32 [16, 1024, 2048], P('tile', 'rep')
- grad_down: float32 [16, 2048, 1024], P('tile', None, 'rep')
The draws below stay inside these ranges and needn't reach their ends.
Inputs may be any that keep to these rules, and one draw needn't show every extreme that they name: `attn_qkv`: Hidden-unit columns of query and key blocks may be strongly aligned in some heads. `assigned_specialists`: within the 256 cells of one strip (aligned blocks of rows), no expert is named by more than 48 cells, a bound that some block reaches of them.
All inputs are finite; a program needn't handle non-finite values.
Results may differ from the reference program's by a relative error of at most 0.018.
Values may be sent and summed in bfloat16 or wider, within the bound.
A program may use at most 128 MiB of HBM per device.

```python
import math
import jax
import jax.numpy as jnp
import numpy as np
from jax import lax

FEATURE_WIDTH = 1024
HEADS = 32
FFW = 2048
CHOSEN_PER_CELL = 2
WIN = 8
COLS = 32
SHIFT = 4
SPECIALIST_NUM = 16
BAND_CELLS = 256
DISPATCH_CAP = 48
NH = 128
GRID_CELLS = 4096
LEAD_HOURS = 8
N_TILE = 16


def draw_attn_qkv(key, part):
    key = jax.random.fold_in(key, 7)
    base = jax.random.normal(key, (FEATURE_WIDTH, 3 * FEATURE_WIDTH), jnp.float32) * FEATURE_WIDTH ** (-0.5)
    return base.astype(jnp.bfloat16)


def plant(array, own_key, smallest, top_value):
    index_at = [jax.random.randint(jax.random.fold_in(own_key, axis), (), 0, length) for axis, length in enumerate(array.shape)]
    widest = array.shape.index(max(array.shape))
    beside = index_at[:widest] + [(index_at[widest] + 1) % array.shape[widest]] + index_at[widest + 1:]
    return array.at[tuple(index_at)].set(smallest).at[tuple(beside)].set(top_value)


def with_spikes(drawn, own_key, source, target, shards_of, factor):
    def block_of(dim):
        return (jnp.arange(drawn.shape[dim]) // (drawn.shape[dim] // shards_of)).reshape((-1,) + (1,) * (drawn.ndim - 1 - dim))

    first = jax.random.permutation(own_key, shards_of)[block_of(target)]
    other_side = (block_of(target) + shards_of // 2) % shards_of
    return jnp.where((block_of(source) == first) | (block_of(source) == other_side), factor * drawn, drawn)


def block_levels(key, dims, pieces, least, high):
    loudness, own = 1.0, jax.random.fold_in(key, 6)
    for position, parts in pieces:
        heights = jnp.exp(jax.random.uniform(jax.random.fold_in(own, position), (parts,), jnp.float32, least / len(pieces), high / len(pieces)))
        loudness = loudness * jnp.repeat(heights, dims[position] // parts).reshape([-1 if axis == position else 1 for axis in range(len(dims))])
    return loudness


def deal_out(stream_key, own, number, rows, count, top, bound, skew):
    ranking = jax.random.permutation(stream_key, count)
    heavy_load, ordinary = shares(count, rows * top, bound, skew, True), shares(count, rows * top, bound, skew, False)
    places = jnp.arange(count)

    def named(sizes, offset_by):
        used = int((sizes > 0).sum())
        fixed = max(1, used // 4)
        moved = fixed + (places - fixed + offset_by * (used - fixed)) % max(1, count - fixed)
        return jnp.zeros((count,), jnp.int32).at[ranking[jnp.where(places < fixed, places, moved)]].set(jnp.asarray(sizes, jnp.int32))

    sizes = jnp.where(number % 4 == 0, named(heavy_load, number // 4), named(ordinary, number - number // 4 - 1))
    mixed = jax.random.permutation(jax.random.fold_in(own, 3), count)
    donor, sink = mixed[0:count // 2 * 2:2], mixed[1:count // 2 * 2:2]
    margin = jnp.minimum(sizes[donor] - 1, bound - sizes[sink]) // 2
    margin = jnp.where((donor == ranking[0]) | (sink == ranking[0]) | (sizes[sink] == 0), 0, jnp.maximum(margin, 0))
    moved = jax.random.randint(jax.random.fold_in(own, 4), (count // 2,), 0, 1 << 20) % (margin + 1)
    sizes = sizes.at[donor].add(-moved).at[sink].add(moved)
    members = jnp.searchsorted(jnp.cumsum(sizes), jnp.arange(rows * top), side="right").astype(jnp.int32)
    grid = members.reshape(top, rows).T
    grid = grid[jax.random.permutation(jax.random.fold_in(own, 1), rows)]
    offset_by = jax.random.randint(jax.random.fold_in(own, 2), (rows, 1), 0, top)
    return jnp.take_along_axis(grid, (jnp.arange(top)[None, :] + offset_by) % top, axis=1)


def shares(number_of, total, most, skew, full):
    weights = [(1 << 20) // math.isqrt(rank ** skew) + 1 for rank in range(1, number_of + 1)]
    largest = most if full else min(most, max(-(-total // number_of), total * weights[0] // sum(weights)))
    least = 1 if total - largest >= number_of - 1 else 0
    counts, rest = [largest] + [least] * (number_of - 1), total - largest - least * (number_of - 1)
    while rest > 0:
        movable = [i for i in range(1, number_of) if counts[i] < largest] or [i for i in range(1, number_of) if counts[i] < most]
        mass, remaining = sum([weights[i] for i in movable]), rest
        for i in movable:
            extra = min(most - counts[i], max(1, remaining * weights[i] // mass), rest)
            counts[i] = counts[i] + extra
            rest = rest - extra
    return np.array(counts)


def normal_values(own_key, shape, scale, bound, pieces=(), kind=jnp.bfloat16):
    result = scale * jax.random.normal(own_key, shape, jnp.float32)
    if pieces:
        result = result * block_levels(own_key, shape, pieces, -0.22, 0.18)
    return jnp.clip(result, -bound, bound).astype(kind)


def gaussian_with(rng, shape, deviation, reach, cuts, heavy, kind=jnp.bfloat16):
    drawn = deviation * jax.random.normal(rng, shape, jnp.float32)
    if cuts:
        drawn = drawn * block_levels(rng, shape, cuts, -0.22, 0.18)
    return jnp.clip(with_spikes(drawn, jax.random.fold_in(rng, 3), *heavy), -reach, reach).astype(kind)


def setup_inputs(seed: int = 0) -> dict:
    streams_of = jax.random.split(jax.random.key(seed), 10)
    patch_features = normal_values(streams_of[0], (LEAD_HOURS, GRID_CELLS, FEATURE_WIDTH), 1.0, 6.0, ((0, 8), (1, 16)))
    labels = plant(jax.random.randint(streams_of[1], (NH, COLS), 0, 4), jax.random.fold_in(streams_of[1], 1), 0, 3).astype(jnp.int32)
    assigned_specialists_keys = jax.random.split(jax.random.fold_in(streams_of[2], 1), LEAD_HOURS * GRID_CELLS // BAND_CELLS)
    assigned_specialists_turns = jax.random.permutation(jax.random.fold_in(streams_of[2], 3), LEAD_HOURS * GRID_CELLS // BAND_CELLS)
    assigned_specialists = jax.vmap(lambda own, number: deal_out(jax.random.fold_in(streams_of[2], 2), own, number, BAND_CELLS, SPECIALIST_NUM, CHOSEN_PER_CELL, DISPATCH_CAP, 2))(assigned_specialists_keys, assigned_specialists_turns).reshape((LEAD_HOURS, GRID_CELLS, CHOSEN_PER_CELL))
    loss_sensitivity = gaussian_with(streams_of[3], (LEAD_HOURS, GRID_CELLS, FEATURE_WIDTH), 1.0, 6.0, ((0, 8), (1, 16)), (0, 2, 8, 2.0))
    attn_qkv = draw_attn_qkv(jax.random.fold_in(streams_of[9], 71), 0)
    attn_out = normal_values(streams_of[5], (FEATURE_WIDTH, FEATURE_WIDTH), FEATURE_WIDTH ** -0.5, 0.1875)
    router = normal_values(streams_of[6], (FEATURE_WIDTH, SPECIALIST_NUM), FEATURE_WIDTH ** -0.5, 0.1875)
    expert_up = normal_values(streams_of[7], (SPECIALIST_NUM, FEATURE_WIDTH, FFW), FEATURE_WIDTH ** -0.5, 0.1875, ((0, 16),))
    expert_down = normal_values(streams_of[8], (SPECIALIST_NUM, FFW, FEATURE_WIDTH), FFW ** -0.5, 0.125, ((0, 16),))
    return {"patch_features": patch_features, "labels": labels, "assigned_specialists": assigned_specialists, "loss_sensitivity": loss_sensitivity, "attn_qkv": attn_qkv, "attn_out": attn_out, "router": router, "expert_up": expert_up, "expert_down": expert_down}


EPSILON = 1e-05

def layer_norm(values):
    values = values.astype(jnp.float32)
    center = values - lax.optimization_barrier(jnp.mean(values, axis=-1, keepdims=True))
    spread = lax.optimization_barrier(jnp.mean(center * center, axis=-1, keepdims=True))
    return center * lax.rsqrt(spread + EPSILON)

def activate(values):
    return jax.nn.gelu(values, approximate=True)

def to_windows(values, win_size):
    row_count = values.shape[0] // win_size
    col_count = values.shape[1] // win_size
    values = values.reshape((row_count, win_size, col_count, win_size) + values.shape[2:])
    values = jnp.swapaxes(values, 1, 2)
    return values.reshape((row_count * col_count, win_size * win_size) + values.shape[4:])

def from_windows(values, row_count, col_count, win_size):
    values = values.reshape((row_count // win_size, col_count // win_size, win_size, win_size) + values.shape[2:])
    values = jnp.swapaxes(values, 1, 2)
    return values.reshape((row_count, col_count) + values.shape[4:])

def window_attention(queries, key_rows, value_rows, label_grid, head_count, win_size):
    row_count, col_count, model_width = queries.shape
    head_dim = model_width // head_count
    cells = win_size * win_size
    query_win = to_windows(queries, win_size).reshape(-1, cells, head_count, head_dim).astype(jnp.float32)
    key_win = to_windows(key_rows, win_size).reshape(-1, cells, head_count, head_dim).astype(jnp.float32)
    value_win = to_windows(value_rows, win_size).reshape(-1, cells, head_count, head_dim).astype(jnp.float32)
    label_win = to_windows(label_grid, win_size)
    scores = jnp.einsum('wqhd,wkhd->whqk', query_win, key_win) * head_dim ** (-0.5)
    same_label = label_win[:, :, None] == label_win[:, None, :]
    allowed = same_label & (label_win[:, None, :] >= 0) | (label_win[:, :, None] < 0)
    scores = jnp.where(allowed[:, None], scores, -jnp.inf)
    row_peak = lax.optimization_barrier(jnp.max(scores, axis=-1, keepdims=True))
    expo = jnp.exp(scores - row_peak)
    row_total = lax.optimization_barrier(jnp.sum(expo, axis=-1, keepdims=True))
    weights_bf = (expo / row_total).astype(jnp.bfloat16)
    context = jnp.einsum('whqk,wkhd->wqhd', weights_bf.astype(jnp.float32), value_win).astype(jnp.bfloat16)
    context = context.reshape(-1, cells, model_width)
    return from_windows(context, row_count, col_count, win_size)

def slot_targets(route_rows, experts, capacity):
    flat_ids = route_rows.reshape(-1).astype(jnp.int32)
    onehot = (flat_ids[:, None] == jnp.arange(experts, dtype=jnp.int32)[None, :]).astype(jnp.int32)
    before = jnp.cumsum(onehot, axis=0) - onehot
    slot_ids = lax.optimization_barrier(jnp.sum(before * onehot, axis=1)).astype(jnp.int32)
    return (flat_ids * capacity + slot_ids).astype(jnp.int32)

def attention_block(tokens_time, labels, attn_qkv, attn_out):
    grid_block = tokens_time.reshape(NH, COLS, FEATURE_WIDTH)
    normed = layer_norm(grid_block).astype(jnp.bfloat16)
    projected = jnp.dot(normed.reshape(-1, FEATURE_WIDTH), attn_qkv, preferred_element_type=jnp.float32)
    projected = projected.astype(jnp.bfloat16).reshape(NH, COLS, 3 * FEATURE_WIDTH)
    padded = jnp.pad(projected, ((SHIFT, SHIFT), (SHIFT, SHIFT), (0, 0)))
    padded_labels = jnp.pad(labels, SHIFT, constant_values=-1)
    context = window_attention(padded[:, :, :FEATURE_WIDTH], padded[:, :, FEATURE_WIDTH:2 * FEATURE_WIDTH], padded[:, :, 2 * FEATURE_WIDTH:], padded_labels, HEADS, WIN)
    context = context[SHIFT:SHIFT + NH, SHIFT:SHIFT + COLS].reshape(-1, FEATURE_WIDTH)
    return tokens_time.astype(jnp.float32) + jnp.dot(context, attn_out, preferred_element_type=jnp.float32)

def route_block(hidden_block, route_rows, cotangent_block, router):
    moe_in = layer_norm(hidden_block).astype(jnp.bfloat16)
    logits = jnp.dot(moe_in, router, preferred_element_type=jnp.float32)
    chosen = jnp.take_along_axis(jax.nn.sigmoid(logits), route_rows, axis=1)
    gate_values = chosen / lax.optimization_barrier(jnp.sum(chosen, axis=1, keepdims=True))
    targets = slot_targets(route_rows, SPECIALIST_NUM, DISPATCH_CAP)
    row_grads = (gate_values[:, :, None] * cotangent_block.astype(jnp.float32)[:, None, :]).astype(jnp.bfloat16)
    inputs = jnp.repeat(moe_in, CHOSEN_PER_CELL, axis=0)
    incoming_features_store = jnp.zeros((SPECIALIST_NUM * DISPATCH_CAP, FEATURE_WIDTH), jnp.bfloat16).at[targets].set(inputs)
    derivative_accumulator = jnp.zeros((SPECIALIST_NUM * DISPATCH_CAP, FEATURE_WIDTH), jnp.bfloat16).at[targets].set(row_grads.reshape(-1, FEATURE_WIDTH))
    return (gate_values, targets, incoming_features_store, derivative_accumulator)

def reference(patch_features, labels, assigned_specialists, loss_sensitivity, attn_qkv, attn_out, router, expert_up, expert_down):
    hidden = lax.map(lambda tokens_time: attention_block(tokens_time, labels, attn_qkv, attn_out), patch_features)
    weight_matrices = LEAD_HOURS * N_TILE
    inner_layer_matrices = hidden.reshape(weight_matrices, BAND_CELLS, FEATURE_WIDTH)
    gate_values, targets, incoming_features_store, derivative_accumulator = jax.vmap(route_block, in_axes=(0, 0, 0, None))(inner_layer_matrices, assigned_specialists.reshape(weight_matrices, BAND_CELLS, CHOSEN_PER_CELL), loss_sensitivity.reshape(weight_matrices, BAND_CELLS, FEATURE_WIDTH), router)
    incoming_features_store = incoming_features_store.reshape(LEAD_HOURS, N_TILE, SPECIALIST_NUM, DISPATCH_CAP, FEATURE_WIDTH)
    derivative_accumulator = derivative_accumulator.reshape(LEAD_HOURS, N_TILE, SPECIALIST_NUM, DISPATCH_CAP, FEATURE_WIDTH)

    def expert_pass(specialist_position):
        up_weight = expert_up[specialist_position]
        down_weight = expert_down[specialist_position]
        incoming_feature_vectors = incoming_features_store[:, :, specialist_position].reshape(LEAD_HOURS, N_TILE * DISPATCH_CAP, FEATURE_WIDTH)
        vector_derivative = derivative_accumulator[:, :, specialist_position].reshape(LEAD_HOURS, N_TILE * DISPATCH_CAP, FEATURE_WIDTH)

        def per_lead_hour(carried_values, duplicate_couple):
            rep_inputs, rep_grads = duplicate_couple
            pre_act = jnp.dot(rep_inputs, up_weight, preferred_element_type=jnp.float32)
            activated = activate(pre_act).astype(jnp.bfloat16)
            result_vectors = jnp.dot(activated, down_weight, preferred_element_type=jnp.float32).astype(jnp.bfloat16)
            act_grads = jnp.dot(rep_grads, down_weight.T, preferred_element_type=jnp.float32)
            _, pullback = jax.vjp(activate, pre_act)
            pre_grads = pullback(act_grads)[0].astype(jnp.bfloat16)
            down_part = jnp.dot(activated.T, rep_grads, preferred_element_type=jnp.float32).astype(jnp.bfloat16)
            up_part = jnp.dot(rep_inputs.T, pre_grads, preferred_element_type=jnp.float32).astype(jnp.bfloat16)
            down_part, up_part = lax.optimization_barrier((down_part, up_part))
            return ((carried_values[0] + up_part.astype(jnp.float32), carried_values[1] + down_part.astype(jnp.float32)), result_vectors)
        first_position = (jnp.zeros((FEATURE_WIDTH, FFW), jnp.float32), jnp.zeros((FFW, FEATURE_WIDTH), jnp.float32))
        (expand_weight_sum, contract_weight_sum), result_vectors = lax.scan(per_lead_hour, first_position, (incoming_feature_vectors, vector_derivative))
        return (result_vectors, expand_weight_sum, contract_weight_sum)
    result_vectors, grad_up, grad_down = lax.map(expert_pass, jnp.arange(SPECIALIST_NUM, dtype=jnp.int32))
    result_vectors = result_vectors.reshape(SPECIALIST_NUM, LEAD_HOURS, N_TILE, DISPATCH_CAP, FEATURE_WIDTH).transpose(1, 2, 0, 3, 4)
    result_vectors = result_vectors.reshape(weight_matrices, SPECIALIST_NUM * DISPATCH_CAP, FEATURE_WIDTH)
    picked = jax.vmap(lambda returned_table, slot_rows: jnp.take(returned_table, slot_rows, axis=0))(result_vectors, targets)
    picked = picked.reshape(weight_matrices, BAND_CELLS, CHOSEN_PER_CELL, FEATURE_WIDTH).astype(jnp.float32)
    specialist_mixture = lax.optimization_barrier(jnp.sum(gate_values[:, :, :, None] * picked, axis=2))
    layer_result = (inner_layer_matrices + specialist_mixture).astype(jnp.bfloat16).reshape(LEAD_HOURS, GRID_CELLS, FEATURE_WIDTH)
    return (layer_result, grad_up, grad_down)
```

```python
import functools

import jax
import jax.numpy as jnp
from jax import lax
from jax.experimental import pallas as pl
from jax.experimental.pallas import tpu as pltpu
from jax.sharding import PartitionSpec as P

F = 1024
FFW = 2048
NE = 16
CAP = 48
T = 256
ROWS = NE * CAP
HB = 512
NB = FFW // HB
GROUPS = 2 * NB
QW = 256
SCALE = 32 ** (-0.5)
EPSILON = 1e-05
GELU_A = 0.7978845608028654
GELU_B = 0.044715
f32 = jnp.float32
bf16 = jnp.bfloat16
MESH = pl.DeviceIdType.MESH

NN = (((1,), (0,)), ((), ()))
NT = (((1,), (1,)), ((), ()))
TN = (((0,), (0,)), ((), ()))


def dot(a, b, dims=NN):
    return lax.dot_general(a, b, dims, preferred_element_type=f32)


def iota(shape, dim):
    return lax.broadcasted_iota(jnp.int32, shape, dim)


def layer_norm(values):
    center = values - jnp.mean(values, axis=-1, keepdims=True)
    spread = jnp.mean(center * center, axis=-1, keepdims=True)
    return center * lax.rsqrt(spread + EPSILON)


def norm_to_windows(src, dst, pairs):
    for p in pairs:
        y = layer_norm(src[p * 64 : p * 64 + 64, :].astype(f32))
        y0 = pltpu.roll(y[:32], 28, 0)
        y1 = pltpu.roll(y[32:], 28, 0)
        for w in range(4):
            block = jnp.concatenate([y0[8 * w : 8 * w + 8], y1[8 * w : 8 * w + 8]], axis=0)
            start = (p // 2) * 128 + w * 32 + (p % 2) * 16
            dst[start : start + 16, :] = block.astype(bf16)


def kernel(
    feat, labels, assigned, sens, w_qkv, w_out, router, w_up, w_down,
    out_layer, out_up, out_down,
    feat_v, sens_v, wq, wk, wv, wo, wu, wd,
    halo, n_own, n_halo, q_own, k_all, v_all, ctx, oh, hid, moe,
    disp, disp_t, meta_send, meta_recv, xl_send, xl_recv, ret, a2, hgn, gate_v,
    stage, crecv, r2, rf,
    load_sem, halo_ss, halo_rs, l_ss, l_rs, m_ss, m_rs, x_ss, x_rs, t_ss, t_rs,
    c_ss, c_rs, x2_ss, x2_rs,
):
    me = lax.axis_index("tile")
    rep = lax.axis_index("rep")
    core = lax.rem(rep, 2)
    xpos = lax.div(rep, 2)
    partner = rep + 1 - 2 * core
    x_next = lax.rem(rep + 2, 8)
    x_prev = lax.rem(rep + 6, 8)

    loads = [
        pltpu.make_async_copy(s, d, load_sem.at[i])
        for i, (s, d) in enumerate(
            [
                (feat, feat_v),
                (sens, sens_v),
                (w_qkv.at[:, F : 2 * F], wk),
                (w_qkv.at[:, 2 * F : 3 * F], wv),
                (w_qkv.at[:, 0:F], wq),
                (w_out, wo),
                (w_down, wd),
                (w_up, wu),
            ]
        )
    ]
    for c in loads:
        c.start()
    ld_feat, ld_sens, ld_k, ld_v, ld_q, ld_o, ld_d, ld_u = loads

    barrier = pltpu.get_barrier_semaphore()
    for k in range(1, NE):
        pl.semaphore_signal(barrier, inc=1, device_id={"tile": lax.rem(me + k, NE)}, device_id_type=MESH)
    for r in (partner, x_next, x_prev):
        pl.semaphore_signal(barrier, inc=1, device_id={"rep": r}, device_id_type=MESH)
    pl.semaphore_wait(barrier, NE - 1 + 3)

    def tile_copy(src, dst, ss, rs, target):
        return pltpu.make_async_remote_copy(
            src_ref=src, dst_ref=dst, send_sem=ss, recv_sem=rs,
            device_id={"tile": target}, device_id_type=MESH,
        )

    def rep_copy(src, dst, ss, rs, target):
        return pltpu.make_async_remote_copy(
            src_ref=src, dst_ref=dst, send_sem=ss, recv_sem=rs,
            device_id={"rep": target}, device_id_type=MESH,
        )

    t_next = lax.rem(me + 1, NE)
    t_prev = lax.rem(me + NE - 1, NE)
    halo_copies = [
        tile_copy(feat.at[T // 2 : T, :], halo.at[0 : T // 2, :], halo_ss.at[0], halo_rs.at[0], t_next),
        tile_copy(feat.at[0 : T // 2, :], halo.at[T // 2 : T, :], halo_ss.at[1], halo_rs.at[1], t_prev),
    ]
    for c in halo_copies:
        c.start()

    def exchange(k, src, dst, ss, rs):
        target = lax.rem(me + k, NE)
        return tile_copy(src.at[target], dst.at[me], ss.at[k], rs.at[k], target)

    def arrival(k, src, dst, ss, rs):
        origin = lax.rem(me + NE - k, NE)
        return tile_copy(src.at[origin], dst.at[origin], ss.at[k], rs.at[k], origin)

    a = assigned[...]
    lane = iota((T, 128), 1)
    member = jnp.where((a[:, 0:1] == lane) | (a[:, 1:2] == lane), 1.0, 0.0).astype(bf16)
    eye = (iota((T, T), 0) == iota((T, T), 1)).astype(f32).astype(bf16)
    before = (iota((T, T), 0) < iota((T, T), 1)).astype(f32).astype(bf16)
    member_t = dot(member, eye, TN)[0:NE]
    rank_t = dot(member, before, TN)[0:NE]
    slot_t = jnp.where(member_t > 0.5, rank_t, -1.0)
    slots = iota((CAP, T), 0).astype(f32)
    for e in range(NE):
        disp[e * CAP : (e + 1) * CAP, :] = jnp.where(slot_t[e : e + 1] == slots, 1.0, 0.0).astype(bf16)
    disp[ROWS:, :] = jnp.zeros((128 - CAP, T), bf16)
    id_sum = jnp.sum(member_t * iota((NE, T), 0).astype(f32), axis=0, keepdims=True)
    id_rows = jnp.broadcast_to(id_sum, (16, T)).astype(bf16)

    ld_sens.wait()

    def send_sens(q, _):
        rows = pl.ds(pl.multiple_of(q * 192, 16), 192)
        part = disp[rows, :]
        for n in range(2):
            block = dot(part, sens_v[:, n * 512 : n * 512 + 512]).astype(bf16)
            xl_send[1, pl.ds(q * 4, 4), :, n * 512 : n * 512 + 512] = block.reshape(4, CAP, 512)
        return _

    lax.fori_loop(0, 4, send_sens, 0)

    def make_meta(e, _):
        rows = disp[pl.ds(pl.multiple_of(e * CAP, 16), 128), :]
        meta_send[e] = dot(id_rows, rows, NT).astype(bf16)
        return _

    lax.fori_loop(0, NE, make_meta, 0)
    sens_send, sens_recv = xl_send.at[1], xl_recv.at[1]

    def start_sens(k, _):
        exchange(k, sens_send, sens_recv, l_ss, l_rs).start()
        exchange(k, meta_send, meta_recv, m_ss, m_rs).start()
        return _

    lax.fori_loop(1, NE, start_sens, 0)
    sens_recv[me] = sens_send[me]
    meta_recv[me] = meta_send[me]

    ld_feat.wait()
    norm_to_windows(feat_v, n_own, range(4))

    def project(src, weight, store):
        def body(n, _):
            cols = pl.ds(pl.multiple_of(n * 256, 256), 256)
            store(cols, dot(src[...], weight[:, cols]).astype(bf16))
            return _

        lax.fori_loop(0, 4, body, 0)

    def into(dst, start):
        def store(cols, block):
            dst[:, start : start + 32, cols] = block.reshape(8, 32, 256)

        return store

    def into_q(cols, block):
        q_own[:, cols] = block

    ld_k.wait()
    project(n_own, wk, into(k_all, 0))
    ld_v.wait()
    project(n_own, wv, into(v_all, 0))
    ld_q.wait()
    project(n_own, wq, into_q)

    n = iota((2 * T, 1), 0)
    is_halo = n >= T
    m = jnp.where(is_halo, n - T, n)
    band, win, row4, col8 = m >> 7, (m >> 5) & 3, (m >> 3) & 3, m & 7
    col = (win * 8 + col8 + 4) & 31
    grid_row = me * 8 + jnp.where(is_halo, 12 * band - 4, 4 * band) + row4
    valid = (grid_row >= 0) & (grid_row < 128)
    pick = jnp.where(grid_row == iota((2 * T, 128), 1), 1.0, 0.0).astype(bf16)
    by_row = dot(pick, labels[...].astype(f32).astype(bf16))
    lab = jnp.sum(jnp.where(iota((2 * T, 32), 1) == col, by_row, 0.0), axis=1, keepdims=True)
    lab = jnp.where(valid, lab + jnp.where(col < 4, 4.0, 0.0), -1.0)
    oh[...] = jnp.where(lab == iota((2 * T, 128), 1).astype(f32), 1.0, 0.0).astype(bf16)

    for c in halo_copies:
        c.wait_recv()
    norm_to_windows(halo, n_halo, range(4))
    project(n_halo, wk, into(k_all, 32))
    project(n_halo, wv, into(v_all, 32))

    diag = (iota((QW, QW), 0) >> 5) == (iota((QW, QW), 1) >> 5)

    def window(bw, _):
        rows = pl.ds(pl.multiple_of(bw * 32, 32), 32)
        halo_rows = pl.ds(pl.multiple_of(T + bw * 32, 32), 32)
        oq = oh[rows, :]
        ok = jnp.concatenate([oq, oh[halo_rows, :]], axis=0)
        allowed = dot(ok, jnp.concatenate([oq] * 8, axis=0), NT)
        bias = (allowed - 1.0) * 1e30
        for g in range(4):
            cols = slice(g * QW, (g + 1) * QW)
            qg = jnp.concatenate([q_own[rows, cols]] * 8, axis=0)
            qg = jnp.where(diag, qg, jnp.zeros_like(qg))
            scores = dot(k_all[bw, :, cols], qg, NT) * SCALE + bias
            peak = jnp.max(scores, axis=0, keepdims=True)
            expo = jnp.exp(scores - peak)
            weights = (expo * (1.0 / jnp.sum(expo, axis=0, keepdims=True))).astype(bf16)
            mixed = dot(weights, v_all[bw, :, cols], TN)
            mixed = jnp.where(diag, mixed, 0.0).reshape(8, 32, QW)
            ctx[rows, cols] = jnp.sum(mixed, axis=0).astype(bf16)
        return _

    lax.fori_loop(0, 8, window, 0)

    ld_o.wait()

    def project_out(nn, _):
        cols = pl.ds(pl.multiple_of(nn * 256, 256), 256)
        o = dot(ctx[...], wo[:, cols])
        for r in range(8):
            base = (r // 4) * 128 + (r % 4) * 8
            parts = [o[base + w * 32 : base + w * 32 + 8] for w in range(4)]
            row = pltpu.roll(jnp.concatenate(parts, axis=0), 4, 0)
            hid[r * 32 : r * 32 + 32, cols] = feat_v[r * 32 : r * 32 + 32, cols].astype(f32) + row
        return _

    lax.fori_loop(0, 4, project_out, 0)

    def norm_hidden(r, _):
        rows = pl.ds(pl.multiple_of(r * 64, 64), 64)
        moe[rows, :] = layer_norm(hid[rows, :]).astype(bf16)
        return _

    lax.fori_loop(0, 4, norm_hidden, 0)

    feat_send, feat_recv = xl_send.at[0], xl_recv.at[0]

    def make_feat(q, _):
        rows = pl.ds(pl.multiple_of(q * 192, 16), 192)
        part = disp[rows, :]
        for n in range(2):
            block = dot(part, moe[:, n * 512 : n * 512 + 512]).astype(bf16)
            xl_send[0, pl.ds(q * 4, 4), :, n * 512 : n * 512 + 512] = block.reshape(4, CAP, 512)
        return _

    lax.fori_loop(0, 4, make_feat, 0)

    def start_feat(k, _):
        exchange(k, feat_send, feat_recv, x_ss, x_rs).start()
        return _

    lax.fori_loop(1, NE, start_feat, 0)
    feat_recv[me] = feat_send[me]

    disp_t[...] = disp[0:ROWS, :].T
    ld_u.wait()

    def transpose_up(i, _):
        rows = pl.ds(pl.multiple_of(i * 256, 256), 256)
        wk[rows, :] = wu[:, pl.ds(pl.multiple_of(i * 256, 256), 256)].T
        wv[rows, :] = wu[:, pl.ds(pl.multiple_of(F + i * 256, 256), 256)].T
        return _

    lax.fori_loop(0, 4, transpose_up, 0)
    ld_d.wait()

    def await_sens(k, _):
        arrival(k, sens_send, sens_recv, l_ss, l_rs).wait_recv()
        arrival(k, meta_send, meta_recv, m_ss, m_rs).wait_recv()
        return _

    lax.fori_loop(1, NE, await_sens, 0)

    def first_grads(i, _):
        rows = pl.ds(pl.multiple_of(i * 256, 256), 256)
        block = dot(wd[rows, :], xl_recv[1].reshape(ROWS, F), NT)
        a2[1, pl.ds(pl.multiple_of(i * 256, 256), 256), :] = block.astype(bf16)
        return _

    lax.fori_loop(0, 8, first_grads, 0)

    meta_all = meta_recv[...].reshape(256, 128)
    spread = (iota((128, ROWS), 0) == lax.rem(iota((128, ROWS), 1), CAP)).astype(f32).astype(bf16)
    ids = dot(meta_all, spread)
    own_part = iota((256, ROWS), 0) == lax.div(iota((256, ROWS), 1), CAP) * 16
    other = jnp.sum(jnp.where(own_part, ids, 0.0), axis=0, keepdims=True) - me.astype(f32)
    eye_r = (iota((NE, NE), 0) == iota((NE, NE), 1)).astype(f32).astype(bf16)
    router_t = dot(eye_r, router[...], NT).astype(bf16)

    def await_feat(k, _):
        arrival(k, feat_send, feat_recv, x_ss, x_rs).wait_recv()
        return _

    lax.fori_loop(1, NE, await_feat, 0)

    logits = dot(router_t, xl_recv[0].reshape(ROWS, F), NT)
    sig = 1.0 / (1.0 + jnp.exp(-logits))
    expert = iota((NE, ROWS), 0)
    mine = jnp.sum(jnp.where(expert == me, sig, 0.0), axis=0, keepdims=True)
    others = jnp.sum(jnp.where(expert.astype(f32) == other, sig, 0.0), axis=0, keepdims=True)
    gate_v[...] = jnp.broadcast_to(mine / (mine + others), (8, ROWS))

    def activate(i):
        def run(weight_t, start):
            u = dot(weight_t[pl.ds(pl.multiple_of(start, 256), 256), :], xl_recv[0].reshape(ROWS, F), NT)
            gate = gate_v[0:1, :]
            u2 = u * u
            t = jnp.tanh(GELU_A * u * (1.0 + GELU_B * u2))
            half = 0.5 * (1.0 + t)
            rows = pl.ds(pl.multiple_of(i * 256, 256), 256)
            a2[0, rows, :] = (u * half * gate).astype(bf16)
            slope = half + 0.5 * u * (1.0 - t * t) * (GELU_A + (3.0 * GELU_A * GELU_B) * u2)
            a2[1, rows, :] = (a2[1, rows, :].astype(f32) * gate * slope).astype(bf16)

        @pl.when(i < 4)
        def _():
            run(wk, i * 256)

        @pl.when(i >= 4)
        def _():
            run(wv, (i - 4) * 256)

    def activate_blocks(lo, hi):
        def body(i, _):
            activate(i)
            return _

        lax.fori_loop(lo, hi, body, 0)

    rv_send = sens_send

    def make_results():
        def drain(k, _):
            exchange(k, sens_send, sens_recv, l_ss, l_rs).wait_send()
            return _

        lax.fori_loop(1, NE, drain, 0)
        for half in range(2):
            lanes = slice(half * 384, (half + 1) * 384)

            def turn(i, _):
                cols = pl.ds(pl.multiple_of(i * 256, 256), 256)
                hgn[:, cols] = a2[0, cols, lanes].T
                return _

            lax.fori_loop(0, 8, turn, 0)

            def product(i, _):
                cols = pl.ds(pl.multiple_of(i * 256, 256), 256)
                block = dot(hgn[...], wd[:, cols]).astype(bf16)
                xl_send[1, half * 8 : half * 8 + 8, :, cols] = block.reshape(8, CAP, 256)
                return _

            lax.fori_loop(0, 4, product, 0)

        def start(k, _):
            exchange(k, rv_send, ret, t_ss, t_rs).start()
            return _

        lax.fori_loop(1, NE, start, 0)
        ret[me] = rv_send[me]

    def column_chunk(j):
        shift = jnp.where(j == 0, 2, jnp.where(j == 1, 1, jnp.where(j == 2, 3, 0)))
        return lax.rem(xpos + shift, 4)

    def core_copy(g, j):
        return rep_copy(stage.at[g, j, 1 - core], crecv.at[g, j], c_ss.at[g, j], c_rs.at[g, j], partner)

    def make_pieces(g):
        kind = lax.rem(g, 2)
        hb = lax.div(g, 2)

        def piece(j, _):
            cols = pl.ds(pl.multiple_of(column_chunk(j) * 256, 256), 256)
            for h in range(2):
                rows = pl.ds(pl.multiple_of(hb * HB + h * 256, 256), 256)
                right = xl_recv[1 - kind, :, :, cols].reshape(ROWS, 256)
                block = dot(a2[kind, rows, :], right).astype(bf16)
                stage[g, j, 0, h] = block[:, 0:128]
                stage[g, j, 1, h] = block[:, 128:256]
            core_copy(g, j).start()
            return _

        lax.fori_loop(0, 4, piece, 0)

    def hop(g, which):
        src = [
            stage.at[g, 0, core, 0], stage.at[g, 1, core, 1], stage.at[g, 1, core, 0],
            stage.at[g, 0, core, 1], stage.at[g, 2, core, 0], stage.at[g, 2, core, 1],
        ][which]
        dst = [
            r2.at[g, 0], rf.at[g, 0, 1], rf.at[g, 0, 0],
            r2.at[g, 1], rf.at[g, 1, 0], rf.at[g, 1, 1],
        ][which]
        return rep_copy(src, dst, x2_ss.at[g, which], x2_rs.at[g, which], x_next if which < 3 else x_prev)

    def add_cores(g):
        for j in range(4):
            core_copy(g, j).wait_recv()
            for h in range(2):
                total = stage[g, j, core, h].astype(f32) + crecv[g, j, h].astype(f32)
                stage[g, j, core, h] = total.astype(bf16)
            for which in {0: (0, 3), 1: (1,), 2: (4,), 3: ()}[j]:
                hop(g, which).start()

    def add_far(g):
        hop(g, 0).wait_recv()
        total = stage[g, 1, core, 0].astype(f32) + r2[g, 0].astype(f32)
        stage[g, 1, core, 0] = total.astype(bf16)
        hop(g, 2).start()
        hop(g, 3).wait_recv()
        total = stage[g, 2, core, 1].astype(f32) + r2[g, 1].astype(f32)
        stage[g, 2, core, 1] = total.astype(bf16)
        hop(g, 5).start()

    def finish(g):
        for which in (1, 2, 4, 5):
            hop(g, which).wait_recv()
        hb = lax.div(g, 2)
        for h in range(2):
            total = (
                stage[g, 3, core, h].astype(f32)
                + rf[g, 0, h].astype(f32)
                + rf[g, 1, h].astype(f32)
            )
            start = pl.multiple_of(hb * HB + h * 256, 256)

            @pl.when(lax.rem(g, 2) == 0)
            def _():
                out_down[pl.ds(start, 256), :] = total

            @pl.when(lax.rem(g, 2) == 1)
            def _():
                out_up[:, pl.ds(start, 256)] = total.T

    def step(s, carry):
        @pl.when(s == 0)
        def _():
            activate_blocks(0, 2)

        @pl.when(s == 1)
        def _():
            activate_blocks(2, 6)

        @pl.when(s == 2)
        def _():
            activate_blocks(6, 8)

        @pl.when(s < GROUPS)
        def _():
            make_pieces(s)

        @pl.when((s >= 1) & (s < GROUPS + 1))
        def _():
            add_cores(s - 1)

        @pl.when((s >= 2) & (s < GROUPS + 2))
        def _():
            add_far(s - 2)

        @pl.when(s >= 3)
        def _():
            finish(s - 3)

        @pl.when(s == 2)
        def _():
            make_results()

        return carry

    lax.fori_loop(0, GROUPS + 3, step, 0)

    def await_results(k, _):
        arrival(k, rv_send, ret, t_ss, t_rs).wait_recv()
        return _

    lax.fori_loop(1, NE, await_results, 0)

    def combine(i, _):
        cols = pl.ds(pl.multiple_of(i * 256, 256), 256)
        mixture = dot(disp_t[...], ret[:, :, cols].reshape(ROWS, 256))
        out_layer[:, cols] = (hid[:, cols] + mixture).astype(bf16)
        return _

    lax.fori_loop(0, 4, combine, 0)

    for c in halo_copies:
        c.wait_send()

    def drain_tiles(k, _):
        exchange(k, meta_send, meta_recv, m_ss, m_rs).wait_send()
        exchange(k, feat_send, feat_recv, x_ss, x_rs).wait_send()
        exchange(k, rv_send, ret, t_ss, t_rs).wait_send()
        return _

    lax.fori_loop(1, NE, drain_tiles, 0)

    def drain_groups(g, _):
        for j in range(4):
            core_copy(g, j).wait_send()
        for which in range(6):
            hop(g, which).wait_send()
        return _

    lax.fori_loop(0, GROUPS, drain_groups, 0)


def on_device(
    patch_features, labels, assigned_specialists, loss_sensitivity,
    attn_qkv, attn_out, router, expert_up, expert_down,
):
    hbm = pl.BlockSpec(memory_space=pl.ANY)
    vmem = pl.BlockSpec(memory_space=pltpu.VMEM)
    dma = pltpu.SemaphoreType.DMA

    def buf(*shape, dtype=bf16):
        return pltpu.VMEM(shape, dtype)

    scratch = [
        buf(T, F), buf(T, F), buf(F, F), buf(F, F), buf(F, F), buf(F, F), buf(F, FFW), buf(FFW, F),
        buf(T, F), buf(T, F), buf(T, F), buf(T, F), buf(8, 64, F), buf(8, 64, F), buf(T, F),
        buf(2 * T, 128), buf(T, F, dtype=f32), buf(T, F),
        buf(ROWS + 128 - CAP, T), buf(T, ROWS), buf(NE, 16, 128), buf(NE, 16, 128),
        buf(2, NE, CAP, F), buf(2, NE, CAP, F), buf(NE, CAP, F), buf(2, FFW, ROWS),
        buf(ROWS // 2, FFW), buf(8, ROWS, dtype=f32),
        buf(GROUPS, 4, 2, 2, 256, 128), buf(GROUPS, 4, 2, 256, 128),
        buf(GROUPS, 2, 256, 128), buf(GROUPS, 2, 2, 256, 128),
        dma((8,)), dma((2,)), dma((2,)),
        dma((NE,)), dma((NE,)), dma((NE,)), dma((NE,)), dma((NE,)), dma((NE,)), dma((NE,)), dma((NE,)),
        dma((GROUPS, 4)), dma((GROUPS, 4)), dma((GROUPS, 6)), dma((GROUPS, 6)),
    ]
    layer, up, down = pl.pallas_call(
        kernel,
        out_shape=(
            jax.ShapeDtypeStruct((T, F), bf16),
            jax.ShapeDtypeStruct((F // 8, FFW), f32),
            jax.ShapeDtypeStruct((FFW, F // 8), f32),
        ),
        in_specs=[hbm, vmem, vmem, hbm, hbm, hbm, vmem, hbm, hbm],
        out_specs=(vmem, vmem, vmem),
        scratch_shapes=scratch,
        compiler_params=pltpu.CompilerParams(
            collective_id=0, has_side_effects=True, vmem_limit_bytes=62 * 1024 * 1024
        ),
        name="layer",
    )(
        patch_features[0], labels, assigned_specialists[0], loss_sensitivity[0],
        attn_qkv, attn_out, router, expert_up[0], expert_down[0],
    )
    return layer[None], up[None], down[None]


def solution(mesh):
    return jax.shard_map(
        on_device,
        mesh=mesh,
        in_specs=(
            P("rep", "tile", None), P(), P("rep", "tile", None), P("rep", "tile", None),
            P(), P(), P(), P("tile", None, None), P("tile", None, None),
        ),
        out_specs=(P("rep", "tile", None), P("tile", "rep", None), P("tile", None, "rep")),
        check_vma=False,
    )
```

```python
import functools

import jax
import jax.numpy as jnp
from jax import lax
from jax.experimental import pallas as pl
from jax.experimental.pallas import tpu as pltpu
from jax.sharding import PartitionSpec as P

F = 1024
FFW = 2048
NE = 16
CAP = 48
T = 256
ROWS = NE * CAP
HB = 512
NB = FFW // HB
GROUPS = 2 * NB
EARLY = 6
OFFSETS = sorted(
    [(a, b) for a in range(4) for b in range(4) if (a, b) != (0, 0)],
    key=lambda o: -(min(o[0], 4 - o[0]) + min(o[1], 4 - o[1])),
)
QW = 256
SCALE = 32 ** (-0.5)
EPSILON = 1e-05
GELU_A = 0.7978845608028654
GELU_B = 0.044715
f32 = jnp.float32
bf16 = jnp.bfloat16
MESH = pl.DeviceIdType.MESH

NN = (((1,), (0,)), ((), ()))
NT = (((1,), (1,)), ((), ()))
TN = (((0,), (0,)), ((), ()))


def dot(a, b, dims=NN):
    return lax.dot_general(a, b, dims, preferred_element_type=f32)


def iota(shape, dim):
    return lax.broadcasted_iota(jnp.int32, shape, dim)


def layer_norm(values):
    center = values - jnp.mean(values, axis=-1, keepdims=True)
    spread = jnp.mean(center * center, axis=-1, keepdims=True)
    return center * lax.rsqrt(spread + EPSILON)


def norm_to_windows(src, dst, pairs):
    for p in pairs:
        y = layer_norm(src[p * 64 : p * 64 + 64, :].astype(f32))
        y0 = pltpu.roll(y[:32], 28, 0)
        y1 = pltpu.roll(y[32:], 28, 0)
        for w in range(4):
            block = jnp.concatenate([y0[8 * w : 8 * w + 8], y1[8 * w : 8 * w + 8]], axis=0)
            start = (p // 2) * 128 + w * 32 + (p % 2) * 16
            dst[start : start + 16, :] = block.astype(bf16)


def kernel(
    feat, labels, assigned, sens, w_qkv, w_out, router, w_up, w_down,
    out_layer, out_up, out_down,
    feat_v, sens_v, wq, wk, wv, wo, wu, wd,
    halo, n_own, n_halo, q_own, k_all, v_all, ctx, oh, hid, moe,
    disp, disp_t, meta_send, meta_recv, xl_send, xl_recv, ret, a2, gate_v,
    stage, crecv, r2, rf,
    load_sem, halo_ss, halo_rs, l_ss, l_rs, m_ss, m_rs, x_ss, x_rs, t_ss, t_rs,
    c_ss, c_rs, x2_ss, x2_rs,
):
    me = lax.axis_index("tile")
    rep = lax.axis_index("rep")
    core = lax.rem(rep, 2)
    xpos = lax.div(rep, 2)
    partner = rep + 1 - 2 * core
    x_next = lax.rem(rep + 2, 8)
    x_prev = lax.rem(rep + 6, 8)

    loads = [
        pltpu.make_async_copy(s, d, load_sem.at[i])
        for i, (s, d) in enumerate(
            [
                (feat, feat_v),
                (sens, sens_v),
                (w_qkv.at[:, F : 2 * F], wk),
                (w_qkv.at[:, 2 * F : 3 * F], wv),
                (w_qkv.at[:, 0:F], wq),
                (w_out, wo),
                (w_down, wd),
                (w_up, wu),
            ]
        )
    ]
    for c in loads[:5]:
        c.start()
    ld_feat, ld_sens, ld_k, ld_v, ld_q, ld_o, ld_d, ld_u = loads

    barrier = pltpu.get_barrier_semaphore()
    y, z = lax.rem(me, 4), lax.div(me, 4)
    to_tile = [lax.rem(z + b, 4) * 4 + lax.rem(y + a, 4) for a, b in OFFSETS]
    from_tile = [lax.rem(z + 4 - b, 4) * 4 + lax.rem(y + 4 - a, 4) for a, b in OFFSETS]
    for t in to_tile:
        pl.semaphore_signal(barrier, inc=1, device_id={"tile": t}, device_id_type=MESH)
    for r in (partner, x_next, x_prev):
        pl.semaphore_signal(barrier, inc=1, device_id={"rep": r}, device_id_type=MESH)
    pl.semaphore_wait(barrier, NE - 1 + 3)

    def tile_copy(src, dst, ss, rs, target):
        return pltpu.make_async_remote_copy(
            src_ref=src, dst_ref=dst, send_sem=ss, recv_sem=rs,
            device_id={"tile": target}, device_id_type=MESH,
        )

    def rep_copy(src, dst, ss, rs, target):
        return pltpu.make_async_remote_copy(
            src_ref=src, dst_ref=dst, send_sem=ss, recv_sem=rs,
            device_id={"rep": target}, device_id_type=MESH,
        )

    t_next = lax.rem(me + 1, NE)
    t_prev = lax.rem(me + NE - 1, NE)
    halo_copies = [
        tile_copy(feat.at[T // 2 : T, :], halo.at[0 : T // 2, :], halo_ss.at[0], halo_rs.at[0], t_next),
        tile_copy(feat.at[0 : T // 2, :], halo.at[T // 2 : T, :], halo_ss.at[1], halo_rs.at[1], t_prev),
    ]
    for c in halo_copies:
        c.start()

    def exchange(i, src, dst, ss, rs):
        t = to_tile[i]
        return tile_copy(src.at[t], dst.at[me], ss.at[i], rs.at[i], t)

    def arrival(i, src, dst, ss, rs):
        t = from_tile[i]
        return tile_copy(src.at[t], dst.at[t], ss.at[i], rs.at[i], t)

    others = range(NE - 1)

    ids_t = assigned[...]
    expert = iota((NE, T), 0)
    member_t = jnp.where((ids_t[0:1] == expert) | (ids_t[1:2] == expert), 1.0, 0.0)
    before = (iota((T, T), 0) < iota((T, T), 1)).astype(f32).astype(bf16)
    rank_t = dot(member_t.astype(bf16), before)
    slot_t = jnp.where(member_t > 0.5, rank_t, -1.0)
    slots = iota((CAP, T), 0).astype(f32)
    for e in range(NE):
        disp[e * CAP : (e + 1) * CAP, :] = jnp.where(slot_t[e : e + 1] == slots, 1.0, 0.0).astype(bf16)
    disp[ROWS:, :] = jnp.zeros((128 - CAP, T), bf16)
    id_sum = jnp.sum(member_t * expert.astype(f32), axis=0, keepdims=True)
    id_rows = jnp.broadcast_to(id_sum, (16, T)).astype(bf16)

    ld_sens.wait()

    def dispatch(src, kind):
        for n in range(2):
            cols = slice(n * 512, n * 512 + 512)
            block = dot(disp[0:ROWS, :], src[:, cols]).astype(bf16)
            xl_send[kind, :, :, cols] = block.reshape(NE, CAP, 512)

    dispatch(sens_v, 1)

    def make_meta(e, _):
        rows = disp[pl.ds(pl.multiple_of(e * CAP, 16), 128), :]
        meta_send[e] = dot(id_rows, rows, NT).astype(bf16)
        return _

    lax.fori_loop(0, NE, make_meta, 0)
    sens_send, sens_recv = xl_send.at[1], xl_recv.at[1]

    def start_sens(which):
        for i in which:
            exchange(i, sens_send, sens_recv, l_ss, l_rs).start()
            exchange(i, meta_send, meta_recv, m_ss, m_rs).start()

    start_sens(range(EARLY))
    sens_recv[me] = sens_send[me]
    meta_recv[me] = meta_send[me]

    ld_feat.wait()
    norm_to_windows(feat_v, n_own, range(4))

    def project(src, weight, dst, start):
        block = dot(src[...], weight[...]).astype(bf16)
        dst[:, start : start + 32, :] = block.reshape(8, 32, F)

    ld_k.wait()
    project(n_own, wk, k_all, 0)
    ld_v.wait()
    project(n_own, wv, v_all, 0)
    ld_q.wait()
    q_own[...] = dot(n_own[...], wq[...]).astype(bf16)
    for c in loads[5:]:
        c.start()

    n = iota((2 * T, 1), 0)
    is_halo = n >= T
    m = jnp.where(is_halo, n - T, n)
    band, win, row4, col8 = m >> 7, (m >> 5) & 3, (m >> 3) & 3, m & 7
    col = (win * 8 + col8 + 4) & 31
    grid_row = me * 8 + jnp.where(is_halo, 12 * band - 4, 4 * band) + row4
    valid = (grid_row >= 0) & (grid_row < 128)
    pick = jnp.where(grid_row == iota((2 * T, 128), 1), 1.0, 0.0).astype(bf16)
    by_row = dot(pick, labels[...].astype(f32).astype(bf16), NT)
    lab = jnp.sum(jnp.where(iota((2 * T, 32), 1) == col, by_row, 0.0), axis=1, keepdims=True)
    lab = jnp.where(valid, lab + jnp.where(col < 4, 4.0, 0.0), -1.0)
    oh[...] = jnp.where(lab == iota((2 * T, 128), 1).astype(f32), 1.0, 0.0).astype(bf16)

    for c in halo_copies:
        c.wait_recv()
    norm_to_windows(halo, n_halo, range(4))
    project(n_halo, wk, k_all, 32)
    project(n_halo, wv, v_all, 32)

    diag = (iota((QW, QW), 0) >> 5) == (iota((QW, QW), 1) >> 5)

    def window_row(b, _):
        parts = []
        for w in range(4):
            bw = b * 4 + w
            rows = pl.ds(pl.multiple_of(bw * 32, 32), 32)
            halo_rows = pl.ds(pl.multiple_of(T + bw * 32, 32), 32)
            oq = oh[rows, :]
            ok = jnp.concatenate([oq, oh[halo_rows, :]], axis=0)
            bias = jnp.concatenate([(dot(oq, ok, NT) - 1.0) * 1e30] * 8, axis=0)
            parts += [(bw, rows, slice(g * QW, (g + 1) * QW), bias) for g in range(4)]
        all_scores = []
        for bw, rows, cols, bias in parts:
            qg = jnp.concatenate([q_own[rows, cols]] * 8, axis=0)
            qg = jnp.where(diag, qg, jnp.zeros_like(qg))
            all_scores.append(dot(qg, k_all[bw, :, cols], NT) * SCALE + bias)
        all_weights = []
        for scores in all_scores:
            expo = jnp.exp(scores - jnp.max(scores, axis=1, keepdims=True))
            all_weights.append((expo * (1.0 / jnp.sum(expo, axis=1, keepdims=True))).astype(bf16))
        for (bw, rows, cols, bias), weights in zip(parts, all_weights):
            mixed = dot(weights, v_all[bw, :, cols])
            mixed = jnp.where(diag, mixed, 0.0).reshape(8, 32, QW)
            ctx[rows, cols] = jnp.sum(mixed, axis=0).astype(bf16)
        return _

    lax.fori_loop(0, 2, window_row, 0)

    ld_o.wait()

    o = dot(ctx[...], wo[...])
    for r in range(8):
        base = (r // 4) * 128 + (r % 4) * 8
        parts = [o[base + w * 32 : base + w * 32 + 8] for w in range(4)]
        row = pltpu.roll(jnp.concatenate(parts, axis=0), 4, 0)
        hid[r * 32 : r * 32 + 32, :] = feat_v[r * 32 : r * 32 + 32, :].astype(f32) + row

    def norm_hidden(r, _):
        rows = pl.ds(pl.multiple_of(r * 64, 64), 64)
        moe[rows, :] = layer_norm(hid[rows, :]).astype(bf16)
        return _

    lax.fori_loop(0, 4, norm_hidden, 0)

    feat_send, feat_recv = xl_send.at[0], xl_recv.at[0]

    dispatch(moe, 0)
    for i in others:
        exchange(i, feat_send, feat_recv, x_ss, x_rs).start()
    start_sens(range(EARLY, NE - 1))
    feat_recv[me] = feat_send[me]

    disp_t[...] = disp[0:ROWS, :].T
    ld_u.wait()

    def transpose_up(i, _):
        rows = pl.ds(pl.multiple_of(i * 256, 256), 256)
        wk[rows, :] = wu[:, pl.ds(pl.multiple_of(i * 256, 256), 256)].T
        wv[rows, :] = wu[:, pl.ds(pl.multiple_of(F + i * 256, 256), 256)].T
        return _

    lax.fori_loop(0, 4, transpose_up, 0)

    for i in others:
        arrival(i, meta_send, meta_recv, m_ss, m_rs).wait_recv()

    meta_all = meta_recv[...].reshape(256, 128)
    spread = (iota((128, ROWS), 0) == lax.rem(iota((128, ROWS), 1), CAP)).astype(f32).astype(bf16)
    ids = dot(meta_all, spread)
    own_part = iota((256, ROWS), 0) == lax.div(iota((256, ROWS), 1), CAP) * 16
    other = jnp.sum(jnp.where(own_part, ids, 0.0), axis=0, keepdims=True) - me.astype(f32)

    for i in others:
        arrival(i, feat_send, feat_recv, x_ss, x_rs).wait_recv()

    logits = dot(router[...], xl_recv[0].reshape(ROWS, F), NT)
    sig = 1.0 / (1.0 + jnp.exp(-logits))
    expert = iota((NE, ROWS), 0)
    mine = jnp.sum(jnp.where(expert == me, sig, 0.0), axis=0, keepdims=True)
    theirs = jnp.sum(jnp.where(expert.astype(f32) == other, sig, 0.0), axis=0, keepdims=True)
    gate_v[...] = jnp.broadcast_to(mine / (mine + theirs), (8, ROWS))

    def activate(weight_t, half):
        def body(i, _):
            start = pl.multiple_of(i * HB, HB)
            u = dot(weight_t[pl.ds(start, HB), :], xl_recv[0].reshape(ROWS, F), NT)
            gate = gate_v[0:1, :]
            u2 = u * u
            t = jnp.tanh(GELU_A * u * (1.0 + GELU_B * u2))
            rise = 0.5 * (1.0 + t)
            rows = pl.ds(pl.multiple_of(half * F + i * HB, HB), HB)
            a2[0, rows, :] = (u * rise * gate).astype(bf16)
            slope = rise + 0.5 * u * (1.0 - t * t) * (GELU_A + (3.0 * GELU_A * GELU_B) * u2)
            a2[1, rows, :] = (slope * gate).astype(bf16)
            return _

        lax.fori_loop(0, F // HB, body, 0)

    activate(wk, 0)
    activate(wv, 1)
    ld_d.wait()
    for i in others:
        arrival(i, sens_send, sens_recv, l_ss, l_rs).wait_recv()

    def first_grads():
        def body(i, _):
            rows = pl.ds(pl.multiple_of(i * HB, HB), HB)
            block = dot(wd[rows, :], xl_recv[1].reshape(ROWS, F), NT)
            a2[1, rows, :] = (block * a2[1, rows, :].astype(f32)).astype(bf16)
            return _

        lax.fori_loop(0, NB, body, 0)

    rv_send = sens_send

    def drain_sens():
        for i in others:
            exchange(i, sens_send, sens_recv, l_ss, l_rs).wait_send()

    def make_results(half):
        lanes = slice(half * 384, (half + 1) * 384)

        def product(i, _):
            cols = pl.ds(pl.multiple_of(i * 512, 512), 512)
            block = dot(a2[0, :, lanes], wd[:, cols], TN).astype(bf16)
            xl_send[1, half * 8 : half * 8 + 8, :, cols] = block.reshape(8, CAP, 512)
            return _

        lax.fori_loop(0, 2, product, 0)

    def send_results():
        for i in others:
            exchange(i, rv_send, ret, t_ss, t_rs).start()
        ret[me] = rv_send[me]

    def chunk(away):
        return lax.rem(xpos + away, 4)

    def core_copy(g):
        return rep_copy(stage.at[g, 1 - core], crecv.at[g], c_ss.at[g], c_rs.at[g], partner)

    def make_pieces(g):
        kind = lax.div(g, NB)
        rows = pl.ds(pl.multiple_of(lax.rem(g, NB) * HB, HB), HB)
        block = dot(a2[kind, rows, :], xl_recv[1 - kind].reshape(ROWS, F)).astype(bf16)
        for q in range(4):
            for c in range(2):
                for h in range(2):
                    start = (2 * q + c) * 128
                    stage[g, c, q, h] = block[h * 256 : h * 256 + 256, start : start + 128]
        core_copy(g).start()

    def hop(g, which):
        away, h = [(2, 0), (1, 1), (1, 0), (2, 1), (3, 0), (3, 1)][which]
        dst = [
            r2.at[g, 0], rf.at[g, 0, 1], rf.at[g, 0, 0],
            r2.at[g, 1], rf.at[g, 1, 0], rf.at[g, 1, 1],
        ][which]
        src = stage.at[g, core, chunk(away), h]
        return rep_copy(src, dst, x2_ss.at[g, which], x2_rs.at[g, which], x_next if which < 3 else x_prev)

    def add_cores(g):
        core_copy(g).wait_recv()
        for away, sends in ((2, (0, 3)), (1, (1,)), (3, (4,)), (0, ())):
            q = chunk(away)
            for h in range(2):
                total = stage[g, core, q, h].astype(f32) + crecv[g, q, h].astype(f32)
                stage[g, core, q, h] = total.astype(bf16)
            for which in sends:
                hop(g, which).start()

    def add_far(g):
        for first, away, h, second in ((0, 1, 0, 2), (3, 3, 1, 5)):
            hop(g, first).wait_recv()
            q = chunk(away)
            total = stage[g, core, q, h].astype(f32) + r2[g, h].astype(f32)
            stage[g, core, q, h] = total.astype(bf16)
            hop(g, second).start()

    def finish(g):
        for which in (1, 2, 4, 5):
            hop(g, which).wait_recv()
        hb = lax.rem(g, NB)
        for h in range(2):
            total = (
                stage[g, core, xpos, h].astype(f32)
                + rf[g, 0, h].astype(f32)
                + rf[g, 1, h].astype(f32)
            )
            start = pl.multiple_of(hb * HB + h * 256, 256)

            @pl.when(g < NB)
            def _():
                out_down[pl.ds(start, 256), :] = total

            @pl.when(g >= NB)
            def _():
                out_up[:, pl.ds(start, 256)] = total.T

    def step(s, carry):
        @pl.when(s < GROUPS)
        def _():
            make_pieces(s)

        @pl.when((s >= 1) & (s < GROUPS + 1))
        def _():
            add_cores(s - 1)

        @pl.when((s >= 2) & (s < GROUPS + 2))
        def _():
            add_far(s - 2)

        @pl.when(s >= 3)
        def _():
            finish(s - 3)

        @pl.when(s == 2)
        def _():
            drain_sens()
            make_results(0)

        @pl.when(s == 3)
        def _():
            first_grads()

        @pl.when(s == 4)
        def _():
            make_results(1)
            send_results()

        return carry

    lax.fori_loop(0, GROUPS + 3, step, 0)

    for i in others:
        arrival(i, rv_send, ret, t_ss, t_rs).wait_recv()

    def combine(i, _):
        cols = pl.ds(pl.multiple_of(i * 256, 256), 256)
        mixture = dot(disp_t[...], ret[:, :, cols].reshape(ROWS, 256))
        out_layer[:, cols] = (hid[:, cols] + mixture).astype(bf16)
        return _

    lax.fori_loop(0, 4, combine, 0)

    for c in halo_copies:
        c.wait_send()

    for i in others:
        exchange(i, meta_send, meta_recv, m_ss, m_rs).wait_send()
        exchange(i, feat_send, feat_recv, x_ss, x_rs).wait_send()
        exchange(i, rv_send, ret, t_ss, t_rs).wait_send()

    def drain_groups(g, _):
        core_copy(g).wait_send()
        for which in range(6):
            hop(g, which).wait_send()
        return _

    lax.fori_loop(0, GROUPS, drain_groups, 0)


def hand_over(layer, up, down, out_layer, out_up, out_down):
    out_layer[...] = layer[...]
    out_up[...] = up[...]
    out_down[...] = down[...]


def on_device(
    patch_features, labels, assigned_specialists, loss_sensitivity,
    attn_qkv, attn_out, router, expert_up, expert_down,
):
    hbm = pl.BlockSpec(memory_space=pl.ANY)
    vmem = pl.BlockSpec(memory_space=pltpu.VMEM)
    dma = pltpu.SemaphoreType.DMA

    def buf(*shape, dtype=bf16):
        return pltpu.VMEM(shape, dtype)

    scratch = [
        buf(T, F), buf(T, F), buf(F, F), buf(F, F), buf(F, F), buf(F, F), buf(F, FFW), buf(FFW, F),
        buf(T, F), buf(T, F), buf(T, F), buf(T, F), buf(8, 64, F), buf(8, 64, F), buf(T, F),
        buf(2 * T, 128), buf(T, F, dtype=f32), buf(T, F),
        buf(ROWS + 128 - CAP, T), buf(T, ROWS), buf(NE, 16, 128), buf(NE, 16, 128),
        buf(2, NE, CAP, F), buf(2, NE, CAP, F), buf(NE, CAP, F), buf(2, FFW, ROWS),
        buf(8, ROWS, dtype=f32),
        buf(GROUPS, 2, 4, 2, 256, 128), buf(GROUPS, 4, 2, 256, 128),
        buf(GROUPS, 2, 256, 128), buf(GROUPS, 2, 2, 256, 128),
        dma((8,)), dma((2,)), dma((2,)),
        dma((NE,)), dma((NE,)), dma((NE,)), dma((NE,)), dma((NE,)), dma((NE,)), dma((NE,)), dma((NE,)),
        dma((GROUPS,)), dma((GROUPS,)), dma((GROUPS, 6)), dma((GROUPS, 6)),
    ]
    layer, up, down = pl.pallas_call(
        kernel,
        out_shape=(
            jax.ShapeDtypeStruct((T, F), bf16),
            jax.ShapeDtypeStruct((F // 8, FFW), f32),
            jax.ShapeDtypeStruct((FFW, F // 8), f32),
        ),
        in_specs=[hbm, vmem, vmem, hbm, hbm, hbm, vmem, hbm, hbm],
        out_specs=(vmem, vmem, vmem),
        scratch_shapes=scratch,
        compiler_params=pltpu.CompilerParams(
            collective_id=0, has_side_effects=True, vmem_limit_bytes=62 * 1024 * 1024
        ),
        name="layer",
    )(
        patch_features[0], labels.T, assigned_specialists[0].T, loss_sensitivity[0],
        attn_qkv, attn_out, router.T, expert_up[0], expert_down[0],
    )
    blocks = [pl.BlockSpec(shape, lambda i: (i, 0)) for shape in ((64, F), (32, FFW), (512, 128))]
    layer, up, down = pl.pallas_call(
        hand_over,
        out_shape=(
            jax.ShapeDtypeStruct((T, F), bf16),
            jax.ShapeDtypeStruct((F // 8, FFW), f32),
            jax.ShapeDtypeStruct((FFW, F // 8), f32),
        ),
        grid=(4,),
        in_specs=blocks,
        out_specs=tuple(blocks),
        name="hand_over",
    )(layer, up, down)
    return layer[None], up[None], down[None]


def solution(mesh):
    return jax.shard_map(
        on_device,
        mesh=mesh,
        in_specs=(
            P("rep", "tile", None), P(), P("rep", "tile", None), P("rep", "tile", None),
            P(), P(), P(), P("tile", None, None), P("tile", None, None),
        ),
        out_specs=(P("rep", "tile", None), P("tile", "rep", None), P("tile", None, "rep")),
        check_vma=False,
    )
```

```python
import functools

import jax
import jax.numpy as jnp
from jax import lax
from jax.experimental import pallas as pl
from jax.experimental.pallas import tpu as pltpu
from jax.sharding import PartitionSpec as P

F = 1024
FFW = 2048
NE = 16
CAP = 48
T = 256
ROWS = NE * CAP
HB = 512
NB = FFW // HB
GROUPS = 2 * NB
EARLY = 6
OFFSETS = sorted(
    [(a, b) for a in range(4) for b in range(4) if (a, b) != (0, 0)],
    key=lambda o: -(min(o[0], 4 - o[0]) + min(o[1], 4 - o[1])),
)
QW = 256
SCALE = 32 ** (-0.5)
EPSILON = 1e-05
GELU_A = 0.7978845608028654
GELU_B = 0.044715
f32 = jnp.float32
bf16 = jnp.bfloat16
MESH = pl.DeviceIdType.MESH

NN = (((1,), (0,)), ((), ()))
NT = (((1,), (1,)), ((), ()))
TN = (((0,), (0,)), ((), ()))


def dot(a, b, dims=NN):
    return lax.dot_general(a, b, dims, preferred_element_type=f32)


def iota(shape, dim):
    return lax.broadcasted_iota(jnp.int32, shape, dim)


def layer_norm(values):
    center = values - jnp.mean(values, axis=-1, keepdims=True)
    spread = jnp.mean(center * center, axis=-1, keepdims=True)
    return center * lax.rsqrt(spread + EPSILON)


def norm_to_windows(src, dst, pairs):
    for p in pairs:
        y = layer_norm(src[p * 64 : p * 64 + 64, :].astype(f32))
        y0 = pltpu.roll(y[:32], 28, 0)
        y1 = pltpu.roll(y[32:], 28, 0)
        for w in range(4):
            block = jnp.concatenate([y0[8 * w : 8 * w + 8], y1[8 * w : 8 * w + 8]], axis=0)
            start = (p // 2) * 128 + w * 32 + (p % 2) * 16
            dst[start : start + 16, :] = block.astype(bf16)


def kernel(
    feat, labels, assigned, sens, w_qkv, w_out, router, w_up, w_down,
    out_layer, out_up, out_down,
    feat_v, sens_v, wq, wk, wv, wo, wu, wd,
    halo, n_own, n_halo, q_own, k_all, v_all, ctx, oh, hid, moe,
    disp, disp_t, meta_send, meta_recv, xl_send, xl_recv, ret, a2, gate_v,
    stage, crecv, r2, rf,
    load_sem, halo_ss, halo_rs, l_ss, l_rs, m_ss, m_rs, x_ss, x_rs, t_ss, t_rs,
    c_ss, c_rs, x2_ss, x2_rs,
    layer_v, up_v, down_v, layer_sem, up_sem, down_sem,
):
    me = lax.axis_index("tile")
    rep = lax.axis_index("rep")
    core = lax.rem(rep, 2)
    xpos = lax.div(rep, 2)
    partner = rep + 1 - 2 * core
    x_next = lax.rem(rep + 2, 8)
    x_prev = lax.rem(rep + 6, 8)

    loads = [
        pltpu.make_async_copy(s, d, load_sem.at[i])
        for i, (s, d) in enumerate(
            [
                (feat, feat_v),
                (sens, sens_v),
                (w_qkv.at[:, F : 2 * F], wk),
                (w_qkv.at[:, 2 * F : 3 * F], wv),
                (w_qkv.at[:, 0:F], wq),
                (w_out, wo),
                (w_down, wd),
                (w_up, wu),
            ]
        )
    ]
    for c in loads[:5]:
        c.start()
    ld_feat, ld_sens, ld_k, ld_v, ld_q, ld_o, ld_d, ld_u = loads

    barrier = pltpu.get_barrier_semaphore()
    y, z = lax.rem(me, 4), lax.div(me, 4)
    to_tile = [lax.rem(z + b, 4) * 4 + lax.rem(y + a, 4) for a, b in OFFSETS]
    from_tile = [lax.rem(z + 4 - b, 4) * 4 + lax.rem(y + 4 - a, 4) for a, b in OFFSETS]
    for t in to_tile:
        pl.semaphore_signal(barrier, inc=1, device_id={"tile": t}, device_id_type=MESH)
    for r in (partner, x_next, x_prev):
        pl.semaphore_signal(barrier, inc=1, device_id={"rep": r}, device_id_type=MESH)
    pl.semaphore_wait(barrier, NE - 1 + 3)

    def tile_copy(src, dst, ss, rs, target):
        return pltpu.make_async_remote_copy(
            src_ref=src, dst_ref=dst, send_sem=ss, recv_sem=rs,
            device_id={"tile": target}, device_id_type=MESH,
        )

    def rep_copy(src, dst, ss, rs, target):
        return pltpu.make_async_remote_copy(
            src_ref=src, dst_ref=dst, send_sem=ss, recv_sem=rs,
            device_id={"rep": target}, device_id_type=MESH,
        )

    t_next = lax.rem(me + 1, NE)
    t_prev = lax.rem(me + NE - 1, NE)
    halo_copies = [
        tile_copy(feat.at[T // 2 : T, :], halo.at[0 : T // 2, :], halo_ss.at[0], halo_rs.at[0], t_next),
        tile_copy(feat.at[0 : T // 2, :], halo.at[T // 2 : T, :], halo_ss.at[1], halo_rs.at[1], t_prev),
    ]
    for c in halo_copies:
        c.start()

    def exchange(i, src, dst, ss, rs):
        t = to_tile[i]
        return tile_copy(src.at[t], dst.at[me], ss.at[i], rs.at[i], t)

    def arrival(i, src, dst, ss, rs):
        t = from_tile[i]
        return tile_copy(src.at[t], dst.at[t], ss.at[i], rs.at[i], t)

    others = range(NE - 1)

    ids_t = assigned[...]
    expert = iota((NE, T), 0)
    member_t = jnp.where((ids_t[0:1] == expert) | (ids_t[1:2] == expert), 1.0, 0.0)
    before = (iota((T, T), 0) < iota((T, T), 1)).astype(f32).astype(bf16)
    rank_t = dot(member_t.astype(bf16), before)
    slot_t = jnp.where(member_t > 0.5, rank_t, -1.0)
    slots = iota((CAP, T), 0).astype(f32)
    for e in range(NE):
        disp[e * CAP : (e + 1) * CAP, :] = jnp.where(slot_t[e : e + 1] == slots, 1.0, 0.0).astype(bf16)
    disp[ROWS:, :] = jnp.zeros((128 - CAP, T), bf16)
    id_sum = jnp.sum(member_t * expert.astype(f32), axis=0, keepdims=True)
    id_rows = jnp.broadcast_to(id_sum, (16, T)).astype(bf16)

    ld_sens.wait()

    def dispatch(src, kind):
        for n in range(2):
            cols = slice(n * 512, n * 512 + 512)
            block = dot(disp[0:ROWS, :], src[:, cols]).astype(bf16)
            xl_send[kind, :, :, cols] = block.reshape(NE, CAP, 512)

    dispatch(sens_v, 1)

    def make_meta(e, _):
        rows = disp[pl.ds(pl.multiple_of(e * CAP, 16), 128), :]
        meta_send[e] = dot(id_rows, rows, NT).astype(bf16)
        return _

    lax.fori_loop(0, NE, make_meta, 0)
    sens_send, sens_recv = xl_send.at[1], xl_recv.at[1]

    def start_sens(which):
        for i in which:
            exchange(i, sens_send, sens_recv, l_ss, l_rs).start()

    for i in others:
        exchange(i, meta_send, meta_recv, m_ss, m_rs).start()
    start_sens(range(EARLY))
    sens_recv[me] = sens_send[me]
    meta_recv[me] = meta_send[me]

    ld_feat.wait()
    norm_to_windows(feat_v, n_own, range(4))

    def project(src, weight, dst, start):
        block = dot(src[...], weight[...]).astype(bf16)
        dst[:, start : start + 32, :] = block.reshape(8, 32, F)

    ld_k.wait()
    project(n_own, wk, k_all, 0)
    ld_v.wait()
    project(n_own, wv, v_all, 0)
    ld_q.wait()
    q_own[...] = dot(n_own[...], wq[...]).astype(bf16)
    for c in loads[5:]:
        c.start()

    n = iota((2 * T, 1), 0)
    is_halo = n >= T
    m = jnp.where(is_halo, n - T, n)
    band, win, row4, col8 = m >> 7, (m >> 5) & 3, (m >> 3) & 3, m & 7
    col = (win * 8 + col8 + 4) & 31
    grid_row = me * 8 + jnp.where(is_halo, 12 * band - 4, 4 * band) + row4
    valid = (grid_row >= 0) & (grid_row < 128)
    pick = jnp.where(grid_row == iota((2 * T, 128), 1), 1.0, 0.0).astype(bf16)
    by_row = dot(pick, labels[...].astype(f32).astype(bf16), NT)
    lab = jnp.sum(jnp.where(iota((2 * T, 32), 1) == col, by_row, 0.0), axis=1, keepdims=True)
    lab = jnp.where(valid, lab + jnp.where(col < 4, 4.0, 0.0), -1.0)
    oh[...] = jnp.where(lab == iota((2 * T, 128), 1).astype(f32), 1.0, 0.0).astype(bf16)

    for c in halo_copies:
        c.wait_recv()
    norm_to_windows(halo, n_halo, range(4))
    project(n_halo, wk, k_all, 32)
    project(n_halo, wv, v_all, 32)

    diag = (iota((QW, QW), 0) >> 5) == (iota((QW, QW), 1) >> 5)

    def window_row(b, _):
        parts = []
        for w in range(4):
            bw = b * 4 + w
            rows = pl.ds(pl.multiple_of(bw * 32, 32), 32)
            halo_rows = pl.ds(pl.multiple_of(T + bw * 32, 32), 32)
            oq = oh[rows, :]
            ok = jnp.concatenate([oq, oh[halo_rows, :]], axis=0)
            bias = jnp.concatenate([(dot(oq, ok, NT) - 1.0) * 1e30] * 8, axis=0)
            parts += [(bw, rows, slice(g * QW, (g + 1) * QW), bias) for g in range(4)]
        all_scores = []
        for bw, rows, cols, bias in parts:
            qg = jnp.concatenate([q_own[rows, cols]] * 8, axis=0)
            qg = jnp.where(diag, qg, jnp.zeros_like(qg))
            all_scores.append(dot(qg, k_all[bw, :, cols], NT) * SCALE + bias)
        all_weights = []
        for scores in all_scores:
            expo = jnp.exp(scores - jnp.max(scores, axis=1, keepdims=True))
            all_weights.append((expo * (1.0 / jnp.sum(expo, axis=1, keepdims=True))).astype(bf16))
        for (bw, rows, cols, bias), weights in zip(parts, all_weights):
            mixed = dot(weights, v_all[bw, :, cols])
            mixed = jnp.where(diag, mixed, 0.0).reshape(8, 32, QW)
            ctx[rows, cols] = jnp.sum(mixed, axis=0).astype(bf16)
        return _

    lax.fori_loop(0, 2, window_row, 0)

    ld_o.wait()

    o = dot(ctx[...], wo[...])
    for r in range(8):
        base = (r // 4) * 128 + (r % 4) * 8
        parts = [o[base + w * 32 : base + w * 32 + 8] for w in range(4)]
        row = pltpu.roll(jnp.concatenate(parts, axis=0), 4, 0)
        hid[r * 32 : r * 32 + 32, :] = feat_v[r * 32 : r * 32 + 32, :].astype(f32) + row

    def norm_hidden(r, _):
        rows = pl.ds(pl.multiple_of(r * 64, 64), 64)
        moe[rows, :] = layer_norm(hid[rows, :]).astype(bf16)
        return _

    lax.fori_loop(0, 4, norm_hidden, 0)

    feat_send, feat_recv = xl_send.at[0], xl_recv.at[0]

    dispatch(moe, 0)
    for i in others:
        exchange(i, feat_send, feat_recv, x_ss, x_rs).start()
    feat_recv[me] = feat_send[me]

    disp_t[...] = disp[0:ROWS, :].T
    ld_u.wait()

    def transpose_up(i, _):
        rows = pl.ds(pl.multiple_of(i * 256, 256), 256)
        wk[rows, :] = wu[:, pl.ds(pl.multiple_of(i * 256, 256), 256)].T
        wv[rows, :] = wu[:, pl.ds(pl.multiple_of(F + i * 256, 256), 256)].T
        return _

    lax.fori_loop(0, 4, transpose_up, 0)

    for i in others:
        arrival(i, meta_send, meta_recv, m_ss, m_rs).wait_recv()

    meta_all = meta_recv[...].reshape(256, 128)
    spread = (iota((128, ROWS), 0) == lax.rem(iota((128, ROWS), 1), CAP)).astype(f32).astype(bf16)
    ids = dot(meta_all, spread)
    own_part = iota((256, ROWS), 0) == lax.div(iota((256, ROWS), 1), CAP) * 16
    other = jnp.sum(jnp.where(own_part, ids, 0.0), axis=0, keepdims=True) - me.astype(f32)

    for i in others:
        exchange(i, feat_send, feat_recv, x_ss, x_rs).wait_send()
    start_sens(range(EARLY, NE - 1))
    for i in others:
        arrival(i, feat_send, feat_recv, x_ss, x_rs).wait_recv()

    logits = dot(router[...], xl_recv[0].reshape(ROWS, F), NT)
    sig = 1.0 / (1.0 + jnp.exp(-logits))
    expert = iota((NE, ROWS), 0)
    mine = jnp.sum(jnp.where(expert == me, sig, 0.0), axis=0, keepdims=True)
    theirs = jnp.sum(jnp.where(expert.astype(f32) == other, sig, 0.0), axis=0, keepdims=True)
    gate_v[...] = jnp.broadcast_to(mine / (mine + theirs), (8, ROWS))

    def activate(weight_t, half):
        def body(i, _):
            start = pl.multiple_of(i * HB, HB)
            u = dot(weight_t[pl.ds(start, HB), :], xl_recv[0].reshape(ROWS, F), NT)
            gate = gate_v[0:1, :]
            u2 = u * u
            t = jnp.tanh(GELU_A * u * (1.0 + GELU_B * u2))
            rise = 0.5 * (1.0 + t)
            rows = pl.ds(pl.multiple_of(half * F + i * HB, HB), HB)
            a2[0, rows, :] = (u * rise * gate).astype(bf16)
            slope = rise + 0.5 * u * (1.0 - t * t) * (GELU_A + (3.0 * GELU_A * GELU_B) * u2)
            a2[1, rows, :] = (slope * gate).astype(bf16)
            return _

        lax.fori_loop(0, F // HB, body, 0)

    activate(wk, 0)
    activate(wv, 1)
    ld_d.wait()
    for i in others:
        arrival(i, sens_send, sens_recv, l_ss, l_rs).wait_recv()

    def first_grads():
        def body(i, _):
            rows = pl.ds(pl.multiple_of(i * HB, HB), HB)
            block = dot(wd[rows, :], xl_recv[1].reshape(ROWS, F), NT)
            a2[1, rows, :] = (block * a2[1, rows, :].astype(f32)).astype(bf16)
            return _

        lax.fori_loop(0, NB, body, 0)

    rv_send = sens_send

    def drain_sens():
        for i in others:
            exchange(i, sens_send, sens_recv, l_ss, l_rs).wait_send()

    def make_results(half):
        lanes = slice(half * 384, (half + 1) * 384)

        def product(i, _):
            cols = pl.ds(pl.multiple_of(i * 512, 512), 512)
            block = dot(a2[0, :, lanes], wd[:, cols], TN).astype(bf16)
            xl_send[1, half * 8 : half * 8 + 8, :, cols] = block.reshape(8, CAP, 512)
            return _

        lax.fori_loop(0, 2, product, 0)

    def send_results():
        for i in others:
            exchange(i, rv_send, ret, t_ss, t_rs).start()
        ret[me] = rv_send[me]

    def chunk(away):
        return lax.rem(xpos + away, 4)

    def core_copy(g):
        return rep_copy(stage.at[g, 1 - core], crecv.at[g], c_ss.at[g], c_rs.at[g], partner)

    def make_pieces(g):
        kind = lax.div(g, NB)
        rows = pl.ds(pl.multiple_of(lax.rem(g, NB) * HB, HB), HB)
        block = dot(a2[kind, rows, :], xl_recv[1 - kind].reshape(ROWS, F)).astype(bf16)
        for q in range(4):
            for c in range(2):
                for h in range(2):
                    start = (2 * q + c) * 128
                    stage[g, c, q, h] = block[h * 256 : h * 256 + 256, start : start + 128]
        core_copy(g).start()

    def hop(g, which):
        away, h = [(2, 0), (1, 1), (1, 0), (2, 1), (3, 0), (3, 1)][which]
        dst = [
            r2.at[g, 0], rf.at[g, 0, 1], rf.at[g, 0, 0],
            r2.at[g, 1], rf.at[g, 1, 0], rf.at[g, 1, 1],
        ][which]
        src = stage.at[g, core, chunk(away), h]
        return rep_copy(src, dst, x2_ss.at[g, which], x2_rs.at[g, which], x_next if which < 3 else x_prev)

    def add_cores(g):
        core_copy(g).wait_recv()
        for away, sends in ((2, (0, 3)), (1, (1,)), (3, (4,)), (0, ())):
            q = chunk(away)
            for h in range(2):
                total = stage[g, core, q, h].astype(f32) + crecv[g, q, h].astype(f32)
                stage[g, core, q, h] = total.astype(bf16)
            for which in sends:
                hop(g, which).start()

    def add_far(g):
        for first, away, h, second in ((0, 1, 0, 2), (3, 3, 1, 5)):
            hop(g, first).wait_recv()
            q = chunk(away)
            total = stage[g, core, q, h].astype(f32) + r2[g, h].astype(f32)
            stage[g, core, q, h] = total.astype(bf16)
            hop(g, second).start()

    def finish(g):
        for which in (1, 2, 4, 5):
            hop(g, which).wait_recv()
        parts = []
        for h in range(2):
            parts.append(
                stage[g, core, xpos, h].astype(f32)
                + rf[g, 0, h].astype(f32)
                + rf[g, 1, h].astype(f32)
            )
        return parts

    def down_copy(hb):
        rows = pl.ds(pl.multiple_of(hb * HB, HB), HB)
        return pltpu.make_async_copy(down_v.at[rows, :], out_down.at[rows, :], down_sem.at[hb])

    def up_copy(hb):
        cols = pl.ds(pl.multiple_of(hb * HB, HB), HB)
        return pltpu.make_async_copy(up_v.at[:, cols], out_up.at[:, cols], up_sem.at[hb])

    def finish_down(hb, _):
        for h, total in enumerate(finish(hb)):
            down_v[pl.ds(pl.multiple_of(hb * HB + h * 256, 256), 256), :] = total
        down_copy(hb).start()
        return _

    def finish_up(hb, _):
        for h, total in enumerate(finish(NB + hb)):
            up_v[:, pl.ds(pl.multiple_of(hb * HB + h * 256, 256), 256)] = total.T
        up_copy(hb).start()
        return _

    def run_groups(first):
        def body(i, carry):
            make_pieces(first + i)

            @pl.when(i >= 1)
            def _():
                add_cores(first + i - 1)

            return carry

        lax.fori_loop(0, NB, body, 0)
        add_cores(first + NB - 1)

    run_groups(0)
    add_far(0)
    drain_sens()
    make_results(0)
    add_far(1)
    make_results(1)
    send_results()
    add_far(2)
    first_grads()
    add_far(3)
    run_groups(NB)

    def far_up(i, _):
        add_far(NB + i)
        finish_down(i, 0)
        return _

    lax.fori_loop(0, NB, far_up, 0)

    for i in others:
        arrival(i, rv_send, ret, t_ss, t_rs).wait_recv()

    def combine(i, _):
        cols = pl.ds(pl.multiple_of(i * 256, 256), 256)
        mixture = dot(disp_t[...], ret[:, :, cols].reshape(ROWS, 256))
        layer_v[:, cols] = (hid[:, cols] + mixture).astype(bf16)
        return _

    lax.fori_loop(0, 4, combine, 0)
    layer_copy = pltpu.make_async_copy(layer_v, out_layer, layer_sem)
    layer_copy.start()
    lax.fori_loop(0, NB, finish_up, 0)

    layer_copy.wait()
    for hb in range(NB):
        down_copy(hb).wait()
        up_copy(hb).wait()
    for c in halo_copies:
        c.wait_send()

    for i in others:
        exchange(i, meta_send, meta_recv, m_ss, m_rs).wait_send()
        exchange(i, rv_send, ret, t_ss, t_rs).wait_send()

    def drain_groups(g, _):
        core_copy(g).wait_send()
        for which in range(6):
            hop(g, which).wait_send()
        return _

    lax.fori_loop(0, GROUPS, drain_groups, 0)


def hand_over(layer, up, down, out_layer, out_up, out_down, sem):
    pairs = ((layer, out_layer), (up, out_up), (down, out_down))
    copies = [pltpu.make_async_copy(a, b, sem.at[i]) for i, (a, b) in enumerate(pairs)]
    for c in copies:
        c.start()
    for c in copies:
        c.wait()


def on_device(
    patch_features, labels, assigned_specialists, loss_sensitivity,
    attn_qkv, attn_out, router, expert_up, expert_down,
):
    hbm = pl.BlockSpec(memory_space=pl.ANY)
    vmem = pl.BlockSpec(memory_space=pltpu.VMEM)
    dma = pltpu.SemaphoreType.DMA

    def buf(*shape, dtype=bf16):
        return pltpu.VMEM(shape, dtype)

    scratch = [
        buf(T, F), buf(T, F), buf(F, F), buf(F, F), buf(F, F), buf(F, F), buf(F, FFW), buf(FFW, F),
        buf(T, F), buf(T, F), buf(T, F), buf(T, F), buf(8, 64, F), buf(8, 64, F), buf(T, F),
        buf(2 * T, 128), buf(T, F, dtype=f32), buf(T, F),
        buf(ROWS + 128 - CAP, T), buf(T, ROWS), buf(NE, 16, 128), buf(NE, 16, 128),
        buf(2, NE, CAP, F), buf(2, NE, CAP, F), buf(NE, CAP, F), buf(2, FFW, ROWS),
        buf(8, ROWS, dtype=f32),
        buf(GROUPS, 2, 4, 2, 256, 128), buf(GROUPS, 4, 2, 256, 128),
        buf(GROUPS, 2, 256, 128), buf(GROUPS, 2, 2, 256, 128),
        dma((8,)), dma((2,)), dma((2,)),
        dma((NE,)), dma((NE,)), dma((NE,)), dma((NE,)), dma((NE,)), dma((NE,)), dma((NE,)), dma((NE,)),
        dma((GROUPS,)), dma((GROUPS,)), dma((GROUPS, 6)), dma((GROUPS, 6)),
        buf(T, F), buf(F // 8, FFW, dtype=f32), buf(FFW, F // 8, dtype=f32),
        dma, dma((NB,)), dma((NB,)),
    ]
    layer, up, down = pl.pallas_call(
        kernel,
        out_shape=(
            jax.ShapeDtypeStruct((T, F), bf16),
            jax.ShapeDtypeStruct((F // 8, FFW), f32),
            jax.ShapeDtypeStruct((FFW, F // 8), f32),
        ),
        in_specs=[hbm, vmem, vmem, hbm, hbm, hbm, vmem, hbm, hbm],
        out_specs=(hbm, hbm, hbm),
        scratch_shapes=scratch,
        compiler_params=pltpu.CompilerParams(
            collective_id=0, has_side_effects=True, vmem_limit_bytes=62 * 1024 * 1024
        ),
        name="layer",
    )(
        patch_features[0], labels.T, assigned_specialists[0].T, loss_sensitivity[0],
        attn_qkv, attn_out, router.T, expert_up[0], expert_down[0],
    )
    layer, up, down = pl.pallas_call(
        hand_over,
        out_shape=(
            jax.ShapeDtypeStruct((T, F), bf16),
            jax.ShapeDtypeStruct((F // 8, FFW), f32),
            jax.ShapeDtypeStruct((FFW, F // 8), f32),
        ),
        in_specs=[vmem, vmem, vmem],
        out_specs=(hbm, hbm, hbm),
        scratch_shapes=[dma((3,))],
        name="hand_over",
    )(layer, up, down)
    return layer[None], up[None], down[None]


def solution(mesh):
    return jax.shard_map(
        on_device,
        mesh=mesh,
        in_specs=(
            P("rep", "tile", None), P(), P("rep", "tile", None), P("rep", "tile", None),
            P(), P(), P(), P("tile", None, None), P("tile", None, None),
        ),
        out_specs=(P("rep", "tile", None), P("tile", "rep", None), P("tile", None, "rep")),
        check_vma=False,
    )
```

```python
import functools

import jax
import jax.numpy as jnp
from jax import lax
from jax.experimental import pallas as pl
from jax.experimental.pallas import tpu as pltpu
from jax.sharding import PartitionSpec as P

F = 1024
FFW = 2048
NE = 16
CAP = 48
T = 256
ROWS = NE * CAP
HB = 512
NB = FFW // HB
GROUPS = 2 * NB
OFFSETS = sorted(
    [(a, b) for a in range(4) for b in range(4) if (a, b) != (0, 0)],
    key=lambda o: -(min(o[0], 4 - o[0]) + min(o[1], 4 - o[1])),
)
QW = 256
SCALE = 32 ** (-0.5)
EPSILON = 1e-05
GELU_A = 0.7978845608028654
GELU_B = 0.044715
f32 = jnp.float32
bf16 = jnp.bfloat16
MESH = pl.DeviceIdType.MESH

NN = (((1,), (0,)), ((), ()))
NT = (((1,), (1,)), ((), ()))
TN = (((0,), (0,)), ((), ()))


def dot(a, b, dims=NN):
    return lax.dot_general(a, b, dims, preferred_element_type=f32)


def iota(shape, dim):
    return lax.broadcasted_iota(jnp.int32, shape, dim)


def layer_norm(values):
    center = values - jnp.mean(values, axis=-1, keepdims=True)
    spread = jnp.mean(center * center, axis=-1, keepdims=True)
    return center * lax.rsqrt(spread + EPSILON)


def norm_to_windows(src, dst, pairs):
    for p in pairs:
        y = layer_norm(src[p * 64 : p * 64 + 64, :].astype(f32))
        y0 = pltpu.roll(y[:32], 28, 0)
        y1 = pltpu.roll(y[32:], 28, 0)
        for w in range(4):
            block = jnp.concatenate([y0[8 * w : 8 * w + 8], y1[8 * w : 8 * w + 8]], axis=0)
            start = (p // 2) * 128 + w * 32 + (p % 2) * 16
            dst[start : start + 16, :] = block.astype(bf16)


def kernel(
    feat, labels, assigned, sens, w_qkv, w_out, router, w_up, w_down,
    out_layer, out_up, out_down,
    feat_v, sens_v, w3, wo, wu, wd,
    halo, n_own, n_halo, q_own, k_all, v_all, ctx, oh, hid, moe,
    disp, disp_t, meta_send, meta_recv, x_send, x_recv, l_send, l_recv, l_full, ret, a2, gate_v,
    stage, crecv, r2, rf,
    load_sem, halo_ss, halo_rs, l_ss, l_rs, m_ss, m_rs, x_ss, x_rs, t_ss, t_rs,
    c_ss, c_rs, x2_ss, x2_rs,
    layer_v, up_v, down_v, layer_sem, up_sem, down_sem,
):
    wq, wk, wv = w3.at[0], w3.at[1], w3.at[2]
    me = lax.axis_index("tile")
    rep = lax.axis_index("rep")
    core = lax.rem(rep, 2)
    xpos = lax.div(rep, 2)
    partner = rep + 1 - 2 * core
    x_next = lax.rem(rep + 2, 8)
    x_prev = lax.rem(rep + 6, 8)

    loads = [
        pltpu.make_async_copy(s, d, load_sem.at[i])
        for i, (s, d) in enumerate(
            [
                (feat, feat_v),
                (sens, sens_v),
                (w_qkv.at[:, F : 2 * F], wk),
                (w_qkv.at[:, 2 * F : 3 * F], wv),
                (w_qkv.at[:, 0:F], wq),
                (w_out, wo),
                (w_down, wd),
                (w_up, wu),
            ]
        )
    ]
    for c in loads[:5]:
        c.start()
    ld_feat, ld_sens, ld_k, ld_v, ld_q, ld_o, ld_d, ld_u = loads

    barrier = pltpu.get_barrier_semaphore()
    y, z = lax.rem(me, 4), lax.div(me, 4)
    to_tile = [lax.rem(z + b, 4) * 4 + lax.rem(y + a, 4) for a, b in OFFSETS]
    from_tile = [lax.rem(z + 4 - b, 4) * 4 + lax.rem(y + 4 - a, 4) for a, b in OFFSETS]
    for t in to_tile:
        pl.semaphore_signal(barrier, inc=1, device_id={"tile": t}, device_id_type=MESH)
    for r in (partner, x_next, x_prev):
        pl.semaphore_signal(barrier, inc=1, device_id={"rep": r}, device_id_type=MESH)
    pl.semaphore_wait(barrier, NE - 1 + 3)

    def tile_copy(src, dst, ss, rs, target):
        return pltpu.make_async_remote_copy(
            src_ref=src, dst_ref=dst, send_sem=ss, recv_sem=rs,
            device_id={"tile": target}, device_id_type=MESH,
        )

    def rep_copy(src, dst, ss, rs, target):
        return pltpu.make_async_remote_copy(
            src_ref=src, dst_ref=dst, send_sem=ss, recv_sem=rs,
            device_id={"rep": target}, device_id_type=MESH,
        )

    t_next = lax.rem(me + 1, NE)
    t_prev = lax.rem(me + NE - 1, NE)
    halo_copies = [
        tile_copy(feat.at[T // 2 : T, :], halo.at[0 : T // 2, :], halo_ss.at[0], halo_rs.at[0], t_next),
        tile_copy(feat.at[0 : T // 2, :], halo.at[T // 2 : T, :], halo_ss.at[1], halo_rs.at[1], t_prev),
    ]
    for c in halo_copies:
        c.start()

    def exchange(i, src, dst, ss, rs):
        t = to_tile[i]
        return tile_copy(src.at[t], dst.at[me], ss.at[i], rs.at[i], t)

    def arrival(i, src, dst, ss, rs):
        t = from_tile[i]
        return tile_copy(src.at[t], dst.at[t], ss.at[i], rs.at[i], t)

    others = range(NE - 1)

    ids_t = assigned[...]
    expert = iota((NE, T), 0)
    member_t = jnp.where((ids_t[0:1] == expert) | (ids_t[1:2] == expert), 1.0, 0.0)
    before = (iota((T, T), 0) < iota((T, T), 1)).astype(f32).astype(bf16)
    rank_t = dot(member_t.astype(bf16), before)
    slot_t = jnp.where(member_t > 0.5, rank_t, -1.0)
    slots = iota((CAP, T), 0).astype(f32)
    for e in range(NE):
        disp[e * CAP : (e + 1) * CAP, :] = jnp.where(slot_t[e : e + 1] == slots, 1.0, 0.0).astype(bf16)
    disp[ROWS:, :] = jnp.zeros((128 - CAP, T), bf16)
    id_sum = jnp.sum(member_t * expert.astype(f32), axis=0, keepdims=True)
    id_rows = jnp.broadcast_to(id_sum, (16, T)).astype(bf16)

    ld_sens.wait()

    def halves(block):
        tiles = [block[:, q * 128 : q * 128 + 128] for q in range(8)]
        return [
            jnp.concatenate([tiles[q][:, h * 64 : h * 64 + 64] for q in range(8)], axis=1)
            for h in range(2)
        ]

    for h, part in enumerate(halves(sens_v[...])):
        block = dot(disp[0:ROWS, :], part).astype(bf16)
        l_send[h] = block.reshape(NE, CAP, F // 2)

    def make_meta(e, _):
        rows = disp[pl.ds(pl.multiple_of(e * CAP, 16), 128), :]
        meta_send[e] = dot(id_rows, rows, NT).astype(bf16)
        return _

    lax.fori_loop(0, NE, make_meta, 0)
    def sens_args(h):
        return l_send.at[h], l_recv.at[h], l_ss.at[h], l_rs.at[h]

    for i in others:
        exchange(i, *sens_args(0)).start()
    for i in others:
        exchange(i, meta_send, meta_recv, m_ss, m_rs).start()
    l_recv[0, me] = l_send[0, me]
    l_recv[1, me] = l_send[1, me]
    meta_recv[me] = meta_send[me]

    ld_feat.wait()
    norm_to_windows(feat_v, n_own, range(4))

    def project(src, weight, dst, start):
        block = dot(src[...], weight[...]).astype(bf16)
        dst[:, start : start + 32, :] = block.reshape(8, 32, F)

    ld_k.wait()
    project(n_own, wk, k_all, 0)
    ld_v.wait()
    project(n_own, wv, v_all, 0)
    ld_q.wait()
    q_own[...] = dot(n_own[...], wq[...]).astype(bf16)
    for c in loads[5:]:
        c.start()

    n = iota((2 * T, 1), 0)
    is_halo = n >= T
    m = jnp.where(is_halo, n - T, n)
    band, win, row4, col8 = m >> 7, (m >> 5) & 3, (m >> 3) & 3, m & 7
    col = (win * 8 + col8 + 4) & 31
    grid_row = me * 8 + jnp.where(is_halo, 12 * band - 4, 4 * band) + row4
    valid = (grid_row >= 0) & (grid_row < 128)
    pick = jnp.where(grid_row == iota((2 * T, 128), 1), 1.0, 0.0).astype(bf16)
    by_row = dot(pick, labels[...].astype(f32).astype(bf16), NT)
    lab = jnp.sum(jnp.where(iota((2 * T, 32), 1) == col, by_row, 0.0), axis=1, keepdims=True)
    lab = jnp.where(valid, lab + jnp.where(col < 4, 4.0, 0.0), -1.0)
    oh[...] = jnp.where(lab == iota((2 * T, 128), 1).astype(f32), 1.0, 0.0).astype(bf16)

    for c in halo_copies:
        c.wait_recv()
    norm_to_windows(halo, n_halo, range(4))
    project(n_halo, wk, k_all, 32)
    project(n_halo, wv, v_all, 32)

    diag = (iota((QW, QW), 0) >> 5) == (iota((QW, QW), 1) >> 5)

    def window_row(b, _):
        parts = []
        for w in range(4):
            bw = b * 4 + w
            rows = pl.ds(pl.multiple_of(bw * 32, 32), 32)
            halo_rows = pl.ds(pl.multiple_of(T + bw * 32, 32), 32)
            oq = oh[rows, :]
            ok = jnp.concatenate([oq, oh[halo_rows, :]], axis=0)
            bias = jnp.concatenate([(dot(oq, ok, NT) - 1.0) * 1e30] * 8, axis=0)
            parts += [(bw, rows, slice(g * QW, (g + 1) * QW), bias) for g in range(4)]
        all_scores = []
        for bw, rows, cols, bias in parts:
            qg = jnp.concatenate([q_own[rows, cols]] * 8, axis=0)
            qg = jnp.where(diag, qg, jnp.zeros_like(qg))
            all_scores.append(dot(qg, k_all[bw, :, cols], NT) * SCALE + bias)
        all_weights = []
        for scores in all_scores:
            expo = jnp.exp(scores - jnp.max(scores, axis=1, keepdims=True))
            all_weights.append((expo * (1.0 / jnp.sum(expo, axis=1, keepdims=True))).astype(bf16))
        for (bw, rows, cols, bias), weights in zip(parts, all_weights):
            mixed = dot(weights, v_all[bw, :, cols])
            mixed = jnp.where(diag, mixed, 0.0).reshape(8, 32, QW)
            ctx[rows, cols] = jnp.sum(mixed, axis=0).astype(bf16)
        return _

    lax.fori_loop(0, 2, window_row, 0)

    ld_o.wait()

    o = dot(ctx[...], wo[...])
    for r in range(8):
        base = (r // 4) * 128 + (r % 4) * 8
        parts = [o[base + w * 32 : base + w * 32 + 8] for w in range(4)]
        row = pltpu.roll(jnp.concatenate(parts, axis=0), 4, 0)
        hid[r * 32 : r * 32 + 32, :] = feat_v[r * 32 : r * 32 + 32, :].astype(f32) + row

    def norm_hidden(r, _):
        rows = pl.ds(pl.multiple_of(r * 64, 64), 64)
        moe[rows, :] = layer_norm(hid[rows, :]).astype(bf16)
        return _

    lax.fori_loop(0, 4, norm_hidden, 0)

    for n in range(2):
        cols = slice(n * 512, n * 512 + 512)
        x_send[:, :, cols] = dot(disp[0:ROWS, :], moe[:, cols]).astype(bf16).reshape(NE, CAP, 512)
    feat_args = (x_send, x_recv, x_ss, x_rs)
    for i in others:
        exchange(i, *feat_args).start()
    x_recv[me] = x_send[me]

    disp_t[...] = disp[0:ROWS, :].T
    ld_u.wait()

    def transpose_up(i, _):
        rows = pl.ds(pl.multiple_of(i * 256, 256), 256)
        wk[rows, :] = wu[:, pl.ds(pl.multiple_of(i * 256, 256), 256)].T
        wv[rows, :] = wu[:, pl.ds(pl.multiple_of(F + i * 256, 256), 256)].T
        return _

    lax.fori_loop(0, 4, transpose_up, 0)
    ld_d.wait()

    for i in others:
        arrival(i, meta_send, meta_recv, m_ss, m_rs).wait_recv()

    meta_all = meta_recv[...].reshape(256, 128)
    spread = (iota((128, ROWS), 0) == lax.rem(iota((128, ROWS), 1), CAP)).astype(f32).astype(bf16)
    ids = dot(meta_all, spread)
    own_part = iota((256, ROWS), 0) == lax.div(iota((256, ROWS), 1), CAP) * 16
    other = jnp.sum(jnp.where(own_part, ids, 0.0), axis=0, keepdims=True) - me.astype(f32)

    for i in others:
        exchange(i, *feat_args).wait_send()
    for i in others:
        exchange(i, *sens_args(1)).start()
    for i in others:
        arrival(i, *feat_args).wait_recv()
    for i in others:
        arrival(i, *sens_args(0)).wait_recv()

    logits = dot(router[...], x_recv[...].reshape(ROWS, F), NT)
    sig = 1.0 / (1.0 + jnp.exp(-logits))
    expert = iota((NE, ROWS), 0)
    mine = jnp.sum(jnp.where(expert == me, sig, 0.0), axis=0, keepdims=True)
    theirs = jnp.sum(jnp.where(expert.astype(f32) == other, sig, 0.0), axis=0, keepdims=True)
    gate_v[...] = jnp.broadcast_to(mine / (mine + theirs), (8, ROWS))

    def activate(hb):
        first = pl.multiple_of(lax.rem(hb, 2) * HB, HB)
        u = dot(w3[1 + lax.div(hb, 2), pl.ds(first, HB), :], x_recv[...].reshape(ROWS, F), NT)
        gate = gate_v[0:1, :]
        u2 = u * u
        t = jnp.tanh(GELU_A * u * (1.0 + GELU_B * u2))
        rise = 0.5 * (1.0 + t)
        rows = pl.ds(pl.multiple_of(hb * HB, HB), HB)
        a2[0, rows, :] = (u * rise * gate).astype(bf16)
        slope = rise + 0.5 * u * (1.0 - t * t) * (GELU_A + (3.0 * GELU_A * GELU_B) * u2)
        a2[1, rows, :] = (slope * gate).astype(bf16)

    def first_grads():
        for q in range(4):
            cols = slice(q * 128, q * 128 + 128)
            low = l_recv[0, :, :, cols].reshape(ROWS, 128)
            high = l_recv[1, :, :, cols].reshape(ROWS, 128)
            l_full[:, q * 256 : q * 256 + 128] = jnp.concatenate([low[:, 0:64], high[:, 0:64]], axis=1)
            l_full[:, q * 256 + 128 : q * 256 + 256] = jnp.concatenate([low[:, 64:], high[:, 64:]], axis=1)

        def body(i, _):
            rows = pl.ds(pl.multiple_of(i * HB, HB), HB)
            block = dot(wd[rows, :], l_full[...], NT)
            a2[1, rows, :] = (block * a2[1, rows, :].astype(f32)).astype(bf16)
            return _

        lax.fori_loop(0, NB, body, 0)

    rv_send = x_send
    result_args = (rv_send, ret, t_ss, t_rs)

    def make_results(half):
        lanes = slice(half * 384, (half + 1) * 384)

        def product(i, _):
            cols = pl.ds(pl.multiple_of(i * 512, 512), 512)
            block = dot(a2[0, :, lanes], wd[:, cols], TN).astype(bf16)
            rv_send[half * 8 : half * 8 + 8, :, cols] = block.reshape(8, CAP, 512)
            return _

        lax.fori_loop(0, 2, product, 0)
        for i in others:

            @pl.when((to_tile[i] >= 8 * half) & (to_tile[i] < 8 * half + 8))
            def _(i=i):
                exchange(i, *result_args).start()

    def chunk(away):
        return lax.rem(xpos + away, 4)

    def core_copy(g, h):
        return rep_copy(stage.at[g, 1 - core, h], crecv.at[g, h], c_ss.at[g, h], c_rs.at[g, h], partner)

    def down_group(half, hb):
        return half * 2 + lax.div(hb, 2), lax.rem(hb, 2)

    def make_down(half, hb):
        g, h = down_group(half, hb)
        rows = pl.ds(pl.multiple_of(hb * HB, HB), HB)
        block = dot(a2[0, rows, :], l_recv[half].reshape(ROWS, F // 2)).astype(bf16)
        for q in range(4):
            top = block[0:256, q * 128 : q * 128 + 128]
            low = block[256:512, q * 128 : q * 128 + 128]
            stage[g, 0, h, q] = jnp.concatenate([top[:, 0:64], low[:, 0:64]], axis=1)
            stage[g, 1, h, q] = jnp.concatenate([top[:, 64:], low[:, 64:]], axis=1)
        core_copy(g, h).start()

    def make_up(hb):
        g = NB + hb
        rows = pl.ds(pl.multiple_of(hb * HB, HB), HB)
        block = dot(a2[1, rows, :], x_recv[...].reshape(ROWS, F)).astype(bf16)
        for h in range(2):
            for q in range(4):
                for c in range(2):
                    start = (2 * q + c) * 128
                    stage[g, c, h, q] = block[h * 256 : h * 256 + 256, start : start + 128]
            core_copy(g, h).start()

    def hop(g, which):
        away, h = [(2, 0), (1, 1), (1, 0), (2, 1), (3, 0), (3, 1)][which]
        dst = [
            r2.at[g, 0], rf.at[g, 0, 1], rf.at[g, 0, 0],
            r2.at[g, 1], rf.at[g, 1, 0], rf.at[g, 1, 1],
        ][which]
        src = stage.at[g, core, h, chunk(away)]
        return rep_copy(src, dst, x2_ss.at[g, which], x2_rs.at[g, which], x_next if which < 3 else x_prev)

    def add_cores(g, h):
        core_copy(g, h).wait_recv()
        total = stage[g, core, h].astype(f32) + crecv[g, h].astype(f32)
        stage[g, core, h] = total.astype(bf16)

    def send_half(g, h):
        for which in ((0, 4), (3, 1))[h]:
            hop(g, which).start()

    def add_down(half, hb):
        g, h = down_group(half, hb)
        add_cores(g, h)

        @pl.when(h == 0)
        def _():
            send_half(g, 0)

        @pl.when(h == 1)
        def _():
            send_half(g, 1)

    def add_up(hb):
        for h in range(2):
            add_cores(NB + hb, h)
            send_half(NB + hb, h)

    def add_far(g):
        for first, away, h, second in ((0, 1, 0, 2), (3, 3, 1, 5)):
            hop(g, first).wait_recv()
            q = chunk(away)
            total = stage[g, core, h, q].astype(f32) + r2[g, h].astype(f32)
            stage[g, core, h, q] = total.astype(bf16)
            hop(g, second).start()

    def finish(g):
        for which in (1, 2, 4, 5):
            hop(g, which).wait_recv()
        parts = []
        for h in range(2):
            parts.append(
                stage[g, core, h, xpos].astype(f32)
                + rf[g, 0, h].astype(f32)
                + rf[g, 1, h].astype(f32)
            )
        return parts

    def down_copy(hb):
        rows = pl.ds(pl.multiple_of(hb * HB, HB), HB)
        return pltpu.make_async_copy(down_v.at[rows, :], out_down.at[rows, :], down_sem.at[hb])

    def up_copy(hb):
        cols = pl.ds(pl.multiple_of(hb * HB, HB), HB)
        return pltpu.make_async_copy(up_v.at[:, cols], out_up.at[:, cols], up_sem.at[hb])

    def finish_down(pair, _):
        low, high = finish(pair), finish(2 + pair)
        for h in range(2):
            rows = pl.multiple_of((pair * 2 + h) * HB, HB)
            down_v[pl.ds(rows, 256), :] = jnp.concatenate([low[h][:, 0:64], high[h][:, 0:64]], axis=1)
            down_v[pl.ds(rows + 256, 256), :] = jnp.concatenate([low[h][:, 64:], high[h][:, 64:]], axis=1)
            down_copy(pair * 2 + h).start()
        return _

    def finish_up(hb, _):
        for h, total in enumerate(finish(NB + hb)):
            up_v[:, pl.ds(pl.multiple_of(hb * HB + h * 256, 256), 256)] = total.T
        up_copy(hb).start()
        return _

    def down_groups(half, before):
        def body(hb, carry):
            before(hb)
            make_down(half, hb)

            @pl.when(hb >= 1)
            def _():
                add_down(half, hb - 1)

            return carry

        lax.fori_loop(0, NB, body, 0)
        add_down(half, NB - 1)

    down_groups(0, activate)
    add_far(0)
    for i in others:
        arrival(i, *sens_args(1)).wait_recv()
    down_groups(1, lambda hb: None)
    add_far(1)
    first_grads()
    add_far(2)

    def up_step(hb, carry):
        make_up(hb)

        @pl.when(hb >= 1)
        def _():
            add_up(hb - 1)

        @pl.when(hb == 1)
        def _():
            make_results(0)

        @pl.when(hb == 2)
        def _():
            make_results(1)

        @pl.when(hb >= 2)
        def _():
            add_far(hb + 1)

        return carry

    lax.fori_loop(0, NB, up_step, 0)
    add_up(NB - 1)
    ret[me] = rv_send[me]

    def far_up(i, carry):
        add_far(NB + i)

        @pl.when(i < 3)
        def _():
            finish_down(i - 1, 0)

        return carry

    lax.fori_loop(1, NB, far_up, 0)

    for i in others:
        arrival(i, *result_args).wait_recv()

    def combine(i, _):
        cols = pl.ds(pl.multiple_of(i * 256, 256), 256)
        mixture = dot(disp_t[...], ret[:, :, cols].reshape(ROWS, 256))
        layer_v[:, cols] = (hid[:, cols] + mixture).astype(bf16)
        return _

    lax.fori_loop(0, 4, combine, 0)
    layer_copy = pltpu.make_async_copy(layer_v, out_layer, layer_sem)
    layer_copy.start()
    lax.fori_loop(0, NB, finish_up, 0)

    layer_copy.wait()
    for hb in range(NB):
        down_copy(hb).wait()
        up_copy(hb).wait()
    for c in halo_copies:
        c.wait_send()

    for i in others:
        exchange(i, meta_send, meta_recv, m_ss, m_rs).wait_send()
        exchange(i, *result_args).wait_send()
        exchange(i, *sens_args(0)).wait_send()
        exchange(i, *sens_args(1)).wait_send()

    def drain_groups(g, _):
        for h in range(2):
            core_copy(g, h).wait_send()
        for which in range(6):
            hop(g, which).wait_send()
        return _

    lax.fori_loop(0, GROUPS, drain_groups, 0)


def hand_over(layer, up, down, out_layer, out_up, out_down, layer_v, up_v, down_v, sem_in, sem_out):
    steps = []
    for a, v, b in ((layer, layer_v, out_layer), (up, up_v, out_up), (down, down_v, out_down)):
        rows = a.shape[0] // 4
        for i in range(4):
            part = pl.ds(i * rows, rows)
            n = len(steps)
            steps.append((
                pltpu.make_async_copy(a.at[part, :], v.at[part, :], sem_in.at[n]),
                pltpu.make_async_copy(v.at[part, :], b.at[part, :], sem_out.at[n]),
            ))
    for first, _ in steps:
        first.start()
    for first, second in steps:
        first.wait()
        second.start()
    for _, second in steps:
        second.wait()


def on_device(
    patch_features, labels, assigned_specialists, loss_sensitivity,
    attn_qkv, attn_out, router, expert_up, expert_down,
):
    hbm = pl.BlockSpec(memory_space=pl.ANY)
    vmem = pl.BlockSpec(memory_space=pltpu.VMEM)
    dma = pltpu.SemaphoreType.DMA

    def buf(*shape, dtype=bf16):
        return pltpu.VMEM(shape, dtype)

    scratch = [
        buf(T, F), buf(T, F), buf(3, F, F), buf(F, F), buf(F, FFW), buf(FFW, F),
        buf(T, F), buf(T, F), buf(T, F), buf(T, F), buf(8, 64, F), buf(8, 64, F), buf(T, F),
        buf(2 * T, 128), buf(T, F, dtype=f32), buf(T, F),
        buf(ROWS + 128 - CAP, T), buf(T, ROWS), buf(NE, 16, 128), buf(NE, 16, 128),
        buf(NE, CAP, F), buf(NE, CAP, F), buf(2, NE, CAP, F // 2), buf(2, NE, CAP, F // 2), buf(ROWS, F),
        buf(NE, CAP, F), buf(2, FFW, ROWS),
        buf(8, ROWS, dtype=f32),
        buf(GROUPS, 2, 2, 4, 256, 128), buf(GROUPS, 2, 4, 256, 128),
        buf(GROUPS, 2, 256, 128), buf(GROUPS, 2, 2, 256, 128),
        dma((8,)), dma((2,)), dma((2,)),
        dma((2, NE)), dma((2, NE)), dma((NE,)), dma((NE,)), dma((NE,)), dma((NE,)), dma((NE,)), dma((NE,)),
        dma((GROUPS, 2)), dma((GROUPS, 2)), dma((GROUPS, 6)), dma((GROUPS, 6)),
        buf(T, F), buf(F // 8, FFW, dtype=f32), buf(FFW, F // 8, dtype=f32),
        dma, dma((NB,)), dma((NB,)),
    ]
    layer, up, down = pl.pallas_call(
        kernel,
        out_shape=(
            jax.ShapeDtypeStruct((T, F), bf16),
            jax.ShapeDtypeStruct((F // 8, FFW), f32),
            jax.ShapeDtypeStruct((FFW, F // 8), f32),
        ),
        in_specs=[hbm, vmem, vmem, hbm, hbm, hbm, vmem, hbm, hbm],
        out_specs=(hbm, hbm, hbm),
        scratch_shapes=scratch,
        compiler_params=pltpu.CompilerParams(
            collective_id=0, has_side_effects=True, vmem_limit_bytes=62 * 1024 * 1024
        ),
        name="layer",
    )(
        patch_features[0], labels.T, assigned_specialists[0].T, loss_sensitivity[0],
        attn_qkv, attn_out, router.T, expert_up[0], expert_down[0],
    )
    layer, up, down = pl.pallas_call(
        hand_over,
        out_shape=(
            jax.ShapeDtypeStruct((T, F), bf16),
            jax.ShapeDtypeStruct((F // 8, FFW), f32),
            jax.ShapeDtypeStruct((FFW, F // 8), f32),
        ),
        in_specs=[hbm, hbm, hbm],
        out_specs=(hbm, hbm, hbm),
        scratch_shapes=[
            buf(T, F), buf(F // 8, FFW, dtype=f32), buf(FFW, F // 8, dtype=f32), dma((12,)), dma((12,)),
        ],
        name="hand_over",
    )(layer, up, down)
    return layer[None], up[None], down[None]


def solution(mesh):
    return jax.shard_map(
        on_device,
        mesh=mesh,
        in_specs=(
            P("rep", "tile", None), P(), P("rep", "tile", None), P("rep", "tile", None),
            P(), P(), P(), P("tile", None, None), P("tile", None, None),
        ),
        out_specs=(P("rep", "tile", None), P("tile", "rep", None), P("tile", None, "rep")),
        check_vma=False,
    )
```

```python
import functools

import jax
import jax.numpy as jnp
from jax import lax
from jax.experimental import pallas as pl
from jax.experimental.pallas import tpu as pltpu
from jax.sharding import PartitionSpec as P

F = 1024
FFW = 2048
NE = 16
CAP = 48
T = 256
ROWS = NE * CAP
HB = 512
NB = FFW // HB
GROUPS = 2 * NB
OFFSETS = sorted(
    [(a, b) for a in range(4) for b in range(4) if (a, b) != (0, 0)],
    key=lambda o: -(min(o[0], 4 - o[0]) + min(o[1], 4 - o[1])),
)
QW = 256
SCALE = 32 ** (-0.5)
EPSILON = 1e-05
GELU_A = 0.7978845608028654
GELU_B = 0.044715
f32 = jnp.float32
bf16 = jnp.bfloat16
MESH = pl.DeviceIdType.MESH

NN = (((1,), (0,)), ((), ()))
NT = (((1,), (1,)), ((), ()))
TN = (((0,), (0,)), ((), ()))


def dot(a, b, dims=NN):
    return lax.dot_general(a, b, dims, preferred_element_type=f32)


def iota(shape, dim):
    return lax.broadcasted_iota(jnp.int32, shape, dim)


def layer_norm(values):
    center = values - jnp.mean(values, axis=-1, keepdims=True)
    spread = jnp.mean(center * center, axis=-1, keepdims=True)
    return center * lax.rsqrt(spread + EPSILON)


def norm_to_windows(src, dst, pairs):
    for p in pairs:
        y = layer_norm(src[p * 64 : p * 64 + 64, :].astype(f32))
        y0 = pltpu.roll(y[:32], 28, 0)
        y1 = pltpu.roll(y[32:], 28, 0)
        for w in range(4):
            block = jnp.concatenate([y0[8 * w : 8 * w + 8], y1[8 * w : 8 * w + 8]], axis=0)
            start = (p // 2) * 128 + w * 32 + (p % 2) * 16
            dst[start : start + 16, :] = block.astype(bf16)


def kernel(
    feat, labels, assigned, sens, w_qkv, w_out, router, w_up, w_down,
    out_layer, out_up, out_down,
    feat_v, sens_v, w3, wo, wu, wd,
    halo, n_own, n_halo, q_own, k_all, v_all, ctx, oh, hid, moe,
    disp, disp_t, meta_send, meta_recv, x_send, x_recv, l_send, l_recv, slope_v, ret, a2, gate_v,
    stage, crecv, r2, rf,
    load_sem, halo_ss, halo_rs, l_ss, l_rs, m_ss, m_rs, x_ss, x_rs, t_ss, t_rs,
    c_ss, c_rs, x2_ss, x2_rs,
    layer_v, up_v, down_v, layer_sem, up_sem, down_sem,
):
    wq, wk, wv = w3.at[0], w3.at[1], w3.at[2]
    me = lax.axis_index("tile")
    rep = lax.axis_index("rep")
    core = lax.rem(rep, 2)
    xpos = lax.div(rep, 2)
    partner = rep + 1 - 2 * core
    x_next = lax.rem(rep + 2, 8)
    x_prev = lax.rem(rep + 6, 8)

    loads = [
        pltpu.make_async_copy(s, d, load_sem.at[i])
        for i, (s, d) in enumerate(
            [
                (feat, feat_v),
                (sens, sens_v),
                (w_qkv.at[:, F : 2 * F], wk),
                (w_qkv.at[:, 2 * F : 3 * F], wv),
                (w_qkv.at[:, 0:F], wq),
                (w_out, wo),
                (w_down, wd),
                (w_up, wu),
            ]
        )
    ]
    for c in loads[:5]:
        c.start()
    ld_feat, ld_sens, ld_k, ld_v, ld_q, ld_o, ld_d, ld_u = loads

    barrier = pltpu.get_barrier_semaphore()
    y, z = lax.rem(me, 4), lax.div(me, 4)
    to_tile = [lax.rem(z + b, 4) * 4 + lax.rem(y + a, 4) for a, b in OFFSETS]
    from_tile = [lax.rem(z + 4 - b, 4) * 4 + lax.rem(y + 4 - a, 4) for a, b in OFFSETS]
    for t in to_tile:
        pl.semaphore_signal(barrier, inc=1, device_id={"tile": t}, device_id_type=MESH)
    for r in (partner, x_next, x_prev):
        pl.semaphore_signal(barrier, inc=1, device_id={"rep": r}, device_id_type=MESH)
    pl.semaphore_wait(barrier, NE - 1 + 3)

    def tile_copy(src, dst, ss, rs, target):
        return pltpu.make_async_remote_copy(
            src_ref=src, dst_ref=dst, send_sem=ss, recv_sem=rs,
            device_id={"tile": target}, device_id_type=MESH,
        )

    def rep_copy(src, dst, ss, rs, target):
        return pltpu.make_async_remote_copy(
            src_ref=src, dst_ref=dst, send_sem=ss, recv_sem=rs,
            device_id={"rep": target}, device_id_type=MESH,
        )

    t_next = lax.rem(me + 1, NE)
    t_prev = lax.rem(me + NE - 1, NE)
    halo_copies = [
        tile_copy(feat.at[T // 2 : T, :], halo.at[0 : T // 2, :], halo_ss.at[0], halo_rs.at[0], t_next),
        tile_copy(feat.at[0 : T // 2, :], halo.at[T // 2 : T, :], halo_ss.at[1], halo_rs.at[1], t_prev),
    ]
    for c in halo_copies:
        c.start()

    def exchange(i, src, dst, ss, rs):
        t = to_tile[i]
        return tile_copy(src.at[t], dst.at[me], ss.at[i], rs.at[i], t)

    def arrival(i, src, dst, ss, rs):
        t = from_tile[i]
        return tile_copy(src.at[t], dst.at[t], ss.at[i], rs.at[i], t)

    others = range(NE - 1)

    ids_t = assigned[...]
    expert = iota((NE, T), 0)
    member_t = jnp.where((ids_t[0:1] == expert) | (ids_t[1:2] == expert), 1.0, 0.0)
    before = (iota((T, T), 0) < iota((T, T), 1)).astype(f32).astype(bf16)
    rank_t = dot(member_t.astype(bf16), before)
    slot_t = jnp.where(member_t > 0.5, rank_t, -1.0)
    slots = iota((CAP, T), 0).astype(f32)
    for e in range(NE):
        disp[e * CAP : (e + 1) * CAP, :] = jnp.where(slot_t[e : e + 1] == slots, 1.0, 0.0).astype(bf16)
    disp[ROWS:, :] = jnp.zeros((128 - CAP, T), bf16)
    id_sum = jnp.sum(member_t * expert.astype(f32), axis=0, keepdims=True)
    id_rows = jnp.broadcast_to(id_sum, (16, T)).astype(bf16)

    ld_sens.wait()

    def halves(block):
        tiles = [block[:, q * 128 : q * 128 + 128] for q in range(8)]
        return [
            jnp.concatenate([tiles[q][:, h * 64 : h * 64 + 64] for q in range(8)], axis=1)
            for h in range(2)
        ]

    for h, part in enumerate(halves(sens_v[...])):
        block = dot(disp[0:ROWS, :], part).astype(bf16)
        l_send[h] = block.reshape(NE, CAP, F // 2)

    def make_meta(e, _):
        rows = disp[pl.ds(pl.multiple_of(e * CAP, 16), 128), :]
        meta_send[e] = dot(id_rows, rows, NT).astype(bf16)
        return _

    lax.fori_loop(0, NE, make_meta, 0)
    def sens_args(h):
        return l_send.at[h], l_recv.at[h], l_ss.at[h], l_rs.at[h]

    for i in others:
        exchange(i, *sens_args(0)).start()
    for i in others:
        exchange(i, meta_send, meta_recv, m_ss, m_rs).start()
    l_recv[0, me] = l_send[0, me]
    l_recv[1, me] = l_send[1, me]
    meta_recv[me] = meta_send[me]

    ld_feat.wait()
    norm_to_windows(feat_v, n_own, range(4))

    def project(src, weight, dst, start):
        block = dot(src[...], weight[...]).astype(bf16)
        dst[:, start : start + 32, :] = block.reshape(8, 32, F)

    ld_k.wait()
    project(n_own, wk, k_all, 0)
    ld_v.wait()
    project(n_own, wv, v_all, 0)
    ld_q.wait()
    q_own[...] = dot(n_own[...], wq[...]).astype(bf16)
    for c in loads[5:]:
        c.start()

    n = iota((2 * T, 1), 0)
    is_halo = n >= T
    m = jnp.where(is_halo, n - T, n)
    band, win, row4, col8 = m >> 7, (m >> 5) & 3, (m >> 3) & 3, m & 7
    col = (win * 8 + col8 + 4) & 31
    grid_row = me * 8 + jnp.where(is_halo, 12 * band - 4, 4 * band) + row4
    valid = (grid_row >= 0) & (grid_row < 128)
    pick = jnp.where(grid_row == iota((2 * T, 128), 1), 1.0, 0.0).astype(bf16)
    by_row = dot(pick, labels[...].astype(f32).astype(bf16), NT)
    lab = jnp.sum(jnp.where(iota((2 * T, 32), 1) == col, by_row, 0.0), axis=1, keepdims=True)
    lab = jnp.where(valid, lab + jnp.where(col < 4, 4.0, 0.0), -1.0)
    oh[...] = jnp.where(lab == iota((2 * T, 128), 1).astype(f32), 1.0, 0.0).astype(bf16)

    for c in halo_copies:
        c.wait_recv()
    norm_to_windows(halo, n_halo, range(4))
    project(n_halo, wk, k_all, 32)
    project(n_halo, wv, v_all, 32)

    diag = (iota((QW, QW), 0) >> 5) == (iota((QW, QW), 1) >> 5)

    def window_row(b, _):
        parts = []
        for w in range(4):
            bw = b * 4 + w
            rows = pl.ds(pl.multiple_of(bw * 32, 32), 32)
            halo_rows = pl.ds(pl.multiple_of(T + bw * 32, 32), 32)
            oq = oh[rows, :]
            ok = jnp.concatenate([oq, oh[halo_rows, :]], axis=0)
            bias = jnp.concatenate([(dot(oq, ok, NT) - 1.0) * 1e30] * 8, axis=0)
            parts += [(bw, rows, slice(g * QW, (g + 1) * QW), bias) for g in range(4)]
        all_scores = []
        for bw, rows, cols, bias in parts:
            qg = jnp.concatenate([q_own[rows, cols]] * 8, axis=0)
            qg = jnp.where(diag, qg, jnp.zeros_like(qg))
            all_scores.append(dot(qg, k_all[bw, :, cols], NT) * SCALE + bias)
        all_weights = []
        for scores in all_scores:
            expo = jnp.exp(scores - jnp.max(scores, axis=1, keepdims=True))
            all_weights.append((expo * (1.0 / jnp.sum(expo, axis=1, keepdims=True))).astype(bf16))
        for (bw, rows, cols, bias), weights in zip(parts, all_weights):
            mixed = dot(weights, v_all[bw, :, cols])
            mixed = jnp.where(diag, mixed, 0.0).reshape(8, 32, QW)
            ctx[rows, cols] = jnp.sum(mixed, axis=0).astype(bf16)
        return _

    lax.fori_loop(0, 2, window_row, 0)

    ld_o.wait()

    o = dot(ctx[...], wo[...])
    for r in range(8):
        base = (r // 4) * 128 + (r % 4) * 8
        parts = [o[base + w * 32 : base + w * 32 + 8] for w in range(4)]
        row = pltpu.roll(jnp.concatenate(parts, axis=0), 4, 0)
        hid[r * 32 : r * 32 + 32, :] = feat_v[r * 32 : r * 32 + 32, :].astype(f32) + row

    def norm_hidden(r, _):
        rows = pl.ds(pl.multiple_of(r * 64, 64), 64)
        moe[rows, :] = layer_norm(hid[rows, :]).astype(bf16)
        return _

    lax.fori_loop(0, 4, norm_hidden, 0)

    for n in range(2):
        cols = slice(n * 512, n * 512 + 512)
        x_send[:, :, cols] = dot(disp[0:ROWS, :], moe[:, cols]).astype(bf16).reshape(NE, CAP, 512)
    feat_args = (x_send, x_recv, x_ss, x_rs)
    for i in others:
        exchange(i, *feat_args).start()
    x_recv[me] = x_send[me]

    disp_t[...] = disp[0:ROWS, :].T
    ld_u.wait()

    def transpose_up(i, _):
        rows = pl.ds(pl.multiple_of(i * 256, 256), 256)
        wk[rows, :] = wu[:, pl.ds(pl.multiple_of(i * 256, 256), 256)].T
        wv[rows, :] = wu[:, pl.ds(pl.multiple_of(F + i * 256, 256), 256)].T
        return _

    lax.fori_loop(0, 4, transpose_up, 0)
    ld_d.wait()

    def split_down(i, _):
        rows = pl.ds(pl.multiple_of(lax.rem(i, 4) * 256, 256), 256)
        for h, part in enumerate(halves(wd[pl.ds(pl.multiple_of(i * 256, 256), 256), :])):
            wu[rows, pl.ds(pl.multiple_of(h * F + lax.div(i, 4) * HB, HB), HB)] = part
        return _

    lax.fori_loop(0, 8, split_down, 0)

    def half_grads(half, hb):
        rows = pl.ds(pl.multiple_of(lax.rem(hb, 2) * HB, HB), HB)
        cols = pl.ds(pl.multiple_of(half * F + lax.div(hb, 2) * HB, HB), HB)
        return dot(wu[rows, cols], l_recv[half].reshape(ROWS, F // 2), NT)

    for i in others:
        arrival(i, *sens_args(0)).wait_recv()

    def first_half(hb, _):
        a2[1, pl.ds(pl.multiple_of(hb * HB, HB), HB), :] = half_grads(0, hb).astype(bf16)
        return _

    lax.fori_loop(0, NB, first_half, 0)

    for i in others:
        arrival(i, meta_send, meta_recv, m_ss, m_rs).wait_recv()

    meta_all = meta_recv[...].reshape(256, 128)
    spread = (iota((128, ROWS), 0) == lax.rem(iota((128, ROWS), 1), CAP)).astype(f32).astype(bf16)
    ids = dot(meta_all, spread)
    own_part = iota((256, ROWS), 0) == lax.div(iota((256, ROWS), 1), CAP) * 16
    other = jnp.sum(jnp.where(own_part, ids, 0.0), axis=0, keepdims=True) - me.astype(f32)

    for i in others:
        exchange(i, *feat_args).wait_send()
    for i in others:
        exchange(i, *sens_args(1)).start()
    for i in others:
        arrival(i, *feat_args).wait_recv()

    logits = dot(router[...], x_recv[...].reshape(ROWS, F), NT)
    sig = 1.0 / (1.0 + jnp.exp(-logits))
    expert = iota((NE, ROWS), 0)
    mine = jnp.sum(jnp.where(expert == me, sig, 0.0), axis=0, keepdims=True)
    theirs = jnp.sum(jnp.where(expert.astype(f32) == other, sig, 0.0), axis=0, keepdims=True)
    gate_v[...] = jnp.broadcast_to(mine / (mine + theirs), (8, ROWS))

    def activate(hb):
        first = pl.multiple_of(lax.rem(hb, 2) * HB, HB)
        u = dot(w3[1 + lax.div(hb, 2), pl.ds(first, HB), :], x_recv[...].reshape(ROWS, F), NT)
        gate = gate_v[0:1, :]
        u2 = u * u
        t = jnp.tanh(GELU_A * u * (1.0 + GELU_B * u2))
        rise = 0.5 * (1.0 + t)
        rows = pl.ds(pl.multiple_of(hb * HB, HB), HB)
        a2[0, rows, :] = (u * rise * gate).astype(bf16)
        slope = rise + 0.5 * u * (1.0 - t * t) * (GELU_A + (3.0 * GELU_A * GELU_B) * u2)
        slope_v[rows, :] = (slope * gate).astype(bf16)

    def first_grads(hb, _):
        rows = pl.ds(pl.multiple_of(hb * HB, HB), HB)
        block = half_grads(1, hb) + a2[1, rows, :].astype(f32)
        a2[1, rows, :] = (block * slope_v[rows, :].astype(f32)).astype(bf16)
        return _

    rv_send = x_send
    result_args = (rv_send, ret, t_ss, t_rs)

    def make_results(half):
        lanes = slice(half * 384, (half + 1) * 384)

        def product(i, _):
            cols = pl.ds(pl.multiple_of(i * 512, 512), 512)
            block = dot(a2[0, :, lanes], wd[:, cols], TN).astype(bf16)
            rv_send[half * 8 : half * 8 + 8, :, cols] = block.reshape(8, CAP, 512)
            return _

        lax.fori_loop(0, 2, product, 0)
        for i in others:

            @pl.when((to_tile[i] >= 8 * half) & (to_tile[i] < 8 * half + 8))
            def _(i=i):
                exchange(i, *result_args).start()

    def chunk(away):
        return lax.rem(xpos + away, 4)

    def core_copy(g, h):
        return rep_copy(stage.at[g, 1 - core, h], crecv.at[g, h], c_ss.at[g, h], c_rs.at[g, h], partner)

    def down_group(half, hb):
        return half * 2 + lax.div(hb, 2), lax.rem(hb, 2)

    def make_down(half, hb):
        g, h = down_group(half, hb)
        rows = pl.ds(pl.multiple_of(hb * HB, HB), HB)
        block = dot(a2[0, rows, :], l_recv[half].reshape(ROWS, F // 2)).astype(bf16)
        for q in range(4):
            top = block[0:256, q * 128 : q * 128 + 128]
            low = block[256:512, q * 128 : q * 128 + 128]
            stage[g, 0, h, q] = jnp.concatenate([top[:, 0:64], low[:, 0:64]], axis=1)
            stage[g, 1, h, q] = jnp.concatenate([top[:, 64:], low[:, 64:]], axis=1)
        core_copy(g, h).start()

    def make_up(hb):
        g = NB + hb
        rows = pl.ds(pl.multiple_of(hb * HB, HB), HB)
        block = dot(a2[1, rows, :], x_recv[...].reshape(ROWS, F)).astype(bf16)
        for h in range(2):
            for q in range(4):
                for c in range(2):
                    start = (2 * q + c) * 128
                    stage[g, c, h, q] = block[h * 256 : h * 256 + 256, start : start + 128]
            core_copy(g, h).start()

    def hop(g, which):
        away, h = [(2, 0), (1, 1), (1, 0), (2, 1), (3, 0), (3, 1)][which]
        dst = [
            r2.at[g, 0], rf.at[g, 0, 1], rf.at[g, 0, 0],
            r2.at[g, 1], rf.at[g, 1, 0], rf.at[g, 1, 1],
        ][which]
        src = stage.at[g, core, h, chunk(away)]
        return rep_copy(src, dst, x2_ss.at[g, which], x2_rs.at[g, which], x_next if which < 3 else x_prev)

    def add_cores(g, h):
        core_copy(g, h).wait_recv()
        total = stage[g, core, h].astype(f32) + crecv[g, h].astype(f32)
        stage[g, core, h] = total.astype(bf16)

    def send_half(g, h):
        for which in ((0, 4), (3, 1))[h]:
            hop(g, which).start()

    def add_down(half, hb):
        g, h = down_group(half, hb)
        add_cores(g, h)

        @pl.when(h == 0)
        def _():
            send_half(g, 0)

        @pl.when(h == 1)
        def _():
            send_half(g, 1)

    def add_up(hb):
        for h in range(2):
            add_cores(NB + hb, h)
            send_half(NB + hb, h)

    def add_last():
        for h, which in ((0, 0), (1, 3)):
            add_cores(GROUPS - 1, h)
            hop(GROUPS - 1, which).start()

    def add_far(g):
        for first, away, h, second in ((0, 1, 0, 2), (3, 3, 1, 5)):
            hop(g, first).wait_recv()
            q = chunk(away)
            total = stage[g, core, h, q].astype(f32) + r2[g, h].astype(f32)
            stage[g, core, h, q] = total.astype(bf16)
            hop(g, second).start()

    def finish(g):
        for which in (1, 2, 4, 5):
            hop(g, which).wait_recv()
        parts = []
        for h in range(2):
            parts.append(
                stage[g, core, h, xpos].astype(f32)
                + rf[g, 0, h].astype(f32)
                + rf[g, 1, h].astype(f32)
            )
        return parts

    def down_copy(hb):
        rows = pl.ds(pl.multiple_of(hb * HB, HB), HB)
        return pltpu.make_async_copy(down_v.at[rows, :], out_down.at[rows, :], down_sem.at[hb])

    def up_copy(hb):
        cols = pl.ds(pl.multiple_of(hb * HB, HB), HB)
        return pltpu.make_async_copy(up_v.at[:, cols], out_up.at[:, cols], up_sem.at[hb])

    def finish_down(pair, _):
        low, high = finish(pair), finish(2 + pair)
        for h in range(2):
            rows = pl.multiple_of((pair * 2 + h) * HB, HB)
            down_v[pl.ds(rows, 256), :] = jnp.concatenate([low[h][:, 0:64], high[h][:, 0:64]], axis=1)
            down_v[pl.ds(rows + 256, 256), :] = jnp.concatenate([low[h][:, 64:], high[h][:, 64:]], axis=1)
            down_copy(pair * 2 + h).start()
        return _

    def finish_up(hb, _):
        for h, total in enumerate(finish(NB + hb)):
            up_v[:, pl.ds(pl.multiple_of(hb * HB + h * 256, 256), 256)] = total.T
        up_copy(hb).start()
        return _

    def down_groups(half, before):
        def body(hb, carry):
            before(hb)
            make_down(half, hb)

            @pl.when(hb >= 1)
            def _():
                add_down(half, hb - 1)

            return carry

        lax.fori_loop(0, NB, body, 0)
        add_down(half, NB - 1)

    down_groups(0, activate)
    add_far(0)
    for i in others:
        arrival(i, *sens_args(1)).wait_recv()
    down_groups(1, lambda hb: None)
    add_far(1)
    make_results(0)
    add_far(2)
    make_results(1)
    ret[me] = rv_send[me]
    add_far(3)
    lax.fori_loop(0, NB, first_grads, 0)

    def up_step(hb, carry):
        make_up(hb)

        @pl.when(hb >= 1)
        def _():
            add_up(hb - 1)

        @pl.when(hb >= 2)
        def _():
            add_far(NB + hb - 2)

        return carry

    lax.fori_loop(0, NB, up_step, 0)
    add_last()
    add_far(GROUPS - 2)
    finish_down(0, 0)
    add_far(GROUPS - 1)
    for which in (1, 4):
        hop(GROUPS - 1, which).start()
    finish_down(1, 0)

    for i in others:
        arrival(i, *result_args).wait_recv()

    def combine(i, _):
        cols = pl.ds(pl.multiple_of(i * 256, 256), 256)
        mixture = dot(disp_t[...], ret[:, :, cols].reshape(ROWS, 256))
        layer_v[:, cols] = (hid[:, cols] + mixture).astype(bf16)
        return _

    lax.fori_loop(0, 4, combine, 0)
    layer_copy = pltpu.make_async_copy(layer_v, out_layer, layer_sem)
    layer_copy.start()
    lax.fori_loop(0, NB, finish_up, 0)

    layer_copy.wait()
    for hb in range(NB):
        down_copy(hb).wait()
        up_copy(hb).wait()
    for c in halo_copies:
        c.wait_send()

    for i in others:
        exchange(i, meta_send, meta_recv, m_ss, m_rs).wait_send()
        exchange(i, *result_args).wait_send()
        exchange(i, *sens_args(0)).wait_send()
        exchange(i, *sens_args(1)).wait_send()

    def drain_groups(g, _):
        for h in range(2):
            core_copy(g, h).wait_send()
        for which in range(6):
            hop(g, which).wait_send()
        return _

    lax.fori_loop(0, GROUPS, drain_groups, 0)


def hand_over(layer, up, down, out_layer, out_up, out_down, layer_v, up_v, down_v, sem_in, sem_out):
    steps = []
    for a, v, b in ((layer, layer_v, out_layer), (up, up_v, out_up), (down, down_v, out_down)):
        rows = a.shape[0] // 4
        for i in range(4):
            part = pl.ds(i * rows, rows)
            n = len(steps)
            steps.append((
                pltpu.make_async_copy(a.at[part, :], v.at[part, :], sem_in.at[n]),
                pltpu.make_async_copy(v.at[part, :], b.at[part, :], sem_out.at[n]),
            ))
    for first, _ in steps:
        first.start()
    for first, second in steps:
        first.wait()
        second.start()
    for _, second in steps:
        second.wait()


def on_device(
    patch_features, labels, assigned_specialists, loss_sensitivity,
    attn_qkv, attn_out, router, expert_up, expert_down,
):
    hbm = pl.BlockSpec(memory_space=pl.ANY)
    vmem = pl.BlockSpec(memory_space=pltpu.VMEM)
    dma = pltpu.SemaphoreType.DMA

    def buf(*shape, dtype=bf16):
        return pltpu.VMEM(shape, dtype)

    scratch = [
        buf(T, F), buf(T, F), buf(3, F, F), buf(F, F), buf(F, FFW), buf(FFW, F),
        buf(T, F), buf(T, F), buf(T, F), buf(T, F), buf(8, 64, F), buf(8, 64, F), buf(T, F),
        buf(2 * T, 128), buf(T, F, dtype=f32), buf(T, F),
        buf(ROWS + 128 - CAP, T), buf(T, ROWS), buf(NE, 16, 128), buf(NE, 16, 128),
        buf(NE, CAP, F), buf(NE, CAP, F), buf(2, NE, CAP, F // 2), buf(2, NE, CAP, F // 2), buf(FFW, ROWS),
        buf(NE, CAP, F), buf(2, FFW, ROWS),
        buf(8, ROWS, dtype=f32),
        buf(GROUPS, 2, 2, 4, 256, 128), buf(GROUPS, 2, 4, 256, 128),
        buf(GROUPS, 2, 256, 128), buf(GROUPS, 2, 2, 256, 128),
        dma((8,)), dma((2,)), dma((2,)),
        dma((2, NE)), dma((2, NE)), dma((NE,)), dma((NE,)), dma((NE,)), dma((NE,)), dma((NE,)), dma((NE,)),
        dma((GROUPS, 2)), dma((GROUPS, 2)), dma((GROUPS, 6)), dma((GROUPS, 6)),
        buf(T, F), buf(F // 8, FFW, dtype=f32), buf(FFW, F // 8, dtype=f32),
        dma, dma((NB,)), dma((NB,)),
    ]
    layer, up, down = pl.pallas_call(
        kernel,
        out_shape=(
            jax.ShapeDtypeStruct((T, F), bf16),
            jax.ShapeDtypeStruct((F // 8, FFW), f32),
            jax.ShapeDtypeStruct((FFW, F // 8), f32),
        ),
        in_specs=[hbm, vmem, vmem, hbm, hbm, hbm, vmem, hbm, hbm],
        out_specs=(hbm, hbm, hbm),
        scratch_shapes=scratch,
        compiler_params=pltpu.CompilerParams(
            collective_id=0, has_side_effects=True, vmem_limit_bytes=62 * 1024 * 1024
        ),
        name="layer",
    )(
        patch_features[0], labels.T, assigned_specialists[0].T, loss_sensitivity[0],
        attn_qkv, attn_out, router.T, expert_up[0], expert_down[0],
    )
    layer, up, down = pl.pallas_call(
        hand_over,
        out_shape=(
            jax.ShapeDtypeStruct((T, F), bf16),
            jax.ShapeDtypeStruct((F // 8, FFW), f32),
            jax.ShapeDtypeStruct((FFW, F // 8), f32),
        ),
        in_specs=[hbm, hbm, hbm],
        out_specs=(hbm, hbm, hbm),
        scratch_shapes=[
            buf(T, F), buf(F // 8, FFW, dtype=f32), buf(FFW, F // 8, dtype=f32), dma((12,)), dma((12,)),
        ],
        name="hand_over",
    )(layer, up, down)
    return layer[None], up[None], down[None]


def solution(mesh):
    return jax.shard_map(
        on_device,
        mesh=mesh,
        in_specs=(
            P("rep", "tile", None), P(), P("rep", "tile", None), P("rep", "tile", None),
            P(), P(), P(), P("tile", None, None), P("tile", None, None),
        ),
        out_specs=(P("rep", "tile", None), P("tile", "rep", None), P("tile", None, "rep")),
        check_vma=False,
    )
```

```python
import functools

import jax
import jax.numpy as jnp
from jax import lax
from jax.experimental import pallas as pl
from jax.experimental.pallas import tpu as pltpu
from jax.sharding import PartitionSpec as P

F = 1024
FFW = 2048
NE = 16
CAP = 48
T = 256
ROWS = NE * CAP
HB = 512
NB = FFW // HB
GROUPS = 2 * NB
OFFSETS = sorted(
    [(a, b) for a in range(4) for b in range(4) if (a, b) != (0, 0)],
    key=lambda o: -(min(o[0], 4 - o[0]) + min(o[1], 4 - o[1])),
)
QW = 256
SCALE = 32 ** (-0.5)
EPSILON = 1e-05
GELU_A = 0.7978845608028654
GELU_B = 0.044715
f32 = jnp.float32
bf16 = jnp.bfloat16
MESH = pl.DeviceIdType.MESH

NN = (((1,), (0,)), ((), ()))
NT = (((1,), (1,)), ((), ()))
TN = (((0,), (0,)), ((), ()))


def dot(a, b, dims=NN):
    return lax.dot_general(a, b, dims, preferred_element_type=f32)


def iota(shape, dim):
    return lax.broadcasted_iota(jnp.int32, shape, dim)


def layer_norm(values):
    center = values - jnp.mean(values, axis=-1, keepdims=True)
    spread = jnp.mean(center * center, axis=-1, keepdims=True)
    return center * lax.rsqrt(spread + EPSILON)


def norm_to_windows(src, dst, pairs):
    for p in pairs:
        y = layer_norm(src[p * 64 : p * 64 + 64, :].astype(f32))
        y0 = pltpu.roll(y[:32], 28, 0)
        y1 = pltpu.roll(y[32:], 28, 0)
        for w in range(4):
            block = jnp.concatenate([y0[8 * w : 8 * w + 8], y1[8 * w : 8 * w + 8]], axis=0)
            start = (p // 2) * 128 + w * 32 + (p % 2) * 16
            dst[start : start + 16, :] = block.astype(bf16)


def kernel(
    feat, labels, assigned, sens, w_qkv, w_out, router, w_up, w_down,
    out_layer, out_up, out_down,
    feat_v, sens_v, w3, wo, wu, wd,
    halo, n_own, n_halo, q_own, k_all, v_all, ctx, oh, hid, moe,
    disp, disp_t, meta_send, meta_recv, x_send, x_recv, l_send, l_recv, slope_v, ret, a2, gate_v,
    stage, crecv, r2, rf,
    load_sem, halo_ss, halo_rs, l_ss, l_rs, m_ss, m_rs, x_ss, x_rs, t_ss, t_rs,
    c_ss, c_rs, x2_ss, x2_rs,
    layer_v, up_v, down_v, layer_sem, up_sem, down_sem,
):
    wq, wk, wv = w3.at[0], w3.at[1], w3.at[2]
    me = lax.axis_index("tile")
    rep = lax.axis_index("rep")
    core = lax.rem(rep, 2)
    xpos = lax.div(rep, 2)
    partner = rep + 1 - 2 * core
    x_next = lax.rem(rep + 2, 8)
    x_prev = lax.rem(rep + 6, 8)

    loads = [
        pltpu.make_async_copy(s, d, load_sem.at[i])
        for i, (s, d) in enumerate(
            [
                (feat, feat_v),
                (sens, sens_v),
                (w_qkv.at[:, F : 2 * F], wk),
                (w_qkv.at[:, 2 * F : 3 * F], wv),
                (w_qkv.at[:, 0:F], wq),
                (w_out, wo),
                (w_down, wd),
                (w_up, wu),
            ]
        )
    ]
    for c in loads[:5]:
        c.start()
    ld_feat, ld_sens, ld_k, ld_v, ld_q, ld_o, ld_d, ld_u = loads

    barrier = pltpu.get_barrier_semaphore()
    y, z = lax.rem(me, 4), lax.div(me, 4)
    to_tile = [lax.rem(z + b, 4) * 4 + lax.rem(y + a, 4) for a, b in OFFSETS]
    from_tile = [lax.rem(z + 4 - b, 4) * 4 + lax.rem(y + 4 - a, 4) for a, b in OFFSETS]
    for t in to_tile:
        pl.semaphore_signal(barrier, inc=1, device_id={"tile": t}, device_id_type=MESH)
    for r in (partner, x_next, x_prev):
        pl.semaphore_signal(barrier, inc=1, device_id={"rep": r}, device_id_type=MESH)
    pl.semaphore_wait(barrier, NE - 1 + 3)

    def tile_copy(src, dst, ss, rs, target):
        return pltpu.make_async_remote_copy(
            src_ref=src, dst_ref=dst, send_sem=ss, recv_sem=rs,
            device_id={"tile": target}, device_id_type=MESH,
        )

    def rep_copy(src, dst, ss, rs, target):
        return pltpu.make_async_remote_copy(
            src_ref=src, dst_ref=dst, send_sem=ss, recv_sem=rs,
            device_id={"rep": target}, device_id_type=MESH,
        )

    t_next = lax.rem(me + 1, NE)
    t_prev = lax.rem(me + NE - 1, NE)
    halo_copies = [
        tile_copy(feat.at[T // 2 : T, :], halo.at[0 : T // 2, :], halo_ss.at[0], halo_rs.at[0], t_next),
        tile_copy(feat.at[0 : T // 2, :], halo.at[T // 2 : T, :], halo_ss.at[1], halo_rs.at[1], t_prev),
    ]
    for c in halo_copies:
        c.start()

    def exchange(i, src, dst, ss, rs):
        t = to_tile[i]
        return tile_copy(src.at[t], dst.at[me], ss.at[i], rs.at[i], t)

    def arrival(i, src, dst, ss, rs):
        t = from_tile[i]
        return tile_copy(src.at[t], dst.at[t], ss.at[i], rs.at[i], t)

    others = range(NE - 1)

    ids_t = assigned[...]
    expert = iota((NE, T), 0)
    member_t = jnp.where((ids_t[0:1] == expert) | (ids_t[1:2] == expert), 1.0, 0.0)
    before = (iota((T, T), 0) < iota((T, T), 1)).astype(f32).astype(bf16)
    rank_t = dot(member_t.astype(bf16), before)
    slot_t = jnp.where(member_t > 0.5, rank_t, -1.0)
    slots = iota((CAP, T), 0).astype(f32)
    for e in range(NE):
        disp[e * CAP : (e + 1) * CAP, :] = jnp.where(slot_t[e : e + 1] == slots, 1.0, 0.0).astype(bf16)
    disp[ROWS:, :] = jnp.zeros((128 - CAP, T), bf16)
    id_sum = jnp.sum(member_t * expert.astype(f32), axis=0, keepdims=True)
    id_rows = jnp.broadcast_to(id_sum, (16, T)).astype(bf16)

    ld_sens.wait()

    def halves(block):
        tiles = [block[:, q * 128 : q * 128 + 128] for q in range(8)]
        return [
            jnp.concatenate([tiles[q][:, h * 64 : h * 64 + 64] for q in range(8)], axis=1)
            for h in range(2)
        ]

    for h, part in enumerate(halves(sens_v[...])):
        block = dot(disp[0:ROWS, :], part).astype(bf16)
        l_send[h] = block.reshape(NE, CAP, F // 2)

    def make_meta(e, _):
        rows = disp[pl.ds(pl.multiple_of(e * CAP, 16), 128), :]
        meta_send[e] = dot(id_rows, rows, NT).astype(bf16)
        return _

    lax.fori_loop(0, NE, make_meta, 0)
    def sens_args(h):
        return l_send.at[h], l_recv.at[h], l_ss.at[h], l_rs.at[h]

    along_z = [i for i in others if OFFSETS[i][0] == 0]
    for i in along_z:
        exchange(i, *sens_args(0)).start()
    l_recv[0, me] = l_send[0, me]
    l_recv[1, me] = l_send[1, me]
    meta_recv[me] = meta_send[me]

    ld_feat.wait()
    norm_to_windows(feat_v, n_own, range(4))

    def project(src, weight, dst, start):
        block = dot(src[...], weight[...]).astype(bf16)
        dst[:, start : start + 32, :] = block.reshape(8, 32, F)

    ld_k.wait()
    project(n_own, wk, k_all, 0)
    ld_v.wait()
    project(n_own, wv, v_all, 0)
    ld_q.wait()
    q_own[...] = dot(n_own[...], wq[...]).astype(bf16)
    for c in loads[5:]:
        c.start()

    n = iota((2 * T, 1), 0)
    is_halo = n >= T
    m = jnp.where(is_halo, n - T, n)
    band, win, row4, col8 = m >> 7, (m >> 5) & 3, (m >> 3) & 3, m & 7
    col = (win * 8 + col8 + 4) & 31
    grid_row = me * 8 + jnp.where(is_halo, 12 * band - 4, 4 * band) + row4
    valid = (grid_row >= 0) & (grid_row < 128)
    pick = jnp.where(grid_row == iota((2 * T, 128), 1), 1.0, 0.0).astype(bf16)
    by_row = dot(pick, labels[...].astype(f32).astype(bf16), NT)
    lab = jnp.sum(jnp.where(iota((2 * T, 32), 1) == col, by_row, 0.0), axis=1, keepdims=True)
    lab = jnp.where(valid, lab + jnp.where(col < 4, 4.0, 0.0), -1.0)
    oh[...] = jnp.where(lab == iota((2 * T, 128), 1).astype(f32), 1.0, 0.0).astype(bf16)

    for c in halo_copies:
        c.wait_recv()
    for i in others:
        if i not in along_z:
            exchange(i, *sens_args(0)).start()
    for i in others:
        exchange(i, meta_send, meta_recv, m_ss, m_rs).start()
    norm_to_windows(halo, n_halo, range(4))
    project(n_halo, wk, k_all, 32)
    project(n_halo, wv, v_all, 32)

    diag = (iota((QW, QW), 0) >> 5) == (iota((QW, QW), 1) >> 5)

    def window_row(b, _):
        parts = []
        for w in range(4):
            bw = b * 4 + w
            rows = pl.ds(pl.multiple_of(bw * 32, 32), 32)
            halo_rows = pl.ds(pl.multiple_of(T + bw * 32, 32), 32)
            oq = oh[rows, :]
            ok = jnp.concatenate([oq, oh[halo_rows, :]], axis=0)
            bias = jnp.concatenate([(dot(oq, ok, NT) - 1.0) * 1e30] * 8, axis=0)
            parts += [(bw, rows, slice(g * QW, (g + 1) * QW), bias) for g in range(4)]
        all_scores = []
        for bw, rows, cols, bias in parts:
            qg = jnp.concatenate([q_own[rows, cols]] * 8, axis=0)
            qg = jnp.where(diag, qg, jnp.zeros_like(qg))
            all_scores.append(dot(qg, k_all[bw, :, cols], NT) * SCALE + bias)
        all_weights = []
        for scores in all_scores:
            expo = jnp.exp(scores - jnp.max(scores, axis=1, keepdims=True))
            all_weights.append((expo * (1.0 / jnp.sum(expo, axis=1, keepdims=True))).astype(bf16))
        for (bw, rows, cols, bias), weights in zip(parts, all_weights):
            mixed = dot(weights, v_all[bw, :, cols])
            mixed = jnp.where(diag, mixed, 0.0).reshape(8, 32, QW)
            ctx[rows, cols] = jnp.sum(mixed, axis=0).astype(bf16)
        return _

    lax.fori_loop(0, 2, window_row, 0)

    ld_o.wait()

    o = dot(ctx[...], wo[...])
    for r in range(8):
        base = (r // 4) * 128 + (r % 4) * 8
        parts = [o[base + w * 32 : base + w * 32 + 8] for w in range(4)]
        row = pltpu.roll(jnp.concatenate(parts, axis=0), 4, 0)
        hid[r * 32 : r * 32 + 32, :] = feat_v[r * 32 : r * 32 + 32, :].astype(f32) + row

    def norm_hidden(r, _):
        rows = pl.ds(pl.multiple_of(r * 64, 64), 64)
        moe[rows, :] = layer_norm(hid[rows, :]).astype(bf16)
        return _

    lax.fori_loop(0, 4, norm_hidden, 0)

    for n in range(2):
        cols = slice(n * 512, n * 512 + 512)
        x_send[:, :, cols] = dot(disp[0:ROWS, :], moe[:, cols]).astype(bf16).reshape(NE, CAP, 512)
    feat_args = (x_send, x_recv, x_ss, x_rs)
    for i in others:
        exchange(i, *feat_args).start()
    x_recv[me] = x_send[me]

    disp_t[...] = disp[0:ROWS, :].T
    ld_u.wait()

    def transpose_up(i, _):
        rows = pl.ds(pl.multiple_of(i * 256, 256), 256)
        wk[rows, :] = wu[:, pl.ds(pl.multiple_of(i * 256, 256), 256)].T
        wv[rows, :] = wu[:, pl.ds(pl.multiple_of(F + i * 256, 256), 256)].T
        return _

    lax.fori_loop(0, 4, transpose_up, 0)
    ld_d.wait()

    def split_down(i, _):
        rows = pl.ds(pl.multiple_of(lax.rem(i, 4) * 256, 256), 256)
        for h, part in enumerate(halves(wd[pl.ds(pl.multiple_of(i * 256, 256), 256), :])):
            wu[rows, pl.ds(pl.multiple_of(h * F + lax.div(i, 4) * HB, HB), HB)] = part
        return _

    lax.fori_loop(0, 8, split_down, 0)

    def half_grads(half, hb):
        rows = pl.ds(pl.multiple_of(lax.rem(hb, 2) * HB, HB), HB)
        cols = pl.ds(pl.multiple_of(half * F + lax.div(hb, 2) * HB, HB), HB)
        return dot(wu[rows, cols], l_recv[half].reshape(ROWS, F // 2), NT)

    for i in others:
        arrival(i, *sens_args(0)).wait_recv()

    def first_half(hb, _):
        a2[1, pl.ds(pl.multiple_of(hb * HB, HB), HB), :] = half_grads(0, hb).astype(bf16)
        return _

    lax.fori_loop(0, NB, first_half, 0)

    for i in others:
        arrival(i, meta_send, meta_recv, m_ss, m_rs).wait_recv()

    meta_all = meta_recv[...].reshape(256, 128)
    spread = (iota((128, ROWS), 0) == lax.rem(iota((128, ROWS), 1), CAP)).astype(f32).astype(bf16)
    ids = dot(meta_all, spread)
    own_part = iota((256, ROWS), 0) == lax.div(iota((256, ROWS), 1), CAP) * 16
    other = jnp.sum(jnp.where(own_part, ids, 0.0), axis=0, keepdims=True) - me.astype(f32)

    for i in others:
        arrival(i, *feat_args).wait_recv()
    for i in others:
        exchange(i, *feat_args).wait_send()
    for i in others:
        exchange(i, *sens_args(1)).start()

    logits = dot(router[...], x_recv[...].reshape(ROWS, F), NT)
    sig = 1.0 / (1.0 + jnp.exp(-logits))
    expert = iota((NE, ROWS), 0)
    mine = jnp.sum(jnp.where(expert == me, sig, 0.0), axis=0, keepdims=True)
    theirs = jnp.sum(jnp.where(expert.astype(f32) == other, sig, 0.0), axis=0, keepdims=True)
    gate_v[...] = jnp.broadcast_to(mine / (mine + theirs), (8, ROWS))

    def activate(hb):
        first = pl.multiple_of(lax.rem(hb, 2) * HB, HB)
        u = dot(w3[1 + lax.div(hb, 2), pl.ds(first, HB), :], x_recv[...].reshape(ROWS, F), NT)
        gate = gate_v[0:1, :]
        u2 = u * u
        t = jnp.tanh(GELU_A * u * (1.0 + GELU_B * u2))
        rise = 0.5 * (1.0 + t)
        rows = pl.ds(pl.multiple_of(hb * HB, HB), HB)
        a2[0, rows, :] = (u * rise * gate).astype(bf16)
        slope = rise + 0.5 * u * (1.0 - t * t) * (GELU_A + (3.0 * GELU_A * GELU_B) * u2)
        slope_v[rows, :] = (slope * gate).astype(bf16)

    def first_grads(hb, _):
        rows = pl.ds(pl.multiple_of(hb * HB, HB), HB)
        block = half_grads(1, hb) + a2[1, rows, :].astype(f32)
        a2[1, rows, :] = (block * slope_v[rows, :].astype(f32)).astype(bf16)
        return _

    rv_send = x_send
    result_args = (rv_send, ret, t_ss, t_rs)

    def make_results(half):
        lanes = slice(half * 384, (half + 1) * 384)

        def product(i, _):
            cols = pl.ds(pl.multiple_of(i * 512, 512), 512)
            block = dot(a2[0, :, lanes], wd[:, cols], TN).astype(bf16)
            rv_send[half * 8 : half * 8 + 8, :, cols] = block.reshape(8, CAP, 512)
            return _

        lax.fori_loop(0, 2, product, 0)
        for i in others:

            @pl.when((to_tile[i] >= 8 * half) & (to_tile[i] < 8 * half + 8))
            def _(i=i):
                exchange(i, *result_args).start()

    def chunk(away):
        return lax.rem(xpos + away, 4)

    def core_copy(g, h):
        return rep_copy(stage.at[g, 1 - core, h], crecv.at[g, h], c_ss.at[g, h], c_rs.at[g, h], partner)

    def down_group(half, hb):
        return half * 2 + lax.div(hb, 2), lax.rem(hb, 2)

    def make_down(half, hb):
        g, h = down_group(half, hb)
        rows = pl.ds(pl.multiple_of(hb * HB, HB), HB)
        block = dot(a2[0, rows, :], l_recv[half].reshape(ROWS, F // 2)).astype(bf16)
        for q in range(4):
            top = block[0:256, q * 128 : q * 128 + 128]
            low = block[256:512, q * 128 : q * 128 + 128]
            stage[g, 0, h, q] = jnp.concatenate([top[:, 0:64], low[:, 0:64]], axis=1)
            stage[g, 1, h, q] = jnp.concatenate([top[:, 64:], low[:, 64:]], axis=1)
        core_copy(g, h).start()

    def make_up(hb):
        g = NB + hb
        rows = pl.ds(pl.multiple_of(hb * HB, HB), HB)
        block = dot(a2[1, rows, :], x_recv[...].reshape(ROWS, F)).astype(bf16)
        for h in range(2):
            for q in range(4):
                for c in range(2):
                    start = (2 * q + c) * 128
                    stage[g, c, h, q] = block[h * 256 : h * 256 + 256, start : start + 128]
            core_copy(g, h).start()

    def hop(g, which):
        away, h = [(2, 0), (1, 1), (1, 0), (2, 1), (3, 0), (3, 1)][which]
        dst = [
            r2.at[g, 0], rf.at[g, 0, 1], rf.at[g, 0, 0],
            r2.at[g, 1], rf.at[g, 1, 0], rf.at[g, 1, 1],
        ][which]
        src = stage.at[g, core, h, chunk(away)]
        return rep_copy(src, dst, x2_ss.at[g, which], x2_rs.at[g, which], x_next if which < 3 else x_prev)

    def add_cores(g, h):
        core_copy(g, h).wait_recv()
        total = stage[g, core, h].astype(f32) + crecv[g, h].astype(f32)
        stage[g, core, h] = total.astype(bf16)

    def send_half(g, h):
        for which in ((0, 4), (3, 1))[h]:
            hop(g, which).start()

    def add_down(half, hb):
        g, h = down_group(half, hb)
        add_cores(g, h)

        @pl.when(h == 0)
        def _():
            send_half(g, 0)

        @pl.when(h == 1)
        def _():
            send_half(g, 1)

    def add_up(hb):
        for h in range(2):
            add_cores(NB + hb, h)
            send_half(NB + hb, h)

    def add_last():
        for h, which in ((0, 0), (1, 3)):
            add_cores(GROUPS - 1, h)
            hop(GROUPS - 1, which).start()

    def add_far(g):
        for first, away, h, second in ((0, 1, 0, 2), (3, 3, 1, 5)):
            hop(g, first).wait_recv()
            q = chunk(away)
            total = stage[g, core, h, q].astype(f32) + r2[g, h].astype(f32)
            stage[g, core, h, q] = total.astype(bf16)
            hop(g, second).start()

    def finish(g):
        for which in (1, 2, 4, 5):
            hop(g, which).wait_recv()
        parts = []
        for h in range(2):
            parts.append(
                stage[g, core, h, xpos].astype(f32)
                + rf[g, 0, h].astype(f32)
                + rf[g, 1, h].astype(f32)
            )
        return parts

    def down_copy(hb):
        rows = pl.ds(pl.multiple_of(hb * HB, HB), HB)
        return pltpu.make_async_copy(down_v.at[rows, :], out_down.at[rows, :], down_sem.at[hb])

    def up_copy(hb):
        cols = pl.ds(pl.multiple_of(hb * HB, HB), HB)
        return pltpu.make_async_copy(up_v.at[:, cols], out_up.at[:, cols], up_sem.at[hb])

    def finish_down(pair, _):
        low, high = finish(pair), finish(2 + pair)
        for h in range(2):
            rows = pl.multiple_of((pair * 2 + h) * HB, HB)
            down_v[pl.ds(rows, 256), :] = jnp.concatenate([low[h][:, 0:64], high[h][:, 0:64]], axis=1)
            down_v[pl.ds(rows + 256, 256), :] = jnp.concatenate([low[h][:, 64:], high[h][:, 64:]], axis=1)
            down_copy(pair * 2 + h).start()
        return _

    def finish_up(hb, _):
        for h, total in enumerate(finish(NB + hb)):
            up_v[:, pl.ds(pl.multiple_of(hb * HB + h * 256, 256), 256)] = total.T
        up_copy(hb).start()
        return _

    def down_groups(half, before):
        def body(hb, carry):
            before(hb)
            make_down(half, hb)

            @pl.when(hb >= 1)
            def _():
                add_down(half, hb - 1)

            return carry

        lax.fori_loop(0, NB, body, 0)
        add_down(half, NB - 1)

    down_groups(0, activate)
    add_far(0)
    for i in others:
        arrival(i, *sens_args(1)).wait_recv()
    down_groups(1, lambda hb: None)
    add_far(1)
    make_results(0)
    make_results(1)
    ret[me] = rv_send[me]
    lax.fori_loop(0, NB, first_grads, 0)

    def up_step(hb, carry):
        make_up(hb)

        @pl.when(hb >= 1)
        def _():
            add_up(hb - 1)

        @pl.when(hb >= 1)
        def _():
            add_far(hb + 1)

        return carry

    lax.fori_loop(0, NB, up_step, 0)
    add_last()
    add_far(GROUPS - 3)
    add_far(GROUPS - 2)
    finish_down(0, 0)
    add_far(GROUPS - 1)
    for which in (1, 4):
        hop(GROUPS - 1, which).start()
    finish_down(1, 0)

    for i in others:
        arrival(i, *result_args).wait_recv()

    def combine(i, _):
        cols = pl.ds(pl.multiple_of(i * 256, 256), 256)
        mixture = dot(disp_t[...], ret[:, :, cols].reshape(ROWS, 256))
        layer_v[:, cols] = (hid[:, cols] + mixture).astype(bf16)
        return _

    lax.fori_loop(0, 4, combine, 0)
    layer_copy = pltpu.make_async_copy(layer_v, out_layer, layer_sem)
    layer_copy.start()
    lax.fori_loop(0, NB, finish_up, 0)

    layer_copy.wait()
    for hb in range(NB):
        down_copy(hb).wait()
        up_copy(hb).wait()
    for c in halo_copies:
        c.wait_send()

    for i in others:
        exchange(i, meta_send, meta_recv, m_ss, m_rs).wait_send()
        exchange(i, *result_args).wait_send()
        exchange(i, *sens_args(0)).wait_send()
        exchange(i, *sens_args(1)).wait_send()

    def drain_groups(g, _):
        for h in range(2):
            core_copy(g, h).wait_send()
        for which in range(6):
            hop(g, which).wait_send()
        return _

    lax.fori_loop(0, GROUPS, drain_groups, 0)


def hand_over(layer, up, down, out_layer, out_up, out_down, layer_v, up_v, down_v, sem_in, sem_out):
    steps = []
    for a, v, b in ((layer, layer_v, out_layer), (up, up_v, out_up), (down, down_v, out_down)):
        rows = a.shape[0] // 4
        for i in range(4):
            part = pl.ds(i * rows, rows)
            n = len(steps)
            steps.append((
                pltpu.make_async_copy(a.at[part, :], v.at[part, :], sem_in.at[n]),
                pltpu.make_async_copy(v.at[part, :], b.at[part, :], sem_out.at[n]),
            ))
    for first, _ in steps:
        first.start()
    for first, second in steps:
        first.wait()
        second.start()
    for _, second in steps:
        second.wait()


def on_device(
    patch_features, labels, assigned_specialists, loss_sensitivity,
    attn_qkv, attn_out, router, expert_up, expert_down,
):
    hbm = pl.BlockSpec(memory_space=pl.ANY)
    vmem = pl.BlockSpec(memory_space=pltpu.VMEM)
    dma = pltpu.SemaphoreType.DMA

    def buf(*shape, dtype=bf16):
        return pltpu.VMEM(shape, dtype)

    scratch = [
        buf(T, F), buf(T, F), buf(3, F, F), buf(F, F), buf(F, FFW), buf(FFW, F),
        buf(T, F), buf(T, F), buf(T, F), buf(T, F), buf(8, 64, F), buf(8, 64, F), buf(T, F),
        buf(2 * T, 128), buf(T, F, dtype=f32), buf(T, F),
        buf(ROWS + 128 - CAP, T), buf(T, ROWS), buf(NE, 16, 128), buf(NE, 16, 128),
        buf(NE, CAP, F), buf(NE, CAP, F), buf(2, NE, CAP, F // 2), buf(2, NE, CAP, F // 2), buf(FFW, ROWS),
        buf(NE, CAP, F), buf(2, FFW, ROWS),
        buf(8, ROWS, dtype=f32),
        buf(GROUPS, 2, 2, 4, 256, 128), buf(GROUPS, 2, 4, 256, 128),
        buf(GROUPS, 2, 256, 128), buf(GROUPS, 2, 2, 256, 128),
        dma((8,)), dma((2,)), dma((2,)),
        dma((2, NE)), dma((2, NE)), dma((NE,)), dma((NE,)), dma((NE,)), dma((NE,)), dma((NE,)), dma((NE,)),
        dma((GROUPS, 2)), dma((GROUPS, 2)), dma((GROUPS, 6)), dma((GROUPS, 6)),
        buf(T, F), buf(F // 8, FFW, dtype=f32), buf(FFW, F // 8, dtype=f32),
        dma, dma((NB,)), dma((NB,)),
    ]
    layer, up, down = pl.pallas_call(
        kernel,
        out_shape=(
            jax.ShapeDtypeStruct((T, F), bf16),
            jax.ShapeDtypeStruct((F // 8, FFW), f32),
            jax.ShapeDtypeStruct((FFW, F // 8), f32),
        ),
        in_specs=[hbm, vmem, vmem, hbm, hbm, hbm, vmem, hbm, hbm],
        out_specs=(hbm, hbm, hbm),
        scratch_shapes=scratch,
        compiler_params=pltpu.CompilerParams(
            collective_id=0, has_side_effects=True, vmem_limit_bytes=62 * 1024 * 1024
        ),
        name="layer",
    )(
        patch_features[0], labels.T, assigned_specialists[0].T, loss_sensitivity[0],
        attn_qkv, attn_out, router.T, expert_up[0], expert_down[0],
    )
    layer, up, down = pl.pallas_call(
        hand_over,
        out_shape=(
            jax.ShapeDtypeStruct((T, F), bf16),
            jax.ShapeDtypeStruct((F // 8, FFW), f32),
            jax.ShapeDtypeStruct((FFW, F // 8), f32),
        ),
        in_specs=[hbm, hbm, hbm],
        out_specs=(hbm, hbm, hbm),
        scratch_shapes=[
            buf(T, F), buf(F // 8, FFW, dtype=f32), buf(FFW, F // 8, dtype=f32), dma((12,)), dma((12,)),
        ],
        name="hand_over",
    )(layer, up, down)
    return layer[None], up[None], down[None]


def solution(mesh):
    return jax.shard_map(
        on_device,
        mesh=mesh,
        in_specs=(
            P("rep", "tile", None), P(), P("rep", "tile", None), P("rep", "tile", None),
            P(), P(), P(), P("tile", None, None), P("tile", None, None),
        ),
        out_specs=(P("rep", "tile", None), P("tile", "rep", None), P("tile", None, "rep")),
        check_vma=False,
    )
```

```python
import functools

import jax
import jax.numpy as jnp
from jax import lax
from jax.experimental import pallas as pl
from jax.experimental.pallas import tpu as pltpu
from jax.sharding import PartitionSpec as P

F = 1024
FFW = 2048
NE = 16
CAP = 48
T = 256
ROWS = NE * CAP
HB = 512
NB = FFW // HB
GROUPS = 2 * NB
OFFSETS = sorted(
    [(a, b) for a in range(4) for b in range(4) if (a, b) != (0, 0)],
    key=lambda o: min(o[0], 4 - o[0]) + min(o[1], 4 - o[1]),
)
QW = 256
SCALE = 32 ** (-0.5)
EPSILON = 1e-05
GELU_A = 0.7978845608028654
GELU_B = 0.044715
f32 = jnp.float32
bf16 = jnp.bfloat16
MESH = pl.DeviceIdType.MESH

NN = (((1,), (0,)), ((), ()))
NT = (((1,), (1,)), ((), ()))
TN = (((0,), (0,)), ((), ()))


def dot(a, b, dims=NN):
    return lax.dot_general(a, b, dims, preferred_element_type=f32)


def iota(shape, dim):
    return lax.broadcasted_iota(jnp.int32, shape, dim)


def layer_norm(values):
    center = values - jnp.mean(values, axis=-1, keepdims=True)
    spread = jnp.mean(center * center, axis=-1, keepdims=True)
    return center * lax.rsqrt(spread + EPSILON)


def norm_to_windows(src, dst, pairs):
    for p in pairs:
        y = layer_norm(src[p * 64 : p * 64 + 64, :].astype(f32))
        y0 = pltpu.roll(y[:32], 28, 0)
        y1 = pltpu.roll(y[32:], 28, 0)
        for w in range(4):
            block = jnp.concatenate([y0[8 * w : 8 * w + 8], y1[8 * w : 8 * w + 8]], axis=0)
            start = (p // 2) * 128 + w * 32 + (p % 2) * 16
            dst[start : start + 16, :] = block.astype(bf16)


def kernel(
    feat, labels, assigned, sens, w_qkv, w_out, router, w_up, w_down,
    out_layer, out_up, out_down,
    feat_v, sens_v, w3, wo, wu, wd,
    halo, n_own, n_halo, q_own, k_all, v_all, ctx, oh, hid, moe,
    disp, disp_t, meta_send, meta_recv, x_send, x_recv, l_send, l_recv, slope_v, ret, a2, gate_v,
    stage, crecv, r2, rf,
    load_sem, halo_ss, halo_rs, l_ss, l_rs, m_ss, m_rs, x_ss, x_rs, t_ss, t_rs,
    c_ss, c_rs, x2_ss, x2_rs,
    layer_v, up_v, down_v, layer_sem, up_sem, down_sem,
):
    wq, wk, wv = w3.at[0], w3.at[1], w3.at[2]
    me = lax.axis_index("tile")
    rep = lax.axis_index("rep")
    core = lax.rem(rep, 2)
    xpos = lax.div(rep, 2)
    partner = rep + 1 - 2 * core
    x_next = lax.rem(rep + 2, 8)
    x_prev = lax.rem(rep + 6, 8)

    loads = [
        pltpu.make_async_copy(s, d, load_sem.at[i])
        for i, (s, d) in enumerate(
            [
                (feat, feat_v),
                (sens, sens_v),
                (w_qkv.at[:, F : 2 * F], wk),
                (w_qkv.at[:, 2 * F : 3 * F], wv),
                (w_qkv.at[:, 0:F], wq),
                (w_out, wo),
                (w_down, wd),
                (w_up, wu),
            ]
        )
    ]
    for c in loads[:5]:
        c.start()
    ld_feat, ld_sens, ld_k, ld_v, ld_q, ld_o, ld_d, ld_u = loads

    barrier = pltpu.get_barrier_semaphore()
    y, z = lax.rem(me, 4), lax.div(me, 4)
    to_tile = [lax.rem(z + b, 4) * 4 + lax.rem(y + a, 4) for a, b in OFFSETS]
    from_tile = [lax.rem(z + 4 - b, 4) * 4 + lax.rem(y + 4 - a, 4) for a, b in OFFSETS]
    for t in to_tile:
        pl.semaphore_signal(barrier, inc=1, device_id={"tile": t}, device_id_type=MESH)
    for r in (partner, x_next, x_prev):
        pl.semaphore_signal(barrier, inc=1, device_id={"rep": r}, device_id_type=MESH)
    pl.semaphore_wait(barrier, NE - 1 + 3)

    def tile_copy(src, dst, ss, rs, target):
        return pltpu.make_async_remote_copy(
            src_ref=src, dst_ref=dst, send_sem=ss, recv_sem=rs,
            device_id={"tile": target}, device_id_type=MESH,
        )

    def rep_copy(src, dst, ss, rs, target):
        return pltpu.make_async_remote_copy(
            src_ref=src, dst_ref=dst, send_sem=ss, recv_sem=rs,
            device_id={"rep": target}, device_id_type=MESH,
        )

    t_next = lax.rem(me + 1, NE)
    t_prev = lax.rem(me + NE - 1, NE)
    halo_copies = [
        tile_copy(feat.at[T // 2 : T, :], halo.at[0 : T // 2, :], halo_ss.at[0], halo_rs.at[0], t_next),
        tile_copy(feat.at[0 : T // 2, :], halo.at[T // 2 : T, :], halo_ss.at[1], halo_rs.at[1], t_prev),
    ]
    for c in halo_copies:
        c.start()

    def exchange(i, src, dst, ss, rs):
        return tile_copy(src.at[to_tile[i]], dst.at[i], ss.at[i], rs.at[i], to_tile[i])

    def arrival(i, src, dst, ss, rs):
        return tile_copy(src.at[from_tile[i]], dst.at[i], ss.at[i], rs.at[i], from_tile[i])

    last = NE - 1
    near, far = range(NE // 2), range(NE // 2, NE - 1)
    others = range(NE - 1)

    ids_t = assigned[...]
    expert = iota((NE, T), 0)
    member_t = jnp.where((ids_t[0:1] == expert) | (ids_t[1:2] == expert), 1.0, 0.0)
    before = (iota((T, T), 0) < iota((T, T), 1)).astype(f32).astype(bf16)
    rank_t = dot(member_t.astype(bf16), before)
    slot_t = jnp.where(member_t > 0.5, rank_t, -1.0)
    slots = iota((CAP, T), 0).astype(f32)
    for e in range(NE):
        disp[e * CAP : (e + 1) * CAP, :] = jnp.where(slot_t[e : e + 1] == slots, 1.0, 0.0).astype(bf16)
    disp[ROWS:, :] = jnp.zeros((128 - CAP, T), bf16)
    id_sum = jnp.sum(member_t * expert.astype(f32), axis=0, keepdims=True)
    id_rows = jnp.broadcast_to(id_sum, (16, T)).astype(bf16)

    ld_sens.wait()

    def halves(block):
        tiles = [block[:, q * 128 : q * 128 + 128] for q in range(8)]
        return [
            jnp.concatenate([tiles[q][:, h * 64 : h * 64 + 64] for q in range(8)], axis=1)
            for h in range(2)
        ]

    for h, part in enumerate(halves(sens_v[...])):
        block = dot(disp[0:ROWS, :], part).astype(bf16)
        l_send[h] = block.reshape(NE, CAP, F // 2)

    def make_meta(e, _):
        rows = disp[pl.ds(pl.multiple_of(e * CAP, 16), 128), :]
        meta_send[e] = dot(id_rows, rows, NT).astype(bf16)
        return _

    lax.fori_loop(0, NE, make_meta, 0)
    def sens_args(h):
        return l_send.at[h], l_recv.at[h], l_ss.at[h], l_rs.at[h]

    along_z = [i for i in others if OFFSETS[i][0] == 0]
    for i in along_z:
        exchange(i, *sens_args(0)).start()
    l_recv[0, last] = l_send[0, me]
    l_recv[1, last] = l_send[1, me]
    meta_recv[last] = meta_send[me]

    ld_feat.wait()
    norm_to_windows(feat_v, n_own, range(4))

    def project(src, weight, dst, start):
        block = dot(src[...], weight[...]).astype(bf16)
        dst[:, start : start + 32, :] = block.reshape(8, 32, F)

    ld_k.wait()
    project(n_own, wk, k_all, 0)
    ld_v.wait()
    project(n_own, wv, v_all, 0)
    ld_q.wait()
    q_own[...] = dot(n_own[...], wq[...]).astype(bf16)
    for c in loads[5:]:
        c.start()

    n = iota((2 * T, 1), 0)
    is_halo = n >= T
    m = jnp.where(is_halo, n - T, n)
    band, win, row4, col8 = m >> 7, (m >> 5) & 3, (m >> 3) & 3, m & 7
    col = (win * 8 + col8 + 4) & 31
    grid_row = me * 8 + jnp.where(is_halo, 12 * band - 4, 4 * band) + row4
    valid = (grid_row >= 0) & (grid_row < 128)
    pick = jnp.where(grid_row == iota((2 * T, 128), 1), 1.0, 0.0).astype(bf16)
    by_row = dot(pick, labels[...].astype(f32).astype(bf16), NT)
    lab = jnp.sum(jnp.where(iota((2 * T, 32), 1) == col, by_row, 0.0), axis=1, keepdims=True)
    lab = jnp.where(valid, lab + jnp.where(col < 4, 4.0, 0.0), -1.0)
    oh[...] = jnp.where(lab == iota((2 * T, 128), 1).astype(f32), 1.0, 0.0).astype(bf16)

    for c in halo_copies:
        c.wait_recv()
    for i in others:
        if i not in along_z:
            exchange(i, *sens_args(0)).start()
    for i in others:
        exchange(i, meta_send, meta_recv, m_ss, m_rs).start()
    norm_to_windows(halo, n_halo, range(4))
    project(n_halo, wk, k_all, 32)
    project(n_halo, wv, v_all, 32)

    diag = (iota((QW, QW), 0) >> 5) == (iota((QW, QW), 1) >> 5)

    def window_row(b, _):
        parts = []
        for w in range(4):
            bw = b * 4 + w
            rows = pl.ds(pl.multiple_of(bw * 32, 32), 32)
            halo_rows = pl.ds(pl.multiple_of(T + bw * 32, 32), 32)
            oq = oh[rows, :]
            ok = jnp.concatenate([oq, oh[halo_rows, :]], axis=0)
            bias = jnp.concatenate([(dot(oq, ok, NT) - 1.0) * 1e30] * 8, axis=0)
            parts += [(bw, rows, slice(g * QW, (g + 1) * QW), bias) for g in range(4)]
        all_scores = []
        for bw, rows, cols, bias in parts:
            qg = jnp.concatenate([q_own[rows, cols]] * 8, axis=0)
            qg = jnp.where(diag, qg, jnp.zeros_like(qg))
            all_scores.append(dot(qg, k_all[bw, :, cols], NT) * SCALE + bias)
        all_weights = []
        for scores in all_scores:
            expo = jnp.exp(scores - jnp.max(scores, axis=1, keepdims=True))
            all_weights.append((expo * (1.0 / jnp.sum(expo, axis=1, keepdims=True))).astype(bf16))
        for (bw, rows, cols, bias), weights in zip(parts, all_weights):
            mixed = dot(weights, v_all[bw, :, cols])
            mixed = jnp.where(diag, mixed, 0.0).reshape(8, 32, QW)
            ctx[rows, cols] = jnp.sum(mixed, axis=0).astype(bf16)
        return _

    lax.fori_loop(0, 2, window_row, 0)

    ld_o.wait()

    o = dot(ctx[...], wo[...])
    for r in range(8):
        base = (r // 4) * 128 + (r % 4) * 8
        parts = [o[base + w * 32 : base + w * 32 + 8] for w in range(4)]
        row = pltpu.roll(jnp.concatenate(parts, axis=0), 4, 0)
        hid[r * 32 : r * 32 + 32, :] = feat_v[r * 32 : r * 32 + 32, :].astype(f32) + row

    def norm_hidden(r, _):
        rows = pl.ds(pl.multiple_of(r * 64, 64), 64)
        moe[rows, :] = layer_norm(hid[rows, :]).astype(bf16)
        return _

    lax.fori_loop(0, 4, norm_hidden, 0)

    for n in range(2):
        cols = slice(n * 512, n * 512 + 512)
        x_send[:, :, cols] = dot(disp[0:ROWS, :], moe[:, cols]).astype(bf16).reshape(NE, CAP, 512)
    feat_args = (x_send, x_recv, x_ss, x_rs)
    for i in near:
        exchange(i, *feat_args).start()
    x_recv[last] = x_send[me]

    disp_t[...] = disp[0:ROWS, :].T
    ld_u.wait()

    def transpose_up(i, _):
        rows = pl.ds(pl.multiple_of(i * 256, 256), 256)
        wk[rows, :] = wu[:, pl.ds(pl.multiple_of(i * 256, 256), 256)].T
        wv[rows, :] = wu[:, pl.ds(pl.multiple_of(F + i * 256, 256), 256)].T
        return _

    lax.fori_loop(0, 4, transpose_up, 0)
    ld_d.wait()

    def split_down(i, _):
        rows = pl.ds(pl.multiple_of(lax.rem(i, 4) * 256, 256), 256)
        for h, part in enumerate(halves(wd[pl.ds(pl.multiple_of(i * 256, 256), 256), :])):
            wu[rows, pl.ds(pl.multiple_of(h * F + lax.div(i, 4) * HB, HB), HB)] = part
        return _

    lax.fori_loop(0, 8, split_down, 0)

    def half_grads(half, hb):
        rows = pl.ds(pl.multiple_of(lax.rem(hb, 2) * HB, HB), HB)
        cols = pl.ds(pl.multiple_of(half * F + lax.div(hb, 2) * HB, HB), HB)
        return dot(wu[rows, cols], l_recv[half].reshape(ROWS, F // 2), NT)

    for i in others:
        arrival(i, *sens_args(0)).wait_recv()

    def first_half(hb, _):
        a2[1, pl.ds(pl.multiple_of(hb * HB, HB), HB), :] = half_grads(0, hb).astype(bf16)
        return _

    lax.fori_loop(0, NB, first_half, 0)

    for i in others:
        arrival(i, meta_send, meta_recv, m_ss, m_rs).wait_recv()

    meta_all = meta_recv[...].reshape(256, 128)
    spread = (iota((128, ROWS), 0) == lax.rem(iota((128, ROWS), 1), CAP)).astype(f32).astype(bf16)
    ids = dot(meta_all, spread)
    own_part = iota((256, ROWS), 0) == lax.div(iota((256, ROWS), 1), CAP) * 16
    other = jnp.sum(jnp.where(own_part, ids, 0.0), axis=0, keepdims=True) - me.astype(f32)

    for i in near:
        exchange(i, *feat_args).wait_send()
    for i in far:
        exchange(i, *feat_args).start()

    def lanes_of(half):
        return slice(half * 384, half * 384 + 384)

    def half_rows(half):
        return x_recv[half * 8 : half * 8 + 8].reshape(ROWS // 2, F)

    def make_gates(half):
        lanes = lanes_of(half)
        logits = dot(router[...], half_rows(half), NT)
        sig = 1.0 / (1.0 + jnp.exp(-logits))
        expert = iota((NE, ROWS // 2), 0)
        mine = jnp.sum(jnp.where(expert == me, sig, 0.0), axis=0, keepdims=True)
        theirs = jnp.where(expert.astype(f32) == other[:, lanes], sig, 0.0)
        theirs = jnp.sum(theirs, axis=0, keepdims=True)
        gate_v[:, lanes] = jnp.broadcast_to(mine / (mine + theirs), (8, ROWS // 2))

    def activate(hb, half):
        lanes = lanes_of(half)
        first = pl.multiple_of(lax.rem(hb, 2) * HB, HB)
        u = dot(w3[1 + lax.div(hb, 2), pl.ds(first, HB), :], half_rows(half), NT)
        gate = gate_v[0:1, lanes]
        u2 = u * u
        t = jnp.tanh(GELU_A * u * (1.0 + GELU_B * u2))
        rise = 0.5 * (1.0 + t)
        rows = pl.ds(pl.multiple_of(hb * HB, HB), HB)
        a2[0, rows, lanes] = (u * rise * gate).astype(bf16)
        slope = rise + 0.5 * u * (1.0 - t * t) * (GELU_A + (3.0 * GELU_A * GELU_B) * u2)
        slope_v[rows, lanes] = (slope * gate).astype(bf16)

    def first_grads(hb, _):
        rows = pl.ds(pl.multiple_of(hb * HB, HB), HB)
        block = half_grads(1, hb) + a2[1, rows, :].astype(f32)
        a2[1, rows, :] = (block * slope_v[rows, :].astype(f32)).astype(bf16)
        return _

    def send_result(i):
        block = w3.at[0, i * CAP : i * CAP + CAP, :]
        return tile_copy(block, ret.at[me], t_ss.at[i], t_rs.at[i], from_tile[i])

    def result_arrival(i):
        block = w3.at[0, i * CAP : i * CAP + CAP, :]
        return tile_copy(block, ret.at[to_tile[i]], t_ss.at[i], t_rs.at[i], from_tile[i])

    def make_results(half):
        def product(i, _):
            cols = pl.ds(pl.multiple_of(i * 512, 512), 512)
            block = dot(a2[0, :, lanes_of(half)], wd[:, cols], TN).astype(bf16)
            w3[0, half * 384 : half * 384 + 384, cols] = block
            return _

        lax.fori_loop(0, 2, product, 0)

    for i in near:
        arrival(i, *feat_args).wait_recv()
    make_gates(0)

    def near_step(hb, carry):
        activate(hb, 0)
        return carry

    lax.fori_loop(0, NB, near_step, 0)
    make_results(0)
    for i in far:
        arrival(i, *feat_args).wait_recv()
    for i in others:
        exchange(i, *sens_args(1)).start()
    make_gates(1)

    def chunk(away):
        return lax.rem(xpos + away, 4)

    def core_copy(g, h):
        return rep_copy(stage.at[g, 1 - core, h], crecv.at[g, h], c_ss.at[g, h], c_rs.at[g, h], partner)

    def down_group(half, hb):
        return half * 2 + lax.div(hb, 2), lax.rem(hb, 2)

    def make_down(half, hb):
        g, h = down_group(half, hb)
        rows = pl.ds(pl.multiple_of(hb * HB, HB), HB)
        block = dot(a2[0, rows, :], l_recv[half].reshape(ROWS, F // 2)).astype(bf16)
        for q in range(4):
            top = block[0:256, q * 128 : q * 128 + 128]
            low = block[256:512, q * 128 : q * 128 + 128]
            stage[g, 0, h, q] = jnp.concatenate([top[:, 0:64], low[:, 0:64]], axis=1)
            stage[g, 1, h, q] = jnp.concatenate([top[:, 64:], low[:, 64:]], axis=1)
        core_copy(g, h).start()

    def make_up(hb):
        g = NB + hb
        rows = pl.ds(pl.multiple_of(hb * HB, HB), HB)
        block = dot(a2[1, rows, :], x_recv[...].reshape(ROWS, F)).astype(bf16)
        for h in range(2):
            for q in range(4):
                for c in range(2):
                    start = (2 * q + c) * 128
                    stage[g, c, h, q] = block[h * 256 : h * 256 + 256, start : start + 128]
            core_copy(g, h).start()

    def hop(g, which):
        away, h = [(2, 0), (1, 1), (1, 0), (2, 1), (3, 0), (3, 1)][which]
        dst = [
            r2.at[g, 0], rf.at[g, 0, 1], rf.at[g, 0, 0],
            r2.at[g, 1], rf.at[g, 1, 0], rf.at[g, 1, 1],
        ][which]
        src = stage.at[g, core, h, chunk(away)]
        return rep_copy(src, dst, x2_ss.at[g, which], x2_rs.at[g, which], x_next if which < 3 else x_prev)

    def add_cores(g, h):
        core_copy(g, h).wait_recv()
        total = stage[g, core, h].astype(f32) + crecv[g, h].astype(f32)
        stage[g, core, h] = total.astype(bf16)

    def send_half(g, h):
        for which in ((0, 4), (3, 1))[h]:
            hop(g, which).start()

    def add_down(half, hb):
        g, h = down_group(half, hb)
        add_cores(g, h)

        @pl.when(h == 0)
        def _():
            send_half(g, 0)

        @pl.when(h == 1)
        def _():
            send_half(g, 1)

    def add_up(hb):
        for h in range(2):
            add_cores(NB + hb, h)
            send_half(NB + hb, h)

    def add_last():
        for h, which in ((0, 0), (1, 3)):
            add_cores(GROUPS - 1, h)
            hop(GROUPS - 1, which).start()

    def add_far(g):
        for first, away, h, second in ((0, 1, 0, 2), (3, 3, 1, 5)):
            hop(g, first).wait_recv()
            q = chunk(away)
            total = stage[g, core, h, q].astype(f32) + r2[g, h].astype(f32)
            stage[g, core, h, q] = total.astype(bf16)
            hop(g, second).start()

    def finish(g):
        for which in (1, 2, 4, 5):
            hop(g, which).wait_recv()
        parts = []
        for h in range(2):
            parts.append(
                stage[g, core, h, xpos].astype(f32)
                + rf[g, 0, h].astype(f32)
                + rf[g, 1, h].astype(f32)
            )
        return parts

    def down_copy(hb):
        rows = pl.ds(pl.multiple_of(hb * HB, HB), HB)
        return pltpu.make_async_copy(down_v.at[rows, :], out_down.at[rows, :], down_sem.at[hb])

    def up_copy(hb):
        cols = pl.ds(pl.multiple_of(hb * HB, HB), HB)
        return pltpu.make_async_copy(up_v.at[:, cols], out_up.at[:, cols], up_sem.at[hb])

    def finish_down(pair, _):
        low, high = finish(pair), finish(2 + pair)
        for h in range(2):
            rows = pl.multiple_of((pair * 2 + h) * HB, HB)
            down_v[pl.ds(rows, 256), :] = jnp.concatenate([low[h][:, 0:64], high[h][:, 0:64]], axis=1)
            down_v[pl.ds(rows + 256, 256), :] = jnp.concatenate([low[h][:, 64:], high[h][:, 64:]], axis=1)
            down_copy(pair * 2 + h).start()
        return _

    def finish_up(hb, _):
        for h, total in enumerate(finish(NB + hb)):
            up_v[:, pl.ds(pl.multiple_of(hb * HB + h * 256, 256), 256)] = total.T
        up_copy(hb).start()
        return _

    def first_half_step(hb, carry):
        activate(hb, 1)

        @pl.when(hb >= 1)
        def _():
            add_down(0, hb - 1)

        make_down(0, hb)
        return carry

    lax.fori_loop(0, NB, first_half_step, 0)
    add_far(0)
    add_down(0, NB - 1)
    for i in others:
        arrival(i, *sens_args(1)).wait_recv()
    for i in near:
        send_result(i).start()

    def second_half_step(hb, carry):
        make_down(1, hb)

        @pl.when(hb >= 1)
        def _():
            add_down(1, hb - 1)

        return carry

    lax.fori_loop(0, NB, second_half_step, 0)
    add_down(1, NB - 1)
    add_far(1)
    make_results(1)
    for i in far:
        send_result(i).start()
    ret[me] = w3[0, last * CAP : ROWS, :]
    lax.fori_loop(0, NB, first_grads, 0)

    def up_step(hb, carry):
        make_up(hb)

        @pl.when(hb >= 1)
        def _():
            add_up(hb - 1)

        @pl.when(hb >= 1)
        def _():
            add_far(hb + 1)

        return carry

    lax.fori_loop(0, NB, up_step, 0)
    add_last()
    add_far(GROUPS - 3)
    add_far(GROUPS - 2)
    finish_down(0, 0)
    add_far(GROUPS - 1)
    for which in (1, 4):
        hop(GROUPS - 1, which).start()
    finish_down(1, 0)

    for i in others:
        result_arrival(i).wait_recv()

    def combine(i, _):
        cols = pl.ds(pl.multiple_of(i * 256, 256), 256)
        mixture = dot(disp_t[...], ret[:, :, cols].reshape(ROWS, 256))
        layer_v[:, cols] = (hid[:, cols] + mixture).astype(bf16)
        return _

    lax.fori_loop(0, 4, combine, 0)
    layer_copy = pltpu.make_async_copy(layer_v, out_layer, layer_sem)
    layer_copy.start()
    lax.fori_loop(0, NB, finish_up, 0)

    layer_copy.wait()
    for hb in range(NB):
        down_copy(hb).wait()
        up_copy(hb).wait()
    for c in halo_copies:
        c.wait_send()

    for i in others:
        exchange(i, meta_send, meta_recv, m_ss, m_rs).wait_send()
        if i in far:
            exchange(i, *feat_args).wait_send()
        send_result(i).wait_send()
        exchange(i, *sens_args(0)).wait_send()
        exchange(i, *sens_args(1)).wait_send()

    def drain_groups(g, _):
        for h in range(2):
            core_copy(g, h).wait_send()
        for which in range(6):
            hop(g, which).wait_send()
        return _

    lax.fori_loop(0, GROUPS, drain_groups, 0)


def hand_over(layer, up, down, out_layer, out_up, out_down, layer_v, up_v, down_v, sem_in, sem_out):
    steps = []
    for a, v, b in ((layer, layer_v, out_layer), (up, up_v, out_up), (down, down_v, out_down)):
        rows = a.shape[0] // 4
        for i in range(4):
            part = pl.ds(i * rows, rows)
            n = len(steps)
            steps.append((
                pltpu.make_async_copy(a.at[part, :], v.at[part, :], sem_in.at[n]),
                pltpu.make_async_copy(v.at[part, :], b.at[part, :], sem_out.at[n]),
            ))
    for first, _ in steps:
        first.start()
    for first, second in steps:
        first.wait()
        second.start()
    for _, second in steps:
        second.wait()


def on_device(
    patch_features, labels, assigned_specialists, loss_sensitivity,
    attn_qkv, attn_out, router, expert_up, expert_down,
):
    hbm = pl.BlockSpec(memory_space=pl.ANY)
    vmem = pl.BlockSpec(memory_space=pltpu.VMEM)
    dma = pltpu.SemaphoreType.DMA

    def buf(*shape, dtype=bf16):
        return pltpu.VMEM(shape, dtype)

    scratch = [
        buf(T, F), buf(T, F), buf(3, F, F), buf(F, F), buf(F, FFW), buf(FFW, F),
        buf(T, F), buf(T, F), buf(T, F), buf(T, F), buf(8, 64, F), buf(8, 64, F), buf(T, F),
        buf(2 * T, 128), buf(T, F, dtype=f32), buf(T, F),
        buf(ROWS + 128 - CAP, T), buf(T, ROWS), buf(NE, 16, 128), buf(NE, 16, 128),
        buf(NE, CAP, F), buf(NE, CAP, F), buf(2, NE, CAP, F // 2), buf(2, NE, CAP, F // 2), buf(FFW, ROWS),
        buf(NE, CAP, F), buf(2, FFW, ROWS),
        buf(8, ROWS, dtype=f32),
        buf(GROUPS, 2, 2, 4, 256, 128), buf(GROUPS, 2, 4, 256, 128),
        buf(GROUPS, 2, 256, 128), buf(GROUPS, 2, 2, 256, 128),
        dma((8,)), dma((2,)), dma((2,)),
        dma((2, NE)), dma((2, NE)), dma((NE,)), dma((NE,)), dma((NE,)), dma((NE,)), dma((NE,)), dma((NE,)),
        dma((GROUPS, 2)), dma((GROUPS, 2)), dma((GROUPS, 6)), dma((GROUPS, 6)),
        buf(T, F), buf(F // 8, FFW, dtype=f32), buf(FFW, F // 8, dtype=f32),
        dma, dma((NB,)), dma((NB,)),
    ]
    layer, up, down = pl.pallas_call(
        kernel,
        out_shape=(
            jax.ShapeDtypeStruct((T, F), bf16),
            jax.ShapeDtypeStruct((F // 8, FFW), f32),
            jax.ShapeDtypeStruct((FFW, F // 8), f32),
        ),
        in_specs=[hbm, vmem, vmem, hbm, hbm, hbm, vmem, hbm, hbm],
        out_specs=(hbm, hbm, hbm),
        scratch_shapes=scratch,
        compiler_params=pltpu.CompilerParams(
            collective_id=0, has_side_effects=True, vmem_limit_bytes=62 * 1024 * 1024
        ),
        name="layer",
    )(
        patch_features[0], labels.T, assigned_specialists[0].T, loss_sensitivity[0],
        attn_qkv, attn_out, router.T, expert_up[0], expert_down[0],
    )
    layer, up, down = pl.pallas_call(
        hand_over,
        out_shape=(
            jax.ShapeDtypeStruct((T, F), bf16),
            jax.ShapeDtypeStruct((F // 8, FFW), f32),
            jax.ShapeDtypeStruct((FFW, F // 8), f32),
        ),
        in_specs=[hbm, hbm, hbm],
        out_specs=(hbm, hbm, hbm),
        scratch_shapes=[
            buf(T, F), buf(F // 8, FFW, dtype=f32), buf(FFW, F // 8, dtype=f32), dma((12,)), dma((12,)),
        ],
        name="hand_over",
    )(layer, up, down)
    return layer[None], up[None], down[None]


def solution(mesh):
    return jax.shard_map(
        on_device,
        mesh=mesh,
        in_specs=(
            P("rep", "tile", None), P(), P("rep", "tile", None), P("rep", "tile", None),
            P(), P(), P(), P("tile", None, None), P("tile", None, None),
        ),
        out_specs=(P("rep", "tile", None), P("tile", "rep", None), P("tile", None, "rep")),
        check_vma=False,
    )
```

```python
import functools

import jax
import jax.numpy as jnp
from jax import lax
from jax.experimental import pallas as pl
from jax.experimental.pallas import tpu as pltpu
from jax.sharding import PartitionSpec as P

F = 1024
FFW = 2048
NE = 16
CAP = 48
T = 256
ROWS = NE * CAP
HB = 512
NB = FFW // HB
GROUPS = 2 * NB
OFFSETS = sorted(
    [(a, b) for a in range(4) for b in range(4) if (a, b) != (0, 0)],
    key=lambda o: -(min(o[0], 4 - o[0]) + min(o[1], 4 - o[1])),
)
QW = 256
SCALE = 32 ** (-0.5)
EPSILON = 1e-05
GELU_A = 0.7978845608028654
GELU_B = 0.044715
f32 = jnp.float32
bf16 = jnp.bfloat16
MESH = pl.DeviceIdType.MESH

NN = (((1,), (0,)), ((), ()))
NT = (((1,), (1,)), ((), ()))
TN = (((0,), (0,)), ((), ()))


def dot(a, b, dims=NN):
    return lax.dot_general(a, b, dims, preferred_element_type=f32)


def iota(shape, dim):
    return lax.broadcasted_iota(jnp.int32, shape, dim)


def layer_norm(values):
    center = values - jnp.mean(values, axis=-1, keepdims=True)
    spread = jnp.mean(center * center, axis=-1, keepdims=True)
    return center * lax.rsqrt(spread + EPSILON)


def norm_to_windows(src, dst, pairs):
    for p in pairs:
        y = layer_norm(src[p * 64 : p * 64 + 64, :].astype(f32))
        y0 = pltpu.roll(y[:32], 28, 0)
        y1 = pltpu.roll(y[32:], 28, 0)
        for w in range(4):
            block = jnp.concatenate([y0[8 * w : 8 * w + 8], y1[8 * w : 8 * w + 8]], axis=0)
            start = (p // 2) * 128 + w * 32 + (p % 2) * 16
            dst[start : start + 16, :] = block.astype(bf16)


def kernel(
    feat, labels, assigned, sens, w_qkv, w_out, router, w_up, w_down,
    out_layer, out_up, out_down,
    feat_v, sens_v, w3, wo, wu, wd,
    halo, n_own, n_halo, q_own, k_all, v_all, ctx, oh, hid, moe,
    disp, disp_t, meta_send, meta_recv, x_send, x_recv, l_send, l_recv, slope_v, ret, a2, gate_v,
    stage, crecv, r2, rf,
    load_sem, halo_ss, halo_rs, l_ss, l_rs, m_ss, m_rs, x_ss, x_rs, t_ss, t_rs,
    c_ss, c_rs, x2_ss, x2_rs,
    layer_v, up_v, down_v, layer_sem, up_sem, down_sem,
):
    wq, wk, wv = w3.at[0], w3.at[1], w3.at[2]
    me = lax.axis_index("tile")
    rep = lax.axis_index("rep")
    core = lax.rem(rep, 2)
    xpos = lax.div(rep, 2)
    partner = rep + 1 - 2 * core
    x_next = lax.rem(rep + 2, 8)
    x_prev = lax.rem(rep + 6, 8)

    loads = [
        pltpu.make_async_copy(s, d, load_sem.at[i])
        for i, (s, d) in enumerate(
            [
                (feat, feat_v),
                (sens, sens_v),
                (w_qkv.at[:, F : 2 * F], wk),
                (w_qkv.at[:, 2 * F : 3 * F], wv),
                (w_qkv.at[:, 0:F], wq),
                (w_out, wo),
                (w_down, wd),
                (w_up, wu),
            ]
        )
    ]
    for c in loads[:5]:
        c.start()
    ld_feat, ld_sens, ld_k, ld_v, ld_q, ld_o, ld_d, ld_u = loads

    barrier = pltpu.get_barrier_semaphore()
    y, z = lax.rem(me, 4), lax.div(me, 4)
    to_tile = [lax.rem(z + b, 4) * 4 + lax.rem(y + a, 4) for a, b in OFFSETS]
    from_tile = [lax.rem(z + 4 - b, 4) * 4 + lax.rem(y + 4 - a, 4) for a, b in OFFSETS]
    for t in to_tile:
        pl.semaphore_signal(barrier, inc=1, device_id={"tile": t}, device_id_type=MESH)
    for r in (partner, x_next, x_prev):
        pl.semaphore_signal(barrier, inc=1, device_id={"rep": r}, device_id_type=MESH)
    pl.semaphore_wait(barrier, NE - 1 + 3)

    def tile_copy(src, dst, ss, rs, target):
        return pltpu.make_async_remote_copy(
            src_ref=src, dst_ref=dst, send_sem=ss, recv_sem=rs,
            device_id={"tile": target}, device_id_type=MESH,
        )

    def rep_copy(src, dst, ss, rs, target):
        return pltpu.make_async_remote_copy(
            src_ref=src, dst_ref=dst, send_sem=ss, recv_sem=rs,
            device_id={"rep": target}, device_id_type=MESH,
        )

    t_next = lax.rem(me + 1, NE)
    t_prev = lax.rem(me + NE - 1, NE)
    halo_copies = [
        tile_copy(feat.at[T // 2 : T, :], halo.at[0 : T // 2, :], halo_ss.at[0], halo_rs.at[0], t_next),
        tile_copy(feat.at[0 : T // 2, :], halo.at[T // 2 : T, :], halo_ss.at[1], halo_rs.at[1], t_prev),
    ]
    for c in halo_copies:
        c.start()

    def exchange(i, src, dst, ss, rs):
        t = to_tile[i]
        return tile_copy(src.at[t], dst.at[me], ss.at[i], rs.at[i], t)

    def arrival(i, src, dst, ss, rs):
        t = from_tile[i]
        return tile_copy(src.at[t], dst.at[t], ss.at[i], rs.at[i], t)

    others = range(NE - 1)

    ids_t = assigned[...]
    expert = iota((NE, T), 0)
    member_t = jnp.where((ids_t[0:1] == expert) | (ids_t[1:2] == expert), 1.0, 0.0)
    before = (iota((T, T), 0) < iota((T, T), 1)).astype(f32).astype(bf16)
    rank_t = dot(member_t.astype(bf16), before)
    slot_t = jnp.where(member_t > 0.5, rank_t, -1.0)
    slots = iota((CAP, T), 0).astype(f32)
    for e in range(NE):
        disp[e * CAP : (e + 1) * CAP, :] = jnp.where(slot_t[e : e + 1] == slots, 1.0, 0.0).astype(bf16)
    disp[ROWS:, :] = jnp.zeros((128 - CAP, T), bf16)
    id_sum = jnp.sum(member_t * expert.astype(f32), axis=0, keepdims=True)
    id_rows = jnp.broadcast_to(id_sum, (16, T)).astype(bf16)

    ld_sens.wait()

    def halves(block):
        tiles = [block[:, q * 128 : q * 128 + 128] for q in range(8)]
        return [
            jnp.concatenate([tiles[q][:, h * 64 : h * 64 + 64] for q in range(8)], axis=1)
            for h in range(2)
        ]

    for h, part in enumerate(halves(sens_v[...])):
        block = dot(disp[0:ROWS, :], part).astype(bf16)
        l_send[h] = block.reshape(NE, CAP, F // 2)

    def make_meta(e, _):
        rows = disp[pl.ds(pl.multiple_of(e * CAP, 16), 128), :]
        meta_send[e] = dot(id_rows, rows, NT).astype(bf16)
        return _

    lax.fori_loop(0, NE, make_meta, 0)
    def sens_args(h):
        return l_send.at[h], l_recv.at[h], l_ss.at[h], l_rs.at[h]

    for i in others:
        exchange(i, *sens_args(0)).start()
    for i in others:
        exchange(i, meta_send, meta_recv, m_ss, m_rs).start()
    l_recv[0, me] = l_send[0, me]
    l_recv[1, me] = l_send[1, me]
    meta_recv[me] = meta_send[me]

    ld_feat.wait()
    norm_to_windows(feat_v, n_own, range(4))

    def project(src, weight, dst, start):
        block = dot(src[...], weight[...]).astype(bf16)
        dst[:, start : start + 32, :] = block.reshape(8, 32, F)

    ld_k.wait()
    project(n_own, wk, k_all, 0)
    ld_v.wait()
    project(n_own, wv, v_all, 0)
    ld_q.wait()
    q_own[...] = dot(n_own[...], wq[...]).astype(bf16)
    for c in loads[5:]:
        c.start()

    n = iota((2 * T, 1), 0)
    is_halo = n >= T
    m = jnp.where(is_halo, n - T, n)
    band, win, row4, col8 = m >> 7, (m >> 5) & 3, (m >> 3) & 3, m & 7
    col = (win * 8 + col8 + 4) & 31
    grid_row = me * 8 + jnp.where(is_halo, 12 * band - 4, 4 * band) + row4
    valid = (grid_row >= 0) & (grid_row < 128)
    pick = jnp.where(grid_row == iota((2 * T, 128), 1), 1.0, 0.0).astype(bf16)
    by_row = dot(pick, labels[...].astype(f32).astype(bf16), NT)
    lab = jnp.sum(jnp.where(iota((2 * T, 32), 1) == col, by_row, 0.0), axis=1, keepdims=True)
    lab = jnp.where(valid, lab + jnp.where(col < 4, 4.0, 0.0), -1.0)
    oh[...] = jnp.where(lab == iota((2 * T, 128), 1).astype(f32), 1.0, 0.0).astype(bf16)

    for c in halo_copies:
        c.wait_recv()
    norm_to_windows(halo, n_halo, range(4))
    project(n_halo, wk, k_all, 32)
    project(n_halo, wv, v_all, 32)

    diag = (iota((QW, QW), 0) >> 5) == (iota((QW, QW), 1) >> 5)

    def window_row(b, _):
        parts = []
        for w in range(4):
            bw = b * 4 + w
            rows = pl.ds(pl.multiple_of(bw * 32, 32), 32)
            halo_rows = pl.ds(pl.multiple_of(T + bw * 32, 32), 32)
            oq = oh[rows, :]
            ok = jnp.concatenate([oq, oh[halo_rows, :]], axis=0)
            bias = jnp.concatenate([(dot(oq, ok, NT) - 1.0) * 1e30] * 8, axis=0)
            parts += [(bw, rows, slice(g * QW, (g + 1) * QW), bias) for g in range(4)]
        all_scores = []
        for bw, rows, cols, bias in parts:
            qg = jnp.concatenate([q_own[rows, cols]] * 8, axis=0)
            qg = jnp.where(diag, qg, jnp.zeros_like(qg))
            all_scores.append(dot(qg, k_all[bw, :, cols], NT) * SCALE + bias)
        all_weights = []
        for scores in all_scores:
            expo = jnp.exp(scores - jnp.max(scores, axis=1, keepdims=True))
            all_weights.append((expo * (1.0 / jnp.sum(expo, axis=1, keepdims=True))).astype(bf16))
        for (bw, rows, cols, bias), weights in zip(parts, all_weights):
            mixed = dot(weights, v_all[bw, :, cols])
            mixed = jnp.where(diag, mixed, 0.0).reshape(8, 32, QW)
            ctx[rows, cols] = jnp.sum(mixed, axis=0).astype(bf16)
        return _

    lax.fori_loop(0, 2, window_row, 0)

    ld_o.wait()

    o = dot(ctx[...], wo[...])
    for r in range(8):
        base = (r // 4) * 128 + (r % 4) * 8
        parts = [o[base + w * 32 : base + w * 32 + 8] for w in range(4)]
        row = pltpu.roll(jnp.concatenate(parts, axis=0), 4, 0)
        hid[r * 32 : r * 32 + 32, :] = feat_v[r * 32 : r * 32 + 32, :].astype(f32) + row

    def norm_hidden(r, _):
        rows = pl.ds(pl.multiple_of(r * 64, 64), 64)
        moe[rows, :] = layer_norm(hid[rows, :]).astype(bf16)
        return _

    lax.fori_loop(0, 4, norm_hidden, 0)

    for n in range(2):
        cols = slice(n * 512, n * 512 + 512)
        x_send[:, :, cols] = dot(disp[0:ROWS, :], moe[:, cols]).astype(bf16).reshape(NE, CAP, 512)
    feat_args = (x_send, x_recv, x_ss, x_rs)
    for i in others:
        exchange(i, *feat_args).start()
    x_recv[me] = x_send[me]

    disp_t[...] = disp[0:ROWS, :].T
    ld_u.wait()

    def transpose_up(i, _):
        rows = pl.ds(pl.multiple_of(i * 256, 256), 256)
        wk[rows, :] = wu[:, pl.ds(pl.multiple_of(i * 256, 256), 256)].T
        wv[rows, :] = wu[:, pl.ds(pl.multiple_of(F + i * 256, 256), 256)].T
        return _

    lax.fori_loop(0, 4, transpose_up, 0)
    ld_d.wait()

    def split_down(i, _):
        rows = pl.ds(pl.multiple_of(lax.rem(i, 4) * 256, 256), 256)
        for h, part in enumerate(halves(wd[pl.ds(pl.multiple_of(i * 256, 256), 256), :])):
            wu[rows, pl.ds(pl.multiple_of(h * F + lax.div(i, 4) * HB, HB), HB)] = part
        return _

    lax.fori_loop(0, 8, split_down, 0)

    def half_grads(half, hb):
        rows = pl.ds(pl.multiple_of(lax.rem(hb, 2) * HB, HB), HB)
        cols = pl.ds(pl.multiple_of(half * F + lax.div(hb, 2) * HB, HB), HB)
        return dot(wu[rows, cols], l_recv[half].reshape(ROWS, F // 2), NT)

    for i in others:
        arrival(i, *sens_args(0)).wait_recv()

    def first_half(hb, _):
        a2[1, pl.ds(pl.multiple_of(hb * HB, HB), HB), :] = half_grads(0, hb).astype(bf16)
        return _

    lax.fori_loop(0, NB, first_half, 0)

    for i in others:
        arrival(i, meta_send, meta_recv, m_ss, m_rs).wait_recv()

    meta_all = meta_recv[...].reshape(256, 128)
    spread = (iota((128, ROWS), 0) == lax.rem(iota((128, ROWS), 1), CAP)).astype(f32).astype(bf16)
    ids = dot(meta_all, spread)
    own_part = iota((256, ROWS), 0) == lax.div(iota((256, ROWS), 1), CAP) * 16
    other = jnp.sum(jnp.where(own_part, ids, 0.0), axis=0, keepdims=True) - me.astype(f32)

    for i in others:
        arrival(i, *feat_args).wait_recv()
    for i in others:
        exchange(i, *feat_args).wait_send()
    for i in others:
        exchange(i, *sens_args(1)).start()

    logits = dot(router[...], x_recv[...].reshape(ROWS, F), NT)
    sig = 1.0 / (1.0 + jnp.exp(-logits))
    expert = iota((NE, ROWS), 0)
    mine = jnp.sum(jnp.where(expert == me, sig, 0.0), axis=0, keepdims=True)
    theirs = jnp.sum(jnp.where(expert.astype(f32) == other, sig, 0.0), axis=0, keepdims=True)
    gate_v[...] = jnp.broadcast_to(mine / (mine + theirs), (8, ROWS))

    def activate(hb):
        first = pl.multiple_of(lax.rem(hb, 2) * HB, HB)
        u = dot(w3[1 + lax.div(hb, 2), pl.ds(first, HB), :], x_recv[...].reshape(ROWS, F), NT)
        gate = gate_v[0:1, :]
        u2 = u * u
        t = jnp.tanh(GELU_A * u * (1.0 + GELU_B * u2))
        rise = 0.5 * (1.0 + t)
        rows = pl.ds(pl.multiple_of(hb * HB, HB), HB)
        a2[0, rows, :] = (u * rise * gate).astype(bf16)
        slope = rise + 0.5 * u * (1.0 - t * t) * (GELU_A + (3.0 * GELU_A * GELU_B) * u2)
        slope_v[rows, :] = (slope * gate).astype(bf16)

    def first_grads(hb, _):
        rows = pl.ds(pl.multiple_of(hb * HB, HB), HB)
        block = half_grads(1, hb) + a2[1, rows, :].astype(f32)
        a2[1, rows, :] = (block * slope_v[rows, :].astype(f32)).astype(bf16)
        return _

    rv_send = x_send
    result_args = (rv_send, ret, t_ss, t_rs)

    def make_results(half):
        lanes = slice(half * 384, (half + 1) * 384)

        def product(i, _):
            cols = pl.ds(pl.multiple_of(i * 512, 512), 512)
            block = dot(a2[0, :, lanes], wd[:, cols], TN).astype(bf16)
            rv_send[half * 8 : half * 8 + 8, :, cols] = block.reshape(8, CAP, 512)
            return _

        lax.fori_loop(0, 2, product, 0)
        for i in others:

            @pl.when((to_tile[i] >= 8 * half) & (to_tile[i] < 8 * half + 8))
            def _(i=i):
                exchange(i, *result_args).start()

    def chunk(away):
        return lax.rem(xpos + away, 4)

    def core_copy(g, h):
        return rep_copy(stage.at[g, 1 - core, h], crecv.at[g, h], c_ss.at[g, h], c_rs.at[g, h], partner)

    def down_group(half, hb):
        return half * 2 + lax.div(hb, 2), lax.rem(hb, 2)

    def make_down(half, hb):
        g, h = down_group(half, hb)
        rows = pl.ds(pl.multiple_of(hb * HB, HB), HB)
        block = dot(a2[0, rows, :], l_recv[half].reshape(ROWS, F // 2)).astype(bf16)
        for q in range(4):
            top = block[0:256, q * 128 : q * 128 + 128]
            low = block[256:512, q * 128 : q * 128 + 128]
            stage[g, 0, h, q] = jnp.concatenate([top[:, 0:64], low[:, 0:64]], axis=1)
            stage[g, 1, h, q] = jnp.concatenate([top[:, 64:], low[:, 64:]], axis=1)
        core_copy(g, h).start()

    def make_up(hb):
        g = NB + hb
        rows = pl.ds(pl.multiple_of(hb * HB, HB), HB)
        block = dot(a2[1, rows, :], x_recv[...].reshape(ROWS, F)).astype(bf16)
        for h in range(2):
            for q in range(4):
                for c in range(2):
                    start = (2 * q + c) * 128
                    stage[g, c, h, q] = block[h * 256 : h * 256 + 256, start : start + 128]
            core_copy(g, h).start()

    def hop(g, which):
        away, h = [(2, 0), (1, 1), (1, 0), (2, 1), (3, 0), (3, 1)][which]
        dst = [
            r2.at[g, 0], rf.at[g, 0, 1], rf.at[g, 0, 0],
            r2.at[g, 1], rf.at[g, 1, 0], rf.at[g, 1, 1],
        ][which]
        src = stage.at[g, core, h, chunk(away)]
        return rep_copy(src, dst, x2_ss.at[g, which], x2_rs.at[g, which], x_next if which < 3 else x_prev)

    def add_cores(g, h):
        core_copy(g, h).wait_recv()
        total = stage[g, core, h].astype(f32) + crecv[g, h].astype(f32)
        stage[g, core, h] = total.astype(bf16)

    def send_half(g, h):
        for which in ((0, 4), (3, 1))[h]:
            hop(g, which).start()

    def add_down(half, hb):
        g, h = down_group(half, hb)
        add_cores(g, h)

        @pl.when(h == 0)
        def _():
            send_half(g, 0)

        @pl.when(h == 1)
        def _():
            send_half(g, 1)

    def add_up(hb):
        for h in range(2):
            add_cores(NB + hb, h)
            send_half(NB + hb, h)

    def add_last():
        for h, which in ((0, 0), (1, 3)):
            add_cores(GROUPS - 1, h)
            hop(GROUPS - 1, which).start()

    def add_far(g):
        for first, away, h, second in ((0, 1, 0, 2), (3, 3, 1, 5)):
            hop(g, first).wait_recv()
            q = chunk(away)
            total = stage[g, core, h, q].astype(f32) + r2[g, h].astype(f32)
            stage[g, core, h, q] = total.astype(bf16)
            hop(g, second).start()

    def finish(g):
        for which in (1, 2, 4, 5):
            hop(g, which).wait_recv()
        parts = []
        for h in range(2):
            parts.append(
                stage[g, core, h, xpos].astype(f32)
                + rf[g, 0, h].astype(f32)
                + rf[g, 1, h].astype(f32)
            )
        return parts

    def down_copy(hb):
        rows = pl.ds(pl.multiple_of(hb * HB, HB), HB)
        return pltpu.make_async_copy(down_v.at[rows, :], out_down.at[rows, :], down_sem.at[hb])

    def up_copy(hb):
        cols = pl.ds(pl.multiple_of(hb * HB, HB), HB)
        return pltpu.make_async_copy(up_v.at[:, cols], out_up.at[:, cols], up_sem.at[hb])

    def finish_down(pair, _):
        low, high = finish(pair), finish(2 + pair)
        for h in range(2):
            rows = pl.multiple_of((pair * 2 + h) * HB, HB)
            down_v[pl.ds(rows, 256), :] = jnp.concatenate([low[h][:, 0:64], high[h][:, 0:64]], axis=1)
            down_v[pl.ds(rows + 256, 256), :] = jnp.concatenate([low[h][:, 64:], high[h][:, 64:]], axis=1)
            down_copy(pair * 2 + h).start()
        return _

    def finish_up(hb, _):
        for h, total in enumerate(finish(NB + hb)):
            up_v[:, pl.ds(pl.multiple_of(hb * HB + h * 256, 256), 256)] = total.T
        up_copy(hb).start()
        return _

    def down_groups(half, before):
        def body(hb, carry):
            before(hb)
            make_down(half, hb)

            @pl.when(hb >= 1)
            def _():
                add_down(half, hb - 1)

            return carry

        lax.fori_loop(0, NB, body, 0)
        add_down(half, NB - 1)

    down_groups(0, activate)
    add_far(0)
    for i in others:
        arrival(i, *sens_args(1)).wait_recv()
    down_groups(1, lambda hb: None)
    add_far(1)
    make_results(0)
    add_far(2)
    make_results(1)
    ret[me] = rv_send[me]
    add_far(3)
    lax.fori_loop(0, NB, first_grads, 0)

    def up_step(hb, carry):
        make_up(hb)

        @pl.when(hb >= 1)
        def _():
            add_up(hb - 1)

        @pl.when(hb >= 2)
        def _():
            add_far(NB + hb - 2)

        return carry

    lax.fori_loop(0, NB, up_step, 0)
    add_last()
    add_far(GROUPS - 2)
    finish_down(0, 0)
    add_far(GROUPS - 1)
    for which in (1, 4):
        hop(GROUPS - 1, which).start()
    finish_down(1, 0)

    for i in others:
        arrival(i, *result_args).wait_recv()

    def combine(i, _):
        cols = pl.ds(pl.multiple_of(i * 256, 256), 256)
        mixture = dot(disp_t[...], ret[:, :, cols].reshape(ROWS, 256))
        layer_v[:, cols] = (hid[:, cols] + mixture).astype(bf16)
        return _

    lax.fori_loop(0, 4, combine, 0)
    layer_copy = pltpu.make_async_copy(layer_v, out_layer, layer_sem)
    layer_copy.start()
    lax.fori_loop(0, NB, finish_up, 0)

    layer_copy.wait()
    for hb in range(NB):
        down_copy(hb).wait()
        up_copy(hb).wait()
    for c in halo_copies:
        c.wait_send()

    for i in others:
        exchange(i, meta_send, meta_recv, m_ss, m_rs).wait_send()
        exchange(i, *result_args).wait_send()
        exchange(i, *sens_args(0)).wait_send()
        exchange(i, *sens_args(1)).wait_send()

    def drain_groups(g, _):
        for h in range(2):
            core_copy(g, h).wait_send()
        for which in range(6):
            hop(g, which).wait_send()
        return _

    lax.fori_loop(0, GROUPS, drain_groups, 0)


def hand_over(layer, up, down, out_layer, out_up, out_down, layer_v, up_v, down_v, sem_in, sem_out):
    steps = []
    for a, v, b in ((layer, layer_v, out_layer), (up, up_v, out_up), (down, down_v, out_down)):
        rows = a.shape[0] // 4
        for i in range(4):
            part = pl.ds(i * rows, rows)
            n = len(steps)
            steps.append((
                pltpu.make_async_copy(a.at[part, :], v.at[part, :], sem_in.at[n]),
                pltpu.make_async_copy(v.at[part, :], b.at[part, :], sem_out.at[n]),
            ))
    for first, _ in steps:
        first.start()
    for first, second in steps:
        first.wait()
        second.start()
    for _, second in steps:
        second.wait()


def on_device(
    patch_features, labels, assigned_specialists, loss_sensitivity,
    attn_qkv, attn_out, router, expert_up, expert_down,
):
    hbm = pl.BlockSpec(memory_space=pl.ANY)
    vmem = pl.BlockSpec(memory_space=pltpu.VMEM)
    dma = pltpu.SemaphoreType.DMA

    def buf(*shape, dtype=bf16):
        return pltpu.VMEM(shape, dtype)

    scratch = [
        buf(T, F), buf(T, F), buf(3, F, F), buf(F, F), buf(F, FFW), buf(FFW, F),
        buf(T, F), buf(T, F), buf(T, F), buf(T, F), buf(8, 64, F), buf(8, 64, F), buf(T, F),
        buf(2 * T, 128), buf(T, F, dtype=f32), buf(T, F),
        buf(ROWS + 128 - CAP, T), buf(T, ROWS), buf(NE, 16, 128), buf(NE, 16, 128),
        buf(NE, CAP, F), buf(NE, CAP, F), buf(2, NE, CAP, F // 2), buf(2, NE, CAP, F // 2), buf(FFW, ROWS),
        buf(NE, CAP, F), buf(2, FFW, ROWS),
        buf(8, ROWS, dtype=f32),
        buf(GROUPS, 2, 2, 4, 256, 128), buf(GROUPS, 2, 4, 256, 128),
        buf(GROUPS, 2, 256, 128), buf(GROUPS, 2, 2, 256, 128),
        dma((8,)), dma((2,)), dma((2,)),
        dma((2, NE)), dma((2, NE)), dma((NE,)), dma((NE,)), dma((NE,)), dma((NE,)), dma((NE,)), dma((NE,)),
        dma((GROUPS, 2)), dma((GROUPS, 2)), dma((GROUPS, 6)), dma((GROUPS, 6)),
        buf(T, F), buf(F // 8, FFW, dtype=f32), buf(FFW, F // 8, dtype=f32),
        dma, dma((NB,)), dma((NB,)),
    ]
    layer, up, down = pl.pallas_call(
        kernel,
        out_shape=(
            jax.ShapeDtypeStruct((T, F), bf16),
            jax.ShapeDtypeStruct((F // 8, FFW), f32),
            jax.ShapeDtypeStruct((FFW, F // 8), f32),
        ),
        in_specs=[hbm, vmem, vmem, hbm, hbm, hbm, vmem, hbm, hbm],
        out_specs=(hbm, hbm, hbm),
        scratch_shapes=scratch,
        compiler_params=pltpu.CompilerParams(
            collective_id=0, has_side_effects=True, vmem_limit_bytes=62 * 1024 * 1024
        ),
        name="layer",
    )(
        patch_features[0], labels.T, assigned_specialists[0].T, loss_sensitivity[0],
        attn_qkv, attn_out, router.T, expert_up[0], expert_down[0],
    )
    layer, up, down = pl.pallas_call(
        hand_over,
        out_shape=(
            jax.ShapeDtypeStruct((T, F), bf16),
            jax.ShapeDtypeStruct((F // 8, FFW), f32),
            jax.ShapeDtypeStruct((FFW, F // 8), f32),
        ),
        in_specs=[hbm, hbm, hbm],
        out_specs=(hbm, hbm, hbm),
        scratch_shapes=[
            buf(T, F), buf(F // 8, FFW, dtype=f32), buf(FFW, F // 8, dtype=f32), dma((12,)), dma((12,)),
        ],
        name="hand_over",
    )(layer, up, down)
    return layer[None], up[None], down[None]


def solution(mesh):
    return jax.shard_map(
        on_device,
        mesh=mesh,
        in_specs=(
            P("rep", "tile", None), P(), P("rep", "tile", None), P("rep", "tile", None),
            P(), P(), P(), P("tile", None, None), P("tile", None, None),
        ),
        out_specs=(P("rep", "tile", None), P("tile", "rep", None), P("tile", None, "rep")),
        check_vma=False,
    )
```
